32 devices in a mesh: gx: 8 (over y, x, core), gy: 4 (over z).
Axes of the slice: x: 2, y: 2, z: 4, core: 2. Of those that a mesh axis runs over, the one named last changes fastest.
Arguments:
- sample_model_status: float32 [3, 80, 64, 1024], P(None, None, 'gy', 'gx'), may hold values from -6 to 6
- friction_rate: float32 [64, 1024], P('gy', 'gx'), may hold values from 0.02 to 0.3
- obs_value: float32 [24], replicated, may hold values from -6 to 6
- obs_error: float32 [24], replicated, may hold values from 0.25 to 2
- taper: float32 [7], replicated, may hold values from 0.2 to 1
- order: int32 [24], replicated, may hold values from 0 to 23, each once
- owner: int32 [24], replicated, may hold values from 0 to 31
- observation_cell: int32 [24], replicated, may hold values from 0 to 6143
- reach: int32 [24], replicated, may hold values from 0 to 6
Outputs:
- analysis: float32 [3, 80, 64, 1024], P(None, None, 'gy', 'gx')
The draws below stay inside these ranges and needn't reach their ends.
Inputs may be any that keep to these rules, and one draw needn't show every extreme that they name: `order`: each observation index appears once. `owner`: device o stands at index o // 4 along gx and o % 4 along gy.
All inputs are finite; a program needn't handle non-finite values.
Results may differ from the reference program's by a relative error of at most 0.0001.
Values sent between devices are 32-bit elements; how exact they have to be, the bound alone decides.
No kernel may reach another device: no remote copies, remote signals or barrier semaphores. Data moves between devices by JAX's collectives and lax.ppermute only.
A program may use at most 64 MiB of HBM per device.

```python
import math
import jax
import jax.numpy as jnp
from jax import lax

M = 80
CR = 16
CC = 128
STEPS = 4
RADIUS = 6
NOBS = 24
NR = 64
NC = 1024
N_GX = 8
N_GY = 4


def set_ends(values, rng, least, largest):
    dims = values.shape
    index_at = [jax.random.randint(jax.random.fold_in(rng, axis), (), 0, dims[axis]) for axis in range(len(dims))]
    values = values.at[tuple(index_at)].set(least)
    longest = dims.index(max(dims))
    index_at[longest] = (index_at[longest] + 1) % dims[longest]
    return values.at[tuple(index_at)].set(largest)


def block_scale(rng, dims, cuts, low, largest):
    level, own = 1.0, jax.random.fold_in(rng, 6)
    for dim, shards_of in cuts:
        steps = jnp.exp(jax.random.uniform(jax.random.fold_in(own, dim), (shards_of,), jnp.float32, low / len(cuts), largest / len(cuts)))
        level = level * jnp.repeat(steps, dims[dim] // shards_of).reshape([-1 if axis == dim else 1 for axis in range(len(dims))])
    return level


def gaussian(rng, shape, scale, most, split=(), kind=jnp.bfloat16):
    entries = jax.random.normal(rng, shape, jnp.float32) * scale
    if len(split) > 0:
        entries = block_scale(rng, shape, split, -0.22, 0.18) * entries
    return jnp.clip(entries, min=-most, max=most).astype(kind)


def setup_inputs(seed: int = 0) -> dict:
    seeds = jax.random.split(jax.random.key(seed), 10)
    return {
        "sample_model_status": gaussian(seeds[0], (3, M, NR, NC), 1.0, 6.0, ((2, 4), (3, 8)), jnp.float32),
        "friction_rate": jnp.clip(jnp.exp(math.log(0.3) - 2.7080503 * jax.random.uniform(seeds[1], (NR, NC), jnp.float32) ** block_scale(seeds[1], (NR, NC), ((0, 4), (1, 8)), -0.2, 0.2)), 0.02, 0.3),
        "obs_value": gaussian(seeds[2], (NOBS,), 1.5, 6.0, (), jnp.float32),
        "obs_error": jnp.clip(jnp.exp(jax.random.uniform(seeds[3], (NOBS,), jnp.float32, math.log(0.25), math.log(2.0))), 0.25, 2.0),
        "taper": jnp.clip(jnp.exp(jax.random.uniform(seeds[4], (RADIUS + 1,), jnp.float32, math.log(0.2), math.log(1.0))), 0.2, 1.0),
        "order": jax.random.permutation(seeds[5], NOBS).astype(jnp.int32),
        "owner": set_ends(jax.random.randint(seeds[6], (NOBS,), 0, N_GX * N_GY), jax.random.fold_in(seeds[6], 1), 0, (N_GX * N_GY) - 1).astype(jnp.int32),
        "observation_cell": set_ends(jax.random.randint(seeds[7], (NOBS,), 0, 3 * CR * CC), jax.random.fold_in(seeds[7], 1), 0, (3 * CR * CC) - 1).astype(jnp.int32),
        "reach": set_ends(jax.random.randint(seeds[8], (NOBS,), 0, RADIUS + 1), jax.random.fold_in(seeds[8], 1), 0, RADIUS).astype(jnp.int32),
    }


courant = 0.4
coriolis = 0.1
epsilon = 1e-06
highest = lax.Precision.HIGHEST

def along_cols(field):
    padded = jnp.pad(field, ((0, 0), (0, 0), (1, 1)))
    return 0.5 * (padded[:, :, 2:] - padded[:, :, :-2])

def along_rows(field):
    padded = jnp.pad(field, ((0, 0), (1, 1), (0, 0)))
    return 0.5 * (padded[:, 2:, :] - padded[:, :-2, :])

def predicted_sample_set(sample_model_status, friction_rate):
    surface_height, flow_x, northward_current = (sample_model_status[0], sample_model_status[1], sample_model_status[2])
    for time_step in range(STEPS):
        surface_height = surface_height - courant * (along_cols(flow_x) + along_rows(northward_current))
        new_x = (1.0 - friction_rate) * flow_x - courant * along_cols(surface_height) + coriolis * northward_current
        new_y = (1.0 - friction_rate) * northward_current - courant * along_rows(surface_height) - coriolis * flow_x
        flow_x, northward_current = (new_x, new_y)
    return jnp.stack([surface_height, flow_x, northward_current])

def taper_weight(tile_x, tile_y, owner, reach, taper, rows_tiles):
    owner_x = owner // rows_tiles
    owner_y = owner % rows_tiles
    distance = jnp.maximum(jnp.abs(tile_x - owner_x), jnp.abs(tile_y - owner_y))
    vertical_levels = jnp.arange(taper.shape[0], dtype=jnp.int32)
    capped = jnp.minimum(distance, taper.shape[0] - 1)
    picked = lax.optimization_barrier(jnp.sum(jnp.where(capped[..., None] == vertical_levels, taper, jnp.zeros_like(taper)), axis=-1))
    return jnp.where(distance <= reach, picked, jnp.zeros_like(picked))

def observe_step(priors, which, obs_value, obs_error):
    member_count = priors.shape[1]
    prior = priors[which]
    prior_mean = jnp.mean(prior)
    anomaly = prior - prior_mean
    variance = jnp.sum(anomaly * anomaly) / (member_count - 1) + epsilon
    error_var = obs_error[which]
    observed = obs_value[which]
    post_mean = (prior_mean * error_var + observed * variance) / (variance + error_var)
    shrink = jnp.sqrt(error_var / (variance + error_var))
    increment = post_mean - prior_mean + (shrink - 1.0) * anomaly
    scaled = 1.0 / ((member_count - 1) * variance)
    return (anomaly, increment, scaled)

def reference(sample_model_status, friction_rate, obs_value, obs_error, taper, order, owner, observation_cell, reach):
    sample_model_status = predicted_sample_set(sample_model_status, friction_rate)
    member_count = sample_model_status.shape[1]
    owner_x = owner // N_GY
    owner_y = owner % N_GY
    field_id = observation_cell // (CR * CC)
    place = observation_cell % (CR * CC)
    mesh_line_total = owner_y * CR + place // CC
    grid_cols = owner_x * CC + place % CC
    priors = sample_model_status[field_id, :, mesh_line_total, grid_cols]
    obs_weights = taper_weight(owner_x[:, None], owner_y[:, None], owner[None, :], reach[None, :], taper, N_GY)
    tile_x = jnp.arange(N_GX, dtype=jnp.int32)[:, None, None]
    tile_y = jnp.arange(N_GY, dtype=jnp.int32)[None, :, None]
    tile_weights = taper_weight(tile_x, tile_y, owner[None, None, :], reach[None, None, :], taper, N_GY)
    identity = jnp.eye(member_count, dtype=jnp.float32)
    transforms = jnp.broadcast_to(identity, (N_GX, N_GY, member_count, member_count))

    def advance(position, carry):
        priors, transforms = carry
        which = order[position]
        anomaly, increment, scaled = observe_step(priors, which, obs_value, obs_error)
        along = jnp.dot(priors, anomaly, precision=highest)
        priors = priors + (obs_weights[:, which] * scaled * along)[:, None] * increment[None, :]
        mapped = jnp.einsum('xymn,n->xym', transforms, anomaly, precision=highest)
        factor = tile_weights[:, :, which] * scaled
        transforms = transforms + (factor[:, :, None] * mapped)[..., None] * increment
        return (priors, transforms)
    priors, transforms = lax.fori_loop(0, order.shape[0], advance, (priors, transforms))
    blocks = sample_model_status.reshape(3, member_count, N_GY, CR, N_GX, CC)
    result = jnp.einsum('fmyrxc,xymn->fnyrxc', blocks, transforms, precision=highest)
    return result.reshape(sample_model_status.shape)
```

```python
import functools

import jax
import jax.numpy as jnp
from jax import lax
from jax.experimental import pallas as pl
from jax.experimental.pallas import tpu as pltpu
from jax.sharding import PartitionSpec as P

STEPS = 4
MARGIN = 2 * STEPS
EPS = 1e-06
NT = (((1,), (1,)), ((), ()))
HIGHEST = lax.Precision.HIGHEST
F32 = jnp.float32
BF16 = jnp.bfloat16
VMEM_LIMIT = 48 * 1024 * 1024

VSPEC = pl.BlockSpec(memory_space=pltpu.VMEM)
SSPEC = pl.BlockSpec(memory_space=pltpu.SMEM)


def lanes_of(shape):
    return lax.broadcasted_iota(jnp.int32, shape, len(shape) - 1)


def sublanes_of(shape):
    return lax.broadcasted_iota(jnp.int32, shape, len(shape) - 2)


def roll_lanes(x, shift):
    size = x.shape[-1]
    shift = shift % size
    return x if shift == 0 else pltpu.roll(x, shift, x.ndim - 1)


def pack_kernel(members, rows, x_ref, drag_ref, left_ref, right_ref):
    cols = x_ref.shape[1]
    lane = lanes_of((8, cols))
    count = 3 * members

    def group(g, carry):
        left = jnp.zeros((8, cols), F32)
        right = jnp.zeros((8, cols), F32)
        for r in range(rows):
            row = x_ref[pl.ds(g * 8 * rows + r, 8, stride=rows), :]
            here = (lane >= MARGIN * r) & (lane < MARGIN * (r + 1))
            left = jnp.where(here, roll_lanes(row, MARGIN * r), left)
            right = jnp.where(here, roll_lanes(row, MARGIN * (r + 1)), right)
        left_ref[pl.ds(pl.multiple_of(g * 8, 8), 8), :] = left
        right_ref[pl.ds(pl.multiple_of(g * 8, 8), 8), :] = right
        return carry

    lax.fori_loop(0, count // 8, group, 0)
    left = jnp.zeros((8, cols), F32)
    right = jnp.zeros((8, cols), F32)
    for r in range(rows):
        row = jnp.broadcast_to(drag_ref[r : r + 1, :], (8, cols))
        here = (lane >= MARGIN * r) & (lane < MARGIN * (r + 1))
        left = jnp.where(here, roll_lanes(row, MARGIN * r), left)
        right = jnp.where(here, roll_lanes(row, MARGIN * (r + 1)), right)
    left_ref[count : count + 8, :] = left
    right_ref[count : count + 8, :] = right


def pack(x, drag, members):
    rows, cols = drag.shape
    out = jax.ShapeDtypeStruct((3 * members + 8, cols), F32)
    return pl.pallas_call(
        functools.partial(pack_kernel, members, rows),
        out_shape=(out, out),
        in_specs=[VSPEC, VSPEC],
        out_specs=(VSPEC, VSPEC),
        compiler_params=pltpu.CompilerParams(vmem_limit_bytes=VMEM_LIMIT),
    )(x, drag)


def wide_row(lane, main, left, left_at, right, right_at):
    cols = main.shape[1]
    halo = jnp.where(lane >= cols - MARGIN, roll_lanes(left, cols - MARGIN - left_at), 0.0)
    halo = jnp.where(lane < MARGIN, roll_lanes(right, -right_at), halo)
    return jnp.concatenate([main, halo], axis=1)


def forecast_kernel(
    members, rows,
    place_ref, order_ref, owner_ref, cell_ref,
    x_ref, above_ref, below_ref, left_ref, right_ref, cabove_ref, cbelow_ref,
    drag_ref, dabove_ref, dbelow_ref,
    out_ref, prior_ref,
    state, keep, slope,
):
    cols = x_ref.shape[1]
    wide = 2 * cols
    total = rows + 2 * MARGIN
    lane = lanes_of((8, cols))
    half = cols // 2
    count = 3 * members

    wlane = lanes_of((8, wide))
    first_x, last_x = place_ref[1], place_ref[2]
    first_y, last_y = place_ref[3], place_ref[4]
    outside = ((first_x == 1) & (wlane >= wide - MARGIN)) | ((last_x == 1) & (wlane >= cols) & (wlane < cols + MARGIN))
    unused = (wlane >= cols + MARGIN) & (wlane < wide - MARGIN)
    factor = jnp.where(outside | unused, 0.0, -0.2)
    for r in range(total):
        if r < MARGIN:
            main = dabove_ref[r : r + 1, :]
            left, la = cabove_ref[count : count + 8, :], MARGIN * r
            right, ra = left, half + MARGIN * r
            ok = jnp.where(first_y == 1, 0.0, 1.0)
        elif r < MARGIN + rows:
            main = drag_ref[r - MARGIN : r - MARGIN + 1, :]
            left, la = left_ref[count : count + 8, :], MARGIN * (r - MARGIN)
            right, ra = right_ref[count : count + 8, :], MARGIN * (r - MARGIN)
            ok = 1.0
        else:
            main = dbelow_ref[r - MARGIN - rows : r - MARGIN - rows + 1, :]
            left, la = cbelow_ref[count : count + 8, :], MARGIN * (r - MARGIN - rows)
            right, ra = left, half + MARGIN * (r - MARGIN - rows)
            ok = jnp.where(last_y == 1, 0.0, 1.0)
        main = jnp.broadcast_to(main, (8, cols))
        keep[r] = 1.0 - wide_row(lane, main, left, la, right, ra)
        slope[r] = factor * ok

    def group(g, carry):
        for f in range(3):
            at = f * members + g * 8
            at8 = pl.multiple_of(at, 8)
            ledge, redge = left_ref[pl.ds(at8, 8), :], right_ref[pl.ds(at8, 8), :]
            cab, cbe = cabove_ref[pl.ds(at8, 8), :], cbelow_ref[pl.ds(at8, 8), :]
            for r in range(total):
                if r < MARGIN:
                    main = above_ref[pl.ds(at * MARGIN + r, 8, stride=MARGIN), :]
                    value = wide_row(lane, main, cab, MARGIN * r, cab, half + MARGIN * r)
                elif r < MARGIN + rows:
                    q = r - MARGIN
                    main = x_ref[pl.ds(at * rows + q, 8, stride=rows), :]
                    value = wide_row(lane, main, ledge, MARGIN * q, redge, MARGIN * q)
                else:
                    q = r - MARGIN - rows
                    main = below_ref[pl.ds(at * MARGIN + q, 8, stride=MARGIN), :]
                    value = wide_row(lane, main, cbe, MARGIN * q, cbe, half + MARGIN * q)
                state[f, r] = value
        for step in range(STEPS):
            reach = 2 * (STEPS - step) - 1
            for r in range(MARGIN - reach, MARGIN + rows + reach):
                u = state[1, r]
                div = (roll_lanes(u, -1) - roll_lanes(u, 1)) + (state[2, r + 1] - state[2, r - 1])
                state[0, r] = state[0, r] + slope[r] * div
            reach -= 1
            for r in range(MARGIN - reach, MARGIN + rows + reach):
                h = state[0, r]
                u, v = state[1, r], state[2, r]
                k, c = keep[r], slope[r]
                state[1, r] = k * u + c * (roll_lanes(h, -1) - roll_lanes(h, 1)) + 0.1 * v
                state[2, r] = k * v + c * (state[0, r + 1] - state[0, r - 1]) - 0.1 * u
        for f in range(3):
            for r in range(rows):
                out_ref[f * rows + r, pl.ds(pl.multiple_of(g * 8, 8), 8), :] = state[f, MARGIN + r, :, 0:cols]
        return carry

    lax.fori_loop(0, members // 8, group, 0)

    prior_ref[...] = jnp.zeros_like(prior_ref)
    for i in range(order_ref.shape[0]):
        which = order_ref[i]

        @pl.when(owner_ref[which] == place_ref[0])
        def _():
            cell = cell_ref[which]
            column = cell % cols
            one = jnp.where(lane == column, 1.0, 0.0)
            prior_ref[i : i + 1, 0:members] = lax.dot_general(
                one, out_ref[cell // cols], NT, precision=HIGHEST, preferred_element_type=F32
            )[0:1]


def forecast(place, order, owner, cell, x, above, below, left, right, cabove, cbelow, drag, dabove, dbelow, members):
    rows, cols = drag.shape
    total = rows + 2 * MARGIN
    return pl.pallas_call(
        functools.partial(forecast_kernel, members, rows),
        out_shape=(
            jax.ShapeDtypeStruct((3 * rows, members, cols), F32),
            jax.ShapeDtypeStruct((order.shape[0], cols), F32),
        ),
        in_specs=[SSPEC] * 4 + [VSPEC] * 10,
        out_specs=(VSPEC, VSPEC),
        scratch_shapes=[
            pltpu.VMEM((3, total, 8, 2 * cols), F32),
            pltpu.VMEM((total, 8, 2 * cols), F32),
            pltpu.VMEM((total, 8, 2 * cols), F32),
        ],
        compiler_params=pltpu.CompilerParams(vmem_limit_bytes=VMEM_LIMIT),
    )(place, order, owner, cell, x, above, below, left, right, cabove, cbelow, drag, dabove, dbelow)


def localize(distance, reach, taper_ref):
    picked = jnp.zeros(distance.shape, F32)
    levels = taper_ref.shape[0]
    capped = jnp.minimum(distance, levels - 1)
    for d in range(levels):
        picked = jnp.where(capped == d, taper_ref[d], picked)
    return jnp.where(distance <= reach, picked, 0.0)


def assimilate_kernel(
    members, rows,
    place_ref, order_ref, owner_ref, reach_ref, value_ref, error_ref, taper_ref,
    prior_ref, forecast_ref,
    out_ref,
):
    n_obs = order_ref.shape[0]
    cols = prior_ref.shape[1]
    size_y = place_ref[5]
    lane1 = lanes_of((1, cols))
    lane = lanes_of((n_obs, cols))
    sub = sublanes_of((n_obs, cols))

    tile_row = jnp.zeros((1, cols), jnp.int32)
    tile_col = jnp.zeros((n_obs, cols), jnp.int32)
    reach_row = jnp.zeros((1, cols), jnp.int32)
    reach_col = jnp.zeros((n_obs, cols), jnp.int32)
    which = [order_ref[i] for i in range(n_obs)]
    for i, k in enumerate(which):
        tile_row = jnp.where(lane1 == i, owner_ref[k], tile_row)
        tile_col = jnp.where(sub == i, owner_ref[k], tile_col)
        reach_row = jnp.where(lane1 == i, reach_ref[k], reach_row)
        reach_col = jnp.where(sub == i, reach_ref[k], reach_col)
    rx, ry = tile_row // size_y, tile_row % size_y
    cx, cy = tile_col // size_y, tile_col % size_y
    distance = jnp.maximum(jnp.abs(cx - rx), jnp.abs(cy - ry))
    onto = localize(distance, reach_row, taper_ref)
    onto_t = localize(distance, reach_col, taper_ref)
    mine = place_ref[0]
    own = localize(
        jnp.maximum(jnp.abs(mine // size_y - rx), jnp.abs(mine % size_y - ry)), reach_row, taper_ref
    )

    priors = prior_ref[...]
    inside = lane < members
    mean_col = jnp.sum(jnp.where(inside, priors, 0.0), axis=1, keepdims=True) / members
    anomalies = jnp.where(inside, priors - mean_col, 0.0)
    padded = jnp.concatenate([anomalies, jnp.zeros((cols - n_obs, cols), F32)], axis=0)
    unit = jnp.where(lanes_of((members, cols)) == sublanes_of((members, cols)), 1.0, 0.0)
    table = lax.dot_general(
        jnp.concatenate([anomalies, unit], axis=0), padded, NT, precision=HIGHEST, preferred_element_type=F32
    )
    mean = jnp.zeros((1, cols), F32)
    for i in range(n_obs):
        mean = jnp.where(lane1 == i, mean_col[i : i + 1, :], mean)

    scales = jnp.zeros((1, cols), F32)
    increments = []
    for i, k in enumerate(which):
        error = error_ref[k]
        row = table[i : i + 1, :]
        column = table[:, i : i + 1]
        power = row[:, i : i + 1]
        variance = power / (members - 1) + EPS
        inverse = 1.0 / (variance + error)
        scaled = 1.0 / ((members - 1) * variance)
        shift = variance * (value_ref[k] - mean[:, i : i + 1]) * inverse
        shrink = jnp.sqrt(error * inverse) - 1.0
        weight = scaled * own[:, i : i + 1]
        alpha_row = onto_t[i : i + 1, :] * row * scaled
        later = lane1 > i
        h = jnp.where(later, shrink * alpha_row, 0.0)
        q = jnp.where(later, shrink * (row + h * power), 0.0)
        alpha = jnp.concatenate(
            [onto[:, i : i + 1] * column[:n_obs] * scaled, column[n_obs:] * weight], axis=0
        )
        table = table + column * h + alpha * q
        mean = mean + alpha_row * shift
        now = anomalies[i : i + 1, :]
        increments.append(shift + shrink * now)
        anomalies = anomalies + jnp.where(sub > i, shrink * alpha[:n_obs], 0.0) * now
        scales = jnp.where(lane1 == i, weight, scales)
    left = table[n_obs:, :] * scales
    right = jnp.where(inside, jnp.concatenate(increments, axis=0), 0.0)
    right = jnp.concatenate([right, jnp.zeros((cols - n_obs, cols), F32)], axis=0)
    change = jnp.dot(left, right, precision=HIGHEST, preferred_element_type=F32)
    change = jnp.concatenate([change, jnp.zeros((cols - members, cols), F32)], axis=0)
    change = jnp.transpose(change)[:members, :]
    high = change.astype(BF16).astype(F32)
    low = change - high
    zero = jnp.zeros((members, cols), F32)
    high = jnp.concatenate([high, zero], axis=1)
    low = jnp.concatenate([low, zero], axis=1)
    factor = (high + roll_lanes(high, members) + roll_lanes(low, 2 * members)).astype(BF16)

    block = 4
    for at in range(0, 3 * rows, block):
        x = jnp.concatenate([forecast_ref[at + b] for b in range(block)], axis=1)
        xh = x.astype(BF16)
        xl = (x - xh.astype(F32)).astype(BF16)
        stack = jnp.concatenate([xh, xl, xh, jnp.zeros((2 * cols - 3 * members, block * cols), BF16)], axis=0)
        y = x + jnp.dot(factor, stack, preferred_element_type=F32)
        for b in range(block):
            f, r = divmod(at + b, rows)
            out_ref[pl.ds(f * members * rows + r, members, stride=rows), :] = y[:, b * cols : (b + 1) * cols]


def assimilate(place, order, owner, reach, value, error, taper, priors, states, members, rows):
    cols = priors.shape[1]
    return pl.pallas_call(
        functools.partial(assimilate_kernel, members, rows),
        out_shape=jax.ShapeDtypeStruct((3 * members * rows, cols), F32),
        in_specs=[SSPEC] * 7 + [VSPEC] * 2,
        out_specs=VSPEC,
        compiler_params=pltpu.CompilerParams(vmem_limit_bytes=VMEM_LIMIT),
    )(place, order, owner, reach, value, error, taper, priors, states)


def to_neighbours(axis, lower, upper):
    count = lax.axis_size(axis)
    forward = [(i, i + 1) for i in range(count - 1)]
    backward = [(target, source) for source, target in forward]
    return lax.ppermute(upper, axis, forward), lax.ppermute(lower, axis, backward)


def add_over(x, axes):
    for axis in axes:
        count = lax.axis_size(axis)
        if count & (count - 1):
            x = lax.psum(x, axis)
            continue
        span = 1
        while span < count:
            x = x + lax.ppermute(x, axis, [(i, i ^ span) for i in range(count)])
            span *= 2
    return x


def body(status, drag, value, error, taper, order, owner, cell, reach):
    members, rows, cols = status.shape[1:]
    ix, iy = lax.axis_index("gx"), lax.axis_index("gy")
    size_x, size_y = lax.axis_size("gx"), lax.axis_size("gy")
    place = jnp.stack(
        [
            ix * size_y + iy,
            (ix == 0).astype(jnp.int32),
            (ix == size_x - 1).astype(jnp.int32),
            (iy == 0).astype(jnp.int32),
            (iy == size_y - 1).astype(jnp.int32),
            jnp.int32(size_y),
        ]
    ).astype(jnp.int32)
    flat = status.reshape(3 * members * rows, cols)
    upper = status[:, :, rows - MARGIN :, :].reshape(-1, cols)
    lower = status[:, :, :MARGIN, :].reshape(-1, cols)
    above, below = to_neighbours("gy", lower, upper)
    first, last = pack(flat, drag, members)
    left, right = to_neighbours("gx", first, last)
    half = cols // 2
    count = left.shape[0]
    small_lower = jnp.concatenate(
        [jnp.concatenate([left[:, :half], right[:, :half]], axis=1), drag[:MARGIN]], axis=0
    )
    small_upper = jnp.concatenate(
        [jnp.concatenate([left[:, half:], right[:, half:]], axis=1), drag[rows - MARGIN :]], axis=0
    )
    cabove, cbelow = to_neighbours("gy", small_lower, small_upper)
    states, priors = forecast(
        place, order, owner, cell, flat, above, below, left, right, cabove, cbelow,
        drag, cabove[count:], cbelow[count:], members,
    )
    priors = add_over(priors, ("gx", "gy"))
    result = assimilate(place, order, owner, reach, value, error, taper, priors, states, members, rows)
    return result.reshape(status.shape)


def solution(mesh):
    in_specs = (P(None, None, "gy", "gx"), P("gy", "gx"), P(), P(), P(), P(), P(), P(), P())
    out_specs = P(None, None, "gy", "gx")
    return jax.shard_map(body, mesh=mesh, in_specs=in_specs, out_specs=out_specs, check_vma=False)
```

```python
import functools

import jax
import jax.numpy as jnp
from jax import lax
from jax.experimental import pallas as pl
from jax.experimental.pallas import tpu as pltpu
from jax.sharding import PartitionSpec as P

STEPS = 4
MARGIN = 2 * STEPS
EPS = 1e-06
NT = (((1,), (1,)), ((), ()))
HIGHEST = lax.Precision.HIGHEST
F32 = jnp.float32
BF16 = jnp.bfloat16
VMEM_LIMIT = 24 * 1024 * 1024

VSPEC = pl.BlockSpec(memory_space=pltpu.VMEM)
SSPEC = pl.BlockSpec(memory_space=pltpu.SMEM)


def lanes_of(shape):
    return lax.broadcasted_iota(jnp.int32, shape, len(shape) - 1)


def sublanes_of(shape):
    return lax.broadcasted_iota(jnp.int32, shape, len(shape) - 2)


def roll_lanes(x, shift):
    size = x.shape[-1]
    shift = shift % size
    return x if shift == 0 else pltpu.roll(x, shift, x.ndim - 1)


def arrange_kernel(members, rows, x_ref, out_ref, lower_ref, upper_ref, left_ref, right_ref):
    cols = x_ref.shape[1]
    lane = lanes_of((8, cols))

    def group(g, carry):
        here = pl.ds(pl.multiple_of(g * 8, 8), 8)
        for f in range(3):
            left = jnp.zeros((8, cols), F32)
            right = jnp.zeros((8, cols), F32)
            depth = MARGIN if f == 2 else MARGIN - 1
            for r in range(rows):
                row = x_ref[pl.ds((f * members + g * 8) * rows + r, 8, stride=rows), :]
                out_ref[f * rows + r, here, :] = row
                if r < depth:
                    lower_ref[f * (MARGIN - 1) + r, here, :] = row
                if r >= rows - depth:
                    upper_ref[f * (MARGIN - 1) + r - rows + depth, here, :] = row
                there = (lane >= MARGIN * r) & (lane < MARGIN * (r + 1))
                left = jnp.where(there, roll_lanes(row, MARGIN * r), left)
                right = jnp.where(there, roll_lanes(row, MARGIN * (r + 1)), right)
            at = pl.ds(pl.multiple_of(f * members + g * 8, 8), 8)
            left_ref[at, :] = left
            right_ref[at, :] = right
        return carry

    lax.fori_loop(0, members // 8, group, 0)


def arrange(x, members, rows):
    cols = x.shape[1]
    edge = jax.ShapeDtypeStruct((3 * members, cols), F32)
    band = jax.ShapeDtypeStruct((3 * MARGIN - 2, members, cols), F32)
    return pl.pallas_call(
        functools.partial(arrange_kernel, members, rows),
        out_shape=(jax.ShapeDtypeStruct((3 * rows, members, cols), F32), band, band, edge, edge),
        in_specs=[VSPEC],
        out_specs=(VSPEC,) * 5,
        compiler_params=pltpu.CompilerParams(vmem_limit_bytes=VMEM_LIMIT),
        cost_estimate=pl.CostEstimate(flops=4_000_000, bytes_accessed=6_000_000, transcendentals=0),
    )(x)


def grid_factor(place_ref, shape, rows, cols):
    row, col = sublanes_of(shape), lanes_of(shape)
    wide = 2 * cols
    low, high = jnp.where(place_ref[3] == 1, MARGIN, 0), jnp.where(place_ref[4] == 1, MARGIN + rows, rows + 2 * MARGIN)
    first, last = jnp.where(place_ref[1] == 1, wide, wide - MARGIN), jnp.where(place_ref[2] == 1, cols, cols + MARGIN)
    ok = (row >= low) & (row < high) & ((col < last) | (col >= first))
    return jnp.where(ok, 1.0, 0.0)


def share_kernel(
    members, rows,
    place_ref, order_ref, owner_ref, cell_ref, state_ref, drag_ref, even_ref, odd_ref,
    keep_ref, prior_ref, turned,
):
    cols = drag_ref.shape[1]
    wide = 2 * cols
    total = rows + 2 * MARGIN
    size_y = place_ref[5]
    ix, iy = place_ref[0] // size_y, place_ref[0] % size_y
    shape = (total, wide)
    lane = lanes_of((total, cols))
    odd = (ix % 2) == 1
    even_part, odd_part = even_ref[...], odd_ref[...]
    before = jnp.where(odd, even_part, odd_part)
    after = jnp.where(odd, odd_part, even_part)
    drag = jnp.concatenate([drag_ref[...], jnp.where(lane < cols // 2, after, before)], axis=1)
    keep = 1.0 - drag
    keep_ref[...] = keep
    slope = 0.2 * grid_factor(place_ref, shape, rows, cols)
    sub, wlane = sublanes_of(shape), lanes_of(shape)
    turned[...] = jnp.zeros_like(turned)
    spot = lanes_of((members, cols))

    def one(i, carry):
        k = order_ref[i]
        tile, cell = owner_ref[k], cell_ref[k]
        field, inner = cell // (rows * cols), cell % (rows * cols)
        row = (tile % size_y - iy) * rows + inner // cols
        col = (tile // size_y - ix) * cols + inner % cols
        near = (row >= -MARGIN) & (row < rows + MARGIN) & (col >= -MARGIN) & (col < cols + MARGIN)

        @pl.when(near)
        def _():
            at = jnp.where(col < 0, col + wide, col)
            start = jnp.where((sub == row + MARGIN) & (wlane == at), 1.0, 0.0)
            h = jnp.where(field == 0, start, 0.0)
            u = jnp.where(field == 1, start, 0.0)
            v = jnp.where(field == 2, start, 0.0)
            for _step in range(STEPS):
                h = h + slope * (
                    (roll_lanes(u, -1) - roll_lanes(u, 1)) + (pltpu.roll(v, total - 1, 0) - pltpu.roll(v, 1, 0))
                )
                u, v = (
                    keep * u + slope * (roll_lanes(h, -1) - roll_lanes(h, 1)) - 0.1 * v,
                    keep * v + slope * (pltpu.roll(h, total - 1, 0) - pltpu.roll(h, 1, 0)) + 0.1 * u,
                )
            sums = jnp.zeros((members, cols), F32)
            for f, weights in enumerate((h, u, v)):
                for r in range(rows):
                    sums = sums + weights[MARGIN + r : MARGIN + r + 1, :cols] * state_ref[f * rows + r]
            column = jnp.sum(sums, axis=1, keepdims=True)
            turned[0:members, :] = jnp.where(spot == i, column, turned[0:members, :])

        return carry

    lax.fori_loop(0, order_ref.shape[0], one, 0)
    prior_ref[...] = jnp.transpose(turned[...])[: prior_ref.shape[0]]


def share(place, order, owner, cell, states, drag, even, odd, members, rows):
    cols = drag.shape[1]
    return pl.pallas_call(
        functools.partial(share_kernel, members, rows),
        out_shape=(
            jax.ShapeDtypeStruct((drag.shape[0], 2 * cols), F32),
            jax.ShapeDtypeStruct((order.shape[0], cols), F32),
        ),
        in_specs=[SSPEC] * 4 + [VSPEC] * 4,
        out_specs=(VSPEC, VSPEC),
        scratch_shapes=[pltpu.VMEM((cols, cols), F32)],
        compiler_params=pltpu.CompilerParams(vmem_limit_bytes=VMEM_LIMIT),
        cost_estimate=pl.CostEstimate(flops=6_000_000, bytes_accessed=2_000_000, transcendentals=0),
    )(place, order, owner, cell, states, drag, even, odd)


def wide_row(lane, main, left, left_at, right, right_at):
    cols = main.shape[1]
    halo = jnp.where(lane >= cols - MARGIN, roll_lanes(left, cols - MARGIN - left_at), 0.0)
    halo = jnp.where(lane < MARGIN, roll_lanes(right, -right_at), halo)
    return jnp.concatenate([main, halo], axis=1)


def forecast_kernel(
    members, rows,
    place_ref, state_ref, above_ref, below_ref, left_ref, right_ref, cabove_ref, cbelow_ref, keep_ref,
    out_ref,
    state, keep, slope,
):
    cols = state_ref.shape[2]
    wide = 2 * cols
    total = rows + 2 * MARGIN
    lane = lanes_of((8, cols))
    half = cols // 2
    factor = -0.2 * grid_factor(place_ref, (total, wide), rows, cols)
    for r in range(total):
        keep[r] = jnp.broadcast_to(keep_ref[r : r + 1, :], (8, wide))
        slope[r] = jnp.broadcast_to(factor[r : r + 1, :], (8, wide))

    def group(g, carry):
        here = pl.ds(pl.multiple_of(g * 8, 8), 8)
        for f in range(3):
            at = pl.ds(pl.multiple_of(f * members + g * 8, 8), 8)
            ledge, redge = left_ref[at, :], right_ref[at, :]
            cab, cbe = cabove_ref[at, :], cbelow_ref[at, :]
            depth = MARGIN if f == 2 else MARGIN - 1
            for r in range(MARGIN - depth, MARGIN + rows + depth):
                if r < MARGIN:
                    main = above_ref[f * (MARGIN - 1) + r - MARGIN + depth, here, :]
                    value = wide_row(lane, main, cab, MARGIN * r, cab, half + MARGIN * r)
                elif r < MARGIN + rows:
                    q = r - MARGIN
                    main = state_ref[f * rows + q, here, :]
                    value = wide_row(lane, main, ledge, MARGIN * q, redge, MARGIN * q)
                else:
                    q = r - MARGIN - rows
                    main = below_ref[f * (MARGIN - 1) + q, here, :]
                    value = wide_row(lane, main, cbe, MARGIN * q, cbe, half + MARGIN * q)
                state[f, r] = value
        for step in range(STEPS):
            reach = 2 * (STEPS - step) - 1
            for r in range(MARGIN - reach, MARGIN + rows + reach):
                u = state[1, r]
                div = (roll_lanes(u, -1) - roll_lanes(u, 1)) + (state[2, r + 1] - state[2, r - 1])
                state[0, r] = state[0, r] + slope[r] * div
            reach -= 1
            for r in range(MARGIN - reach, MARGIN + rows + reach):
                h = state[0, r]
                u, v = state[1, r], state[2, r]
                k, c = keep[r], slope[r]
                state[1, r] = k * u + c * (roll_lanes(h, -1) - roll_lanes(h, 1)) + 0.1 * v
                state[2, r] = k * v + c * (state[0, r + 1] - state[0, r - 1]) - 0.1 * u
        for f in range(3):
            for r in range(rows):
                out_ref[f * rows + r, here, :] = state[f, MARGIN + r, :, 0:cols]
        return carry

    lax.fori_loop(0, members // 8, group, 0)


def forecast(place, states, above, below, left, right, cabove, cbelow, keep):
    members, cols = states.shape[1:]
    rows = states.shape[0] // 3
    total = rows + 2 * MARGIN
    return pl.pallas_call(
        functools.partial(forecast_kernel, members, rows),
        out_shape=jax.ShapeDtypeStruct(states.shape, F32),
        in_specs=[SSPEC] + [VSPEC] * 8,
        out_specs=VSPEC,
        scratch_shapes=[
            pltpu.VMEM((3, total, 8, 2 * cols), F32),
            pltpu.VMEM((total, 8, 2 * cols), F32),
            pltpu.VMEM((total, 8, 2 * cols), F32),
        ],
        compiler_params=pltpu.CompilerParams(vmem_limit_bytes=VMEM_LIMIT),
        cost_estimate=pl.CostEstimate(flops=60_000_000, bytes_accessed=30_000_000, transcendentals=0),
    )(place, states, above, below, left, right, cabove, cbelow, keep)


def localize(distance, reach, taper_ref):
    picked = jnp.zeros(distance.shape, F32)
    levels = taper_ref.shape[0]
    capped = jnp.minimum(distance, levels - 1)
    for d in range(levels):
        picked = jnp.where(capped == d, taper_ref[d], picked)
    return jnp.where(distance <= reach, picked, 0.0)


def assimilate_kernel(
    members, rows,
    place_ref, order_ref, owner_ref, reach_ref, value_ref, error_ref, taper_ref,
    prior_ref, forecast_ref,
    out_ref,
):
    n_obs = order_ref.shape[0]
    cols = prior_ref.shape[1]
    size_y = place_ref[5]
    lane1 = lanes_of((1, cols))
    lane = lanes_of((n_obs, cols))
    sub = sublanes_of((n_obs, cols))

    tile_row = jnp.zeros((1, cols), jnp.int32)
    tile_col = jnp.zeros((n_obs, cols), jnp.int32)
    reach_row = jnp.zeros((1, cols), jnp.int32)
    reach_col = jnp.zeros((n_obs, cols), jnp.int32)
    which = [order_ref[i] for i in range(n_obs)]
    for i, k in enumerate(which):
        tile_row = jnp.where(lane1 == i, owner_ref[k], tile_row)
        tile_col = jnp.where(sub == i, owner_ref[k], tile_col)
        reach_row = jnp.where(lane1 == i, reach_ref[k], reach_row)
        reach_col = jnp.where(sub == i, reach_ref[k], reach_col)
    rx, ry = tile_row // size_y, tile_row % size_y
    cx, cy = tile_col // size_y, tile_col % size_y
    distance = jnp.maximum(jnp.abs(cx - rx), jnp.abs(cy - ry))
    onto = localize(distance, reach_row, taper_ref)
    onto_t = localize(distance, reach_col, taper_ref)
    mine = place_ref[0]
    own = localize(
        jnp.maximum(jnp.abs(mine // size_y - rx), jnp.abs(mine % size_y - ry)), reach_row, taper_ref
    )

    priors = prior_ref[...]
    inside = lane < members
    mean_col = jnp.sum(jnp.where(inside, priors, 0.0), axis=1, keepdims=True) / members
    anomalies = jnp.where(inside, priors - mean_col, 0.0)
    padded = jnp.concatenate([anomalies, jnp.zeros((cols - n_obs, cols), F32)], axis=0)
    unit = jnp.where(lanes_of((members, cols)) == sublanes_of((members, cols)), 1.0, 0.0)
    table = lax.dot_general(
        jnp.concatenate([anomalies, unit], axis=0), padded, NT, precision=HIGHEST, preferred_element_type=F32
    )
    mean = jnp.zeros((1, cols), F32)
    for i in range(n_obs):
        mean = jnp.where(lane1 == i, mean_col[i : i + 1, :], mean)

    scales = jnp.zeros((1, cols), F32)
    increments = []
    for i, k in enumerate(which):
        error = error_ref[k]
        row = table[i : i + 1, :]
        column = table[:, i : i + 1]
        power = row[:, i : i + 1]
        variance = power / (members - 1) + EPS
        inverse = 1.0 / (variance + error)
        scaled = 1.0 / ((members - 1) * variance)
        shift = variance * (value_ref[k] - mean[:, i : i + 1]) * inverse
        shrink = jnp.sqrt(error * inverse) - 1.0
        weight = scaled * own[:, i : i + 1]
        alpha_row = onto_t[i : i + 1, :] * row * scaled
        later = lane1 > i
        h = jnp.where(later, shrink * alpha_row, 0.0)
        q = jnp.where(later, shrink * (row + h * power), 0.0)
        alpha = jnp.concatenate(
            [onto[:, i : i + 1] * column[:n_obs] * scaled, column[n_obs:] * weight], axis=0
        )
        table = table + column * h + alpha * q
        mean = mean + alpha_row * shift
        now = anomalies[i : i + 1, :]
        increments.append(shift + shrink * now)
        anomalies = anomalies + jnp.where(sub > i, shrink * alpha[:n_obs], 0.0) * now
        scales = jnp.where(lane1 == i, weight, scales)
    left = table[n_obs:, :] * scales
    right = jnp.where(inside, jnp.concatenate(increments, axis=0), 0.0)
    right = jnp.concatenate([right, jnp.zeros((cols - n_obs, cols), F32)], axis=0)
    change = jnp.dot(left, right, precision=HIGHEST, preferred_element_type=F32)
    change = jnp.concatenate([change, jnp.zeros((cols - members, cols), F32)], axis=0)
    change = jnp.transpose(change)[:members, :]
    high = change.astype(BF16).astype(F32)
    low = change - high
    zero = jnp.zeros((members, cols), F32)
    high = jnp.concatenate([high, zero], axis=1)
    low = jnp.concatenate([low, zero], axis=1)
    factor = (high + roll_lanes(high, members) + roll_lanes(low, 2 * members)).astype(BF16)

    block = 4
    for at in range(0, 3 * rows, block):
        x = jnp.concatenate([forecast_ref[at + b] for b in range(block)], axis=1)
        xh = x.astype(BF16)
        xl = (x - xh.astype(F32)).astype(BF16)
        stack = jnp.concatenate([xh, xl, xh, jnp.zeros((2 * cols - 3 * members, block * cols), BF16)], axis=0)
        y = x + jnp.dot(factor, stack, preferred_element_type=F32)
        for b in range(block):
            f, r = divmod(at + b, rows)
            out_ref[pl.ds(f * members * rows + r, members, stride=rows), :] = y[:, b * cols : (b + 1) * cols]


def assimilate(place, order, owner, reach, value, error, taper, priors, states, members, rows):
    cols = priors.shape[1]
    return pl.pallas_call(
        functools.partial(assimilate_kernel, members, rows),
        out_shape=jax.ShapeDtypeStruct((3 * members * rows, cols), F32),
        in_specs=[SSPEC] * 7 + [VSPEC] * 2,
        out_specs=VSPEC,
        compiler_params=pltpu.CompilerParams(vmem_limit_bytes=VMEM_LIMIT),
    )(place, order, owner, reach, value, error, taper, priors, states)


def to_neighbours(axis, lower, upper):
    count = lax.axis_size(axis)
    forward = [(i, i + 1) for i in range(count - 1)]
    backward = [(target, source) for source, target in forward]
    return lax.ppermute(upper, axis, forward), lax.ppermute(lower, axis, backward)


def swap_pairs(x, axis):
    count = lax.axis_size(axis)

    def swap(start):
        pairs = [(i, i + 1) for i in range(start, count - 1, 2)]
        return lax.ppermute(x, axis, pairs + [(b, a) for a, b in pairs])

    return swap(0), swap(1)


def add_over(x, axes):
    for axis in axes:
        count = lax.axis_size(axis)
        if count & (count - 1):
            x = lax.psum(x, axis)
            continue
        span = 1
        while span < count:
            x = x + lax.ppermute(x, axis, [(i, i ^ span) for i in range(count)])
            span *= 2
    return x


def body(status, drag, value, error, taper, order, owner, cell, reach):
    members, rows, cols = status.shape[1:]
    ix, iy = lax.axis_index("gx"), lax.axis_index("gy")
    size_x, size_y = lax.axis_size("gx"), lax.axis_size("gy")
    place = jnp.stack(
        [
            ix * size_y + iy,
            (ix == 0).astype(jnp.int32),
            (ix == size_x - 1).astype(jnp.int32),
            (iy == 0).astype(jnp.int32),
            (iy == size_y - 1).astype(jnp.int32),
            jnp.int32(size_y),
        ]
    ).astype(jnp.int32)
    flat = status.reshape(3 * members * rows, cols)
    even, odd = swap_pairs(drag, "gy")
    is_odd = (iy % 2) == 1
    above = jnp.where(is_odd, even[rows - MARGIN :], odd[rows - MARGIN :])
    below = jnp.where(is_odd, odd[:MARGIN], even[:MARGIN])
    drag = jnp.concatenate([above, drag, below], axis=0)
    even, odd = swap_pairs(drag, "gx")

    states, lower, upper, first, last = arrange(flat, members, rows)
    above, below = to_neighbours("gy", lower, upper)
    keep, priors = share(place, order, owner, cell, states, drag, even, odd, members, rows)
    left, right = to_neighbours("gx", first, last)
    half = cols // 2
    small_lower = jnp.concatenate([left[:, :half], right[:, :half]], axis=1)
    small_upper = jnp.concatenate([left[:, half:], right[:, half:]], axis=1)
    cabove, cbelow = to_neighbours("gy", small_lower, small_upper)
    states = forecast(place, states, above, below, left, right, cabove, cbelow, keep)
    priors = add_over(priors, ("gx", "gy"))
    result = assimilate(place, order, owner, reach, value, error, taper, priors, states, members, rows)
    return result.reshape(status.shape)


def solution(mesh):
    in_specs = (P(None, None, "gy", "gx"), P("gy", "gx"), P(), P(), P(), P(), P(), P(), P())
    out_specs = P(None, None, "gy", "gx")
    return jax.shard_map(body, mesh=mesh, in_specs=in_specs, out_specs=out_specs, check_vma=False)
```

```python
import functools

import jax
import jax.numpy as jnp
from jax import lax
from jax.experimental import pallas as pl
from jax.experimental.pallas import tpu as pltpu
from jax.sharding import PartitionSpec as P

STEPS = 4
MARGIN = 2 * STEPS
EPS = 1e-06
NT = (((1,), (1,)), ((), ()))
HIGHEST = lax.Precision.HIGHEST
F32 = jnp.float32
BF16 = jnp.bfloat16
VMEM_LIMIT = 12 * 1024 * 1024

VSPEC = pl.BlockSpec(memory_space=pltpu.VMEM)
SSPEC = pl.BlockSpec(memory_space=pltpu.SMEM)


def lanes_of(shape):
    return lax.broadcasted_iota(jnp.int32, shape, len(shape) - 1)


def sublanes_of(shape):
    return lax.broadcasted_iota(jnp.int32, shape, len(shape) - 2)


def roll_lanes(x, shift):
    size = x.shape[-1]
    shift = shift % size
    return x if shift == 0 else pltpu.roll(x, shift, x.ndim - 1)


def arrange_kernel(members, rows, x_ref, out_ref, lower_ref, upper_ref, left_ref, right_ref):
    cols = x_ref.shape[1]
    lane = lanes_of((8, cols))

    def group(g, carry):
        here = pl.ds(pl.multiple_of(g * 8, 8), 8)
        for f in range(3):
            left = jnp.zeros((8, cols), F32)
            right = jnp.zeros((8, cols), F32)
            depth = MARGIN if f == 2 else MARGIN - 1
            for r in range(rows):
                row = x_ref[pl.ds((f * members + g * 8) * rows + r, 8, stride=rows), :]
                out_ref[f * rows + r, here, :] = row
                if r < depth:
                    lower_ref[f * (MARGIN - 1) + r, here, :] = row
                if r >= rows - depth:
                    upper_ref[f * (MARGIN - 1) + r - rows + depth, here, :] = row
                there = (lane >= MARGIN * r) & (lane < MARGIN * (r + 1))
                left = jnp.where(there, roll_lanes(row, MARGIN * r), left)
                right = jnp.where(there, roll_lanes(row, MARGIN * (r + 1)), right)
            at = pl.ds(pl.multiple_of(f * members + g * 8, 8), 8)
            left_ref[at, :] = left
            right_ref[at, :] = right
        return carry

    lax.fori_loop(0, members // 8, group, 0)


def arrange(x, members, rows):
    cols = x.shape[1]
    edge = jax.ShapeDtypeStruct((3 * members, cols), F32)
    band = jax.ShapeDtypeStruct((3 * MARGIN - 2, members, cols), F32)
    return pl.pallas_call(
        functools.partial(arrange_kernel, members, rows),
        out_shape=(jax.ShapeDtypeStruct((3 * rows, members, cols), F32), band, band, edge, edge),
        in_specs=[VSPEC],
        out_specs=(VSPEC,) * 5,
        compiler_params=pltpu.CompilerParams(vmem_limit_bytes=VMEM_LIMIT),
        cost_estimate=pl.CostEstimate(flops=4_000_000, bytes_accessed=6_000_000, transcendentals=0),
    )(x)


def extend_kernel(place_ref, drag_ref, even_ref, odd_ref, first_ref, last_ref, drag_out, lower_ref, upper_ref):
    rows = drag_ref.shape[0]
    count = first_ref.shape[0]
    odd = place_ref[0] % place_ref[5] % 2 == 1
    above = jnp.where(odd, even_ref[rows - MARGIN :, :], odd_ref[rows - MARGIN :, :])
    below = jnp.where(odd, odd_ref[:MARGIN, :], even_ref[:MARGIN, :])
    drag = jnp.concatenate([above, drag_ref[...], below], axis=0)
    drag_out[...] = drag
    lower_ref[:count, :] = first_ref[...]
    upper_ref[:count, :] = last_ref[...]
    lower_ref[count:, :] = drag
    upper_ref[count:, :] = drag


def extend(place, drag, even, odd, first, last):
    rows, cols = drag.shape
    total = rows + 2 * MARGIN
    message = jax.ShapeDtypeStruct((first.shape[0] + total, cols), F32)
    return pl.pallas_call(
        extend_kernel,
        out_shape=(jax.ShapeDtypeStruct((total, cols), F32), message, message),
        in_specs=[SSPEC] + [VSPEC] * 5,
        out_specs=(VSPEC,) * 3,
        compiler_params=pltpu.CompilerParams(vmem_limit_bytes=VMEM_LIMIT),
    )(place, drag, even, odd, first, last)


def grid_factor(place_ref, shape, rows, cols):
    row, col = sublanes_of(shape), lanes_of(shape)
    wide = 2 * cols
    low, high = jnp.where(place_ref[3] == 1, MARGIN, 0), jnp.where(place_ref[4] == 1, MARGIN + rows, rows + 2 * MARGIN)
    first, last = jnp.where(place_ref[1] == 1, wide, wide - MARGIN), jnp.where(place_ref[2] == 1, cols, cols + MARGIN)
    ok = (row >= low) & (row < high) & ((col < last) | (col >= first))
    return jnp.where(ok, 1.0, 0.0)


def share_kernel(
    members, rows,
    place_ref, order_ref, owner_ref, cell_ref, state_ref, drag_ref, before_ref, after_ref,
    keep_ref, prior_ref, turned,
):
    cols = drag_ref.shape[1]
    wide = 2 * cols
    total = rows + 2 * MARGIN
    size_y = place_ref[5]
    ix, iy = place_ref[0] // size_y, place_ref[0] % size_y
    shape = (total, wide)
    lane = lanes_of((total, cols))
    margins = jnp.where(lane < cols // 2, after_ref[...], before_ref[...])
    drag = jnp.concatenate([drag_ref[...], margins], axis=1)
    keep = 1.0 - drag
    keep_ref[...] = keep
    slope = 0.2 * grid_factor(place_ref, shape, rows, cols)
    sub, wlane = sublanes_of(shape), lanes_of(shape)
    turned[...] = jnp.zeros_like(turned)
    spot = lanes_of((members, cols))

    def one(i, carry):
        k = order_ref[i]
        tile, cell = owner_ref[k], cell_ref[k]
        field, inner = cell // (rows * cols), cell % (rows * cols)
        row = (tile % size_y - iy) * rows + inner // cols
        col = (tile // size_y - ix) * cols + inner % cols
        near = (row >= -MARGIN) & (row < rows + MARGIN) & (col >= -MARGIN) & (col < cols + MARGIN)

        @pl.when(near)
        def _():
            at = jnp.where(col < 0, col + wide, col)
            start = jnp.where((sub == row + MARGIN) & (wlane == at), 1.0, 0.0)
            h = jnp.where(field == 0, start, 0.0)
            u = jnp.where(field == 1, start, 0.0)
            v = jnp.where(field == 2, start, 0.0)
            for _step in range(STEPS):
                h = h + slope * (
                    (roll_lanes(u, -1) - roll_lanes(u, 1)) + (pltpu.roll(v, total - 1, 0) - pltpu.roll(v, 1, 0))
                )
                u, v = (
                    keep * u + slope * (roll_lanes(h, -1) - roll_lanes(h, 1)) - 0.1 * v,
                    keep * v + slope * (pltpu.roll(h, total - 1, 0) - pltpu.roll(h, 1, 0)) + 0.1 * u,
                )
            sums = jnp.zeros((members, cols), F32)
            for f, weights in enumerate((h, u, v)):
                for r in range(rows):
                    sums = sums + weights[MARGIN + r : MARGIN + r + 1, :cols] * state_ref[f * rows + r]
            column = jnp.sum(sums, axis=1, keepdims=True)
            turned[0:members, :] = jnp.where(spot == i, column, turned[0:members, :])

        return carry

    lax.fori_loop(0, order_ref.shape[0], one, 0)
    prior_ref[...] = jnp.transpose(turned[...])[: prior_ref.shape[0]]


def share(place, order, owner, cell, states, drag, before, after, members, rows):
    cols = drag.shape[1]
    return pl.pallas_call(
        functools.partial(share_kernel, members, rows),
        out_shape=(
            jax.ShapeDtypeStruct((drag.shape[0], 2 * cols), F32),
            jax.ShapeDtypeStruct((order.shape[0], cols), F32),
        ),
        in_specs=[SSPEC] * 4 + [VSPEC] * 4,
        out_specs=(VSPEC, VSPEC),
        scratch_shapes=[pltpu.VMEM((cols, cols), F32)],
        compiler_params=pltpu.CompilerParams(vmem_limit_bytes=VMEM_LIMIT),
        cost_estimate=pl.CostEstimate(flops=6_000_000, bytes_accessed=2_000_000, transcendentals=0),
    )(place, order, owner, cell, states, drag, before, after)


def wide_row(lane, main, left, left_at, right, right_at):
    cols = main.shape[1]
    halo = jnp.where(lane >= cols - MARGIN, roll_lanes(left, cols - MARGIN - left_at), 0.0)
    halo = jnp.where(lane < MARGIN, roll_lanes(right, -right_at), halo)
    return jnp.concatenate([main, halo], axis=1)


def forecast_kernel(
    members, rows,
    place_ref, state_ref, above_ref, below_ref, left_ref, right_ref, cabove_ref, cbelow_ref, keep_ref,
    out_ref,
    state, keep, slope,
):
    cols = state_ref.shape[2]
    wide = 2 * cols
    total = rows + 2 * MARGIN
    lane = lanes_of((8, cols))
    half = cols // 2
    factor = -0.2 * grid_factor(place_ref, (total, wide), rows, cols)
    for r in range(total):
        keep[r] = jnp.broadcast_to(keep_ref[r : r + 1, :], (8, wide))
        slope[r] = jnp.broadcast_to(factor[r : r + 1, :], (8, wide))

    def group(g, carry):
        here = pl.ds(pl.multiple_of(g * 8, 8), 8)
        for f in range(3):
            at = pl.ds(pl.multiple_of(f * members + g * 8, 8), 8)
            ledge, redge = left_ref[at, :], right_ref[at, :]
            cab, cbe = cabove_ref[at, :], cbelow_ref[at, :]
            depth = MARGIN if f == 2 else MARGIN - 1
            for r in range(MARGIN - depth, MARGIN + rows + depth):
                if r < MARGIN:
                    main = above_ref[f * (MARGIN - 1) + r - MARGIN + depth, here, :]
                    value = wide_row(lane, main, cab, MARGIN * r, cab, half + MARGIN * r)
                elif r < MARGIN + rows:
                    q = r - MARGIN
                    main = state_ref[f * rows + q, here, :]
                    value = wide_row(lane, main, ledge, MARGIN * q, redge, MARGIN * q)
                else:
                    q = r - MARGIN - rows
                    main = below_ref[f * (MARGIN - 1) + q, here, :]
                    value = wide_row(lane, main, cbe, MARGIN * q, cbe, half + MARGIN * q)
                state[f, r] = value
        for step in range(STEPS):
            reach = 2 * (STEPS - step) - 1
            for r in range(MARGIN - reach, MARGIN + rows + reach):
                u = state[1, r]
                div = (roll_lanes(u, -1) - roll_lanes(u, 1)) + (state[2, r + 1] - state[2, r - 1])
                state[0, r] = state[0, r] + slope[r] * div
            reach -= 1
            for r in range(MARGIN - reach, MARGIN + rows + reach):
                h = state[0, r]
                u, v = state[1, r], state[2, r]
                k, c = keep[r], slope[r]
                state[1, r] = k * u + c * (roll_lanes(h, -1) - roll_lanes(h, 1)) + 0.1 * v
                state[2, r] = k * v + c * (state[0, r + 1] - state[0, r - 1]) - 0.1 * u
        for f in range(3):
            for r in range(rows):
                out_ref[f * rows + r, here, :] = state[f, MARGIN + r, :, 0:cols]
        return carry

    lax.fori_loop(0, members // 8, group, 0)


def forecast(place, states, above, below, left, right, cabove, cbelow, keep):
    members, cols = states.shape[1:]
    rows = states.shape[0] // 3
    total = rows + 2 * MARGIN
    return pl.pallas_call(
        functools.partial(forecast_kernel, members, rows),
        out_shape=jax.ShapeDtypeStruct(states.shape, F32),
        in_specs=[SSPEC] + [VSPEC] * 8,
        out_specs=VSPEC,
        scratch_shapes=[
            pltpu.VMEM((3, total, 8, 2 * cols), F32),
            pltpu.VMEM((total, 8, 2 * cols), F32),
            pltpu.VMEM((total, 8, 2 * cols), F32),
        ],
        compiler_params=pltpu.CompilerParams(vmem_limit_bytes=VMEM_LIMIT),
        cost_estimate=pl.CostEstimate(flops=60_000_000, bytes_accessed=30_000_000, transcendentals=0),
    )(place, states, above, below, left, right, cabove, cbelow, keep)


def localize(distance, reach, taper_ref):
    picked = jnp.zeros(distance.shape, F32)
    levels = taper_ref.shape[0]
    capped = jnp.minimum(distance, levels - 1)
    for d in range(levels):
        picked = jnp.where(capped == d, taper_ref[d], picked)
    return jnp.where(distance <= reach, picked, 0.0)


def assimilate_kernel(
    members, rows,
    place_ref, order_ref, owner_ref, reach_ref, value_ref, error_ref, taper_ref,
    prior_ref, forecast_ref,
    out_ref,
):
    n_obs = order_ref.shape[0]
    cols = prior_ref.shape[1]
    size_y = place_ref[5]
    lane1 = lanes_of((1, cols))
    lane = lanes_of((n_obs, cols))
    sub = sublanes_of((n_obs, cols))

    tile_row = jnp.zeros((1, cols), jnp.int32)
    tile_col = jnp.zeros((n_obs, cols), jnp.int32)
    reach_row = jnp.zeros((1, cols), jnp.int32)
    reach_col = jnp.zeros((n_obs, cols), jnp.int32)
    which = [order_ref[i] for i in range(n_obs)]
    for i, k in enumerate(which):
        tile_row = jnp.where(lane1 == i, owner_ref[k], tile_row)
        tile_col = jnp.where(sub == i, owner_ref[k], tile_col)
        reach_row = jnp.where(lane1 == i, reach_ref[k], reach_row)
        reach_col = jnp.where(sub == i, reach_ref[k], reach_col)
    rx, ry = tile_row // size_y, tile_row % size_y
    cx, cy = tile_col // size_y, tile_col % size_y
    distance = jnp.maximum(jnp.abs(cx - rx), jnp.abs(cy - ry))
    onto = localize(distance, reach_row, taper_ref)
    onto_t = localize(distance, reach_col, taper_ref)
    mine = place_ref[0]
    own = localize(
        jnp.maximum(jnp.abs(mine // size_y - rx), jnp.abs(mine % size_y - ry)), reach_row, taper_ref
    )

    priors = prior_ref[...]
    inside = lane < members
    mean_col = jnp.sum(jnp.where(inside, priors, 0.0), axis=1, keepdims=True) / members
    anomalies = jnp.where(inside, priors - mean_col, 0.0)
    padded = jnp.concatenate([anomalies, jnp.zeros((cols - n_obs, cols), F32)], axis=0)
    unit = jnp.where(lanes_of((members, cols)) == sublanes_of((members, cols)), 1.0, 0.0)
    table = lax.dot_general(
        jnp.concatenate([anomalies, unit], axis=0), padded, NT, precision=HIGHEST, preferred_element_type=F32
    )
    mean = jnp.zeros((1, cols), F32)
    for i in range(n_obs):
        mean = jnp.where(lane1 == i, mean_col[i : i + 1, :], mean)

    scales = jnp.zeros((1, cols), F32)
    increments = []
    for i, k in enumerate(which):
        error = error_ref[k]
        row = table[i : i + 1, :]
        column = table[:, i : i + 1]
        power = row[:, i : i + 1]
        variance = power / (members - 1) + EPS
        inverse = 1.0 / (variance + error)
        scaled = 1.0 / ((members - 1) * variance)
        shift = variance * (value_ref[k] - mean[:, i : i + 1]) * inverse
        shrink = jnp.sqrt(error * inverse) - 1.0
        weight = scaled * own[:, i : i + 1]
        alpha_row = onto_t[i : i + 1, :] * row * scaled
        later = lane1 > i
        h = jnp.where(later, shrink * alpha_row, 0.0)
        q = jnp.where(later, shrink * (row + h * power), 0.0)
        alpha = jnp.concatenate(
            [onto[:, i : i + 1] * column[:n_obs] * scaled, column[n_obs:] * weight], axis=0
        )
        table = table + column * h + alpha * q
        mean = mean + alpha_row * shift
        now = anomalies[i : i + 1, :]
        increments.append(shift + shrink * now)
        anomalies = anomalies + jnp.where(sub > i, shrink * alpha[:n_obs], 0.0) * now
        scales = jnp.where(lane1 == i, weight, scales)
    left = table[n_obs:, :] * scales
    right = jnp.where(inside, jnp.concatenate(increments, axis=0), 0.0)
    right = jnp.concatenate([right, jnp.zeros((cols - n_obs, cols), F32)], axis=0)
    change = jnp.dot(left, right, precision=HIGHEST, preferred_element_type=F32)
    change = jnp.concatenate([change, jnp.zeros((cols - members, cols), F32)], axis=0)
    change = jnp.transpose(change)[:members, :]
    high = change.astype(BF16).astype(F32)
    low = change - high
    zero = jnp.zeros((members, cols), F32)
    high = jnp.concatenate([high, zero], axis=1)
    low = jnp.concatenate([low, zero], axis=1)
    factor = (high + roll_lanes(high, members) + roll_lanes(low, 2 * members)).astype(BF16)

    block = 4
    for at in range(0, 3 * rows, block):
        x = jnp.concatenate([forecast_ref[at + b] for b in range(block)], axis=1)
        xh = x.astype(BF16)
        xl = (x - xh.astype(F32)).astype(BF16)
        stack = jnp.concatenate([xh, xl, xh, jnp.zeros((2 * cols - 3 * members, block * cols), BF16)], axis=0)
        y = x + jnp.dot(factor, stack, preferred_element_type=F32)
        for b in range(block):
            f, r = divmod(at + b, rows)
            out_ref[pl.ds(f * members * rows + r, members, stride=rows), :] = y[:, b * cols : (b + 1) * cols]


def assimilate(place, order, owner, reach, value, error, taper, priors, states, members, rows):
    cols = priors.shape[1]
    return pl.pallas_call(
        functools.partial(assimilate_kernel, members, rows),
        out_shape=jax.ShapeDtypeStruct((3 * members * rows, cols), F32),
        in_specs=[SSPEC] * 7 + [VSPEC] * 2,
        out_specs=VSPEC,
        compiler_params=pltpu.CompilerParams(vmem_limit_bytes=VMEM_LIMIT),
    )(place, order, owner, reach, value, error, taper, priors, states)


def to_neighbours(axis, lower, upper):
    count = lax.axis_size(axis)
    forward = [(i, i + 1) for i in range(count - 1)]
    backward = [(target, source) for source, target in forward]
    return lax.ppermute(upper, axis, forward), lax.ppermute(lower, axis, backward)


def swap_pairs(x, axis):
    count = lax.axis_size(axis)

    def swap(start):
        pairs = [(i, i + 1) for i in range(start, count - 1, 2)]
        return lax.ppermute(x, axis, pairs + [(b, a) for a, b in pairs])

    return swap(0), swap(1)


def add_over(x, axes):
    for axis in axes:
        count = lax.axis_size(axis)
        if count & (count - 1):
            x = lax.psum(x, axis)
            continue
        span = 1
        while span < count:
            x = x + lax.ppermute(x, axis, [(i, i ^ span) for i in range(count)])
            span *= 2
    return x


def body(status, drag, value, error, taper, order, owner, cell, reach):
    members, rows, cols = status.shape[1:]
    ix, iy = lax.axis_index("gx"), lax.axis_index("gy")
    size_x, size_y = lax.axis_size("gx"), lax.axis_size("gy")
    place = jnp.stack(
        [
            ix * size_y + iy,
            (ix == 0).astype(jnp.int32),
            (ix == size_x - 1).astype(jnp.int32),
            (iy == 0).astype(jnp.int32),
            (iy == size_y - 1).astype(jnp.int32),
            jnp.int32(size_y),
        ]
    ).astype(jnp.int32)
    flat = status.reshape(3 * members * rows, cols)
    even, odd = swap_pairs(drag, "gy")
    states, lower, upper, first, last = arrange(flat, members, rows)
    drag, first, last = extend(place, drag, even, odd, first, last)
    first, last, lower, upper = lax.optimization_barrier((first, last, lower, upper))
    left, right = to_neighbours("gx", first, last)
    above, below = to_neighbours("gy", lower, upper)
    count = 3 * members
    keep, priors = share(place, order, owner, cell, states, drag, left[count:], right[count:], members, rows)
    half = cols // 2
    left, right = left[:count], right[:count]
    small_lower = jnp.concatenate([left[:, :half], right[:, :half]], axis=1)
    small_upper = jnp.concatenate([left[:, half:], right[:, half:]], axis=1)
    small_lower, small_upper, priors = lax.optimization_barrier((small_lower, small_upper, priors))
    cabove, cbelow = to_neighbours("gy", small_lower, small_upper)
    states = forecast(place, states, above, below, left, right, cabove, cbelow, keep)
    priors = add_over(priors, ("gx", "gy"))
    result = assimilate(place, order, owner, reach, value, error, taper, priors, states, members, rows)
    return result.reshape(status.shape)


def solution(mesh):
    in_specs = (P(None, None, "gy", "gx"), P("gy", "gx"), P(), P(), P(), P(), P(), P(), P())
    out_specs = P(None, None, "gy", "gx")
    return jax.shard_map(body, mesh=mesh, in_specs=in_specs, out_specs=out_specs, check_vma=False)
```

```python
import functools

import jax
import jax.numpy as jnp
from jax import lax
from jax.experimental import pallas as pl
from jax.experimental.pallas import tpu as pltpu
from jax.sharding import PartitionSpec as P

STEPS = 4
MARGIN = 2 * STEPS
EPS = 1e-06
NT = (((1,), (1,)), ((), ()))
HIGHEST = lax.Precision.HIGHEST
F32 = jnp.float32
BF16 = jnp.bfloat16
VMEM_LIMIT = 12 * 1024 * 1024

VSPEC = pl.BlockSpec(memory_space=pltpu.VMEM)
SSPEC = pl.BlockSpec(memory_space=pltpu.SMEM)


def lanes_of(shape):
    return lax.broadcasted_iota(jnp.int32, shape, len(shape) - 1)


def sublanes_of(shape):
    return lax.broadcasted_iota(jnp.int32, shape, len(shape) - 2)


def roll_lanes(x, shift):
    size = x.shape[-1]
    shift = shift % size
    return x if shift == 0 else pltpu.roll(x, shift, x.ndim - 1)


def arrange_kernel(members, rows, x_ref, out_ref, lower_ref, upper_ref, left_ref, right_ref):
    cols = x_ref.shape[1]
    lane = lanes_of((8, cols))

    def group(g, carry):
        here = pl.ds(pl.multiple_of(g * 8, 8), 8)
        for f in range(3):
            left = jnp.zeros((8, cols), F32)
            right = jnp.zeros((8, cols), F32)
            depth = MARGIN if f == 2 else MARGIN - 1
            for r in range(rows):
                row = x_ref[pl.ds((f * members + g * 8) * rows + r, 8, stride=rows), :]
                out_ref[f * rows + r, here, :] = row
                if r < depth:
                    lower_ref[f * (MARGIN - 1) + r, here, :] = row
                if r >= rows - depth:
                    upper_ref[f * (MARGIN - 1) + r - rows + depth, here, :] = row
                there = (lane >= MARGIN * r) & (lane < MARGIN * (r + 1))
                left = jnp.where(there, roll_lanes(row, MARGIN * r), left)
                right = jnp.where(there, roll_lanes(row, MARGIN * (r + 1)), right)
            at = pl.ds(pl.multiple_of(f * members + g * 8, 8), 8)
            left_ref[at, :] = left
            right_ref[at, :] = right
        return carry

    lax.fori_loop(0, members // 8, group, 0)


def arrange(x, members, rows):
    cols = x.shape[1]
    edge = jax.ShapeDtypeStruct((3 * members, cols), F32)
    band = jax.ShapeDtypeStruct((3 * MARGIN - 2, members, cols), F32)
    return pl.pallas_call(
        functools.partial(arrange_kernel, members, rows),
        out_shape=(jax.ShapeDtypeStruct((3 * rows, members, cols), F32), band, band, edge, edge),
        in_specs=[VSPEC],
        out_specs=(VSPEC,) * 5,
        compiler_params=pltpu.CompilerParams(vmem_limit_bytes=VMEM_LIMIT),
        cost_estimate=pl.CostEstimate(flops=4_000_000, bytes_accessed=6_000_000, transcendentals=0),
    )(x)


def extend_kernel(place_ref, drag_ref, even_ref, odd_ref, first_ref, last_ref, drag_out, even_out, odd_out):
    rows = drag_ref.shape[0]
    count = first_ref.shape[0]
    odd_y = place_ref[0] % place_ref[5] % 2 == 1
    odd_x = place_ref[0] // place_ref[5] % 2 == 1
    above = jnp.where(odd_y, even_ref[rows - MARGIN :, :], odd_ref[rows - MARGIN :, :])
    below = jnp.where(odd_y, odd_ref[:MARGIN, :], even_ref[:MARGIN, :])
    drag = jnp.concatenate([above, drag_ref[...], below], axis=0)
    drag_out[...] = drag
    even_out[:count, :] = jnp.where(odd_x, first_ref[...], last_ref[...])
    odd_out[:count, :] = jnp.where(odd_x, last_ref[...], first_ref[...])
    even_out[count:, :] = drag
    odd_out[count:, :] = drag


def extend(place, drag, even, odd, first, last):
    rows, cols = drag.shape
    total = rows + 2 * MARGIN
    message = jax.ShapeDtypeStruct((first.shape[0] + total, cols), F32)
    return pl.pallas_call(
        extend_kernel,
        out_shape=(jax.ShapeDtypeStruct((total, cols), F32), message, message),
        in_specs=[SSPEC] + [VSPEC] * 5,
        out_specs=(VSPEC,) * 3,
        compiler_params=pltpu.CompilerParams(vmem_limit_bytes=VMEM_LIMIT),
    )(place, drag, even, odd, first, last)


def corner_kernel(place_ref, even_ref, odd_ref, left_ref, right_ref, even_out, odd_out):
    count, cols = left_ref.shape
    half = cols // 2
    odd_y = place_ref[0] % place_ref[5] % 2 == 1
    odd_x = place_ref[0] // place_ref[5] % 2 == 1
    even, odd = even_ref[:count, :], odd_ref[:count, :]
    left, right = jnp.where(odd_x, even, odd), jnp.where(odd_x, odd, even)
    left_ref[...] = left
    right_ref[...] = right
    first_half = lanes_of((count, cols)) < half
    lower = jnp.where(first_half, left, roll_lanes(right, half))
    upper = jnp.where(first_half, roll_lanes(left, half), right)
    even_out[...] = jnp.where(odd_y, lower, upper)
    odd_out[...] = jnp.where(odd_y, upper, lower)


def corner(place, even, odd, count):
    cols = even.shape[1]
    return pl.pallas_call(
        corner_kernel,
        out_shape=(jax.ShapeDtypeStruct((count, cols), F32),) * 4,
        in_specs=[SSPEC] + [VSPEC] * 2,
        out_specs=(VSPEC,) * 4,
        compiler_params=pltpu.CompilerParams(vmem_limit_bytes=VMEM_LIMIT),
    )(place, even, odd)


def grid_factor(place_ref, shape, rows, cols):
    row, col = sublanes_of(shape), lanes_of(shape)
    wide = 2 * cols
    low, high = jnp.where(place_ref[3] == 1, MARGIN, 0), jnp.where(place_ref[4] == 1, MARGIN + rows, rows + 2 * MARGIN)
    first, last = jnp.where(place_ref[1] == 1, wide, wide - MARGIN), jnp.where(place_ref[2] == 1, cols, cols + MARGIN)
    ok = (row >= low) & (row < high) & ((col < last) | (col >= first))
    return jnp.where(ok, 1.0, 0.0)


def share_kernel(
    members, rows,
    place_ref, order_ref, owner_ref, cell_ref, state_ref, drag_ref, even_ref, odd_ref,
    keep_ref, prior_ref, turned,
):
    cols = drag_ref.shape[1]
    wide = 2 * cols
    total = rows + 2 * MARGIN
    size_y = place_ref[5]
    ix, iy = place_ref[0] // size_y, place_ref[0] % size_y
    shape = (total, wide)
    lane = lanes_of((total, cols))
    odd = ix % 2 == 1
    here = even_ref.shape[0] - total
    even_part, odd_part = even_ref[here:, :], odd_ref[here:, :]
    before = jnp.where(odd, even_part, odd_part)
    after = jnp.where(odd, odd_part, even_part)
    margins = jnp.where(lane < cols // 2, after, before)
    drag = jnp.concatenate([drag_ref[...], margins], axis=1)
    keep = 1.0 - drag
    keep_ref[...] = keep
    slope = 0.2 * grid_factor(place_ref, shape, rows, cols)
    sub, wlane = sublanes_of(shape), lanes_of(shape)
    turned[...] = jnp.zeros_like(turned)
    spot = lanes_of((members, cols))

    def one(i, carry):
        k = order_ref[i]
        tile, cell = owner_ref[k], cell_ref[k]
        field, inner = cell // (rows * cols), cell % (rows * cols)
        row = (tile % size_y - iy) * rows + inner // cols
        col = (tile // size_y - ix) * cols + inner % cols
        near = (row >= -MARGIN) & (row < rows + MARGIN) & (col >= -MARGIN) & (col < cols + MARGIN)

        @pl.when(near)
        def _():
            at = jnp.where(col < 0, col + wide, col)
            start = jnp.where((sub == row + MARGIN) & (wlane == at), 1.0, 0.0)
            h = jnp.where(field == 0, start, 0.0)
            u = jnp.where(field == 1, start, 0.0)
            v = jnp.where(field == 2, start, 0.0)
            for _step in range(STEPS):
                h = h + slope * (
                    (roll_lanes(u, -1) - roll_lanes(u, 1)) + (pltpu.roll(v, total - 1, 0) - pltpu.roll(v, 1, 0))
                )
                u, v = (
                    keep * u + slope * (roll_lanes(h, -1) - roll_lanes(h, 1)) - 0.1 * v,
                    keep * v + slope * (pltpu.roll(h, total - 1, 0) - pltpu.roll(h, 1, 0)) + 0.1 * u,
                )
            sums = jnp.zeros((members, cols), F32)
            for f, weights in enumerate((h, u, v)):
                for r in range(rows):
                    sums = sums + weights[MARGIN + r : MARGIN + r + 1, :cols] * state_ref[f * rows + r]
            column = jnp.sum(sums, axis=1, keepdims=True)
            turned[0:members, :] = jnp.where(spot == i, column, turned[0:members, :])

        return carry

    lax.fori_loop(0, order_ref.shape[0], one, 0)
    prior_ref[...] = jnp.transpose(turned[...])[: prior_ref.shape[0]]


def share(place, order, owner, cell, states, drag, even, odd, members, rows):
    cols = drag.shape[1]
    return pl.pallas_call(
        functools.partial(share_kernel, members, rows),
        out_shape=(
            jax.ShapeDtypeStruct((drag.shape[0], 2 * cols), F32),
            jax.ShapeDtypeStruct((order.shape[0], cols), F32),
        ),
        in_specs=[SSPEC] * 4 + [VSPEC] * 4,
        out_specs=(VSPEC, VSPEC),
        scratch_shapes=[pltpu.VMEM((cols, cols), F32)],
        compiler_params=pltpu.CompilerParams(vmem_limit_bytes=VMEM_LIMIT),
        cost_estimate=pl.CostEstimate(flops=6_000_000, bytes_accessed=2_000_000, transcendentals=0),
    )(place, order, owner, cell, states, drag, even, odd)


def wide_row(lane, main, left, left_at, right, right_at):
    cols = main.shape[1]
    halo = jnp.where(lane >= cols - MARGIN, roll_lanes(left, cols - MARGIN - left_at), 0.0)
    halo = jnp.where(lane < MARGIN, roll_lanes(right, -right_at), halo)
    return jnp.concatenate([main, halo], axis=1)


def forecast_kernel(
    members, rows,
    place_ref, state_ref, above_ref, below_ref, left_ref, right_ref, ceven_ref, codd_ref, keep_ref,
    out_ref,
    state, keep, slope,
):
    cols = state_ref.shape[2]
    wide = 2 * cols
    total = rows + 2 * MARGIN
    lane = lanes_of((8, cols))
    half = cols // 2
    factor = -0.2 * grid_factor(place_ref, (total, wide), rows, cols)
    odd_y = place_ref[0] % place_ref[5] % 2 == 1
    for r in range(total):
        keep[r] = jnp.broadcast_to(keep_ref[r : r + 1, :], (8, wide))
        slope[r] = jnp.broadcast_to(factor[r : r + 1, :], (8, wide))

    def group(g, carry):
        here = pl.ds(pl.multiple_of(g * 8, 8), 8)
        for f in range(3):
            at = pl.ds(pl.multiple_of(f * members + g * 8, 8), 8)
            ledge, redge = left_ref[at, :], right_ref[at, :]
            ceven, codd = ceven_ref[at, :], codd_ref[at, :]
            cab, cbe = jnp.where(odd_y, ceven, codd), jnp.where(odd_y, codd, ceven)
            depth = MARGIN if f == 2 else MARGIN - 1
            for r in range(MARGIN - depth, MARGIN + rows + depth):
                if r < MARGIN:
                    main = above_ref[f * (MARGIN - 1) + r - MARGIN + depth, here, :]
                    value = wide_row(lane, main, cab, MARGIN * r, cab, half + MARGIN * r)
                elif r < MARGIN + rows:
                    q = r - MARGIN
                    main = state_ref[f * rows + q, here, :]
                    value = wide_row(lane, main, ledge, MARGIN * q, redge, MARGIN * q)
                else:
                    q = r - MARGIN - rows
                    main = below_ref[f * (MARGIN - 1) + q, here, :]
                    value = wide_row(lane, main, cbe, MARGIN * q, cbe, half + MARGIN * q)
                state[f, r] = value
        for step in range(STEPS):
            reach = 2 * (STEPS - step) - 1
            for r in range(MARGIN - reach, MARGIN + rows + reach):
                u = state[1, r]
                div = (roll_lanes(u, -1) - roll_lanes(u, 1)) + (state[2, r + 1] - state[2, r - 1])
                state[0, r] = state[0, r] + slope[r] * div
            reach -= 1
            for r in range(MARGIN - reach, MARGIN + rows + reach):
                h = state[0, r]
                u, v = state[1, r], state[2, r]
                k, c = keep[r], slope[r]
                state[1, r] = k * u + c * (roll_lanes(h, -1) - roll_lanes(h, 1)) + 0.1 * v
                state[2, r] = k * v + c * (state[0, r + 1] - state[0, r - 1]) - 0.1 * u
        for f in range(3):
            for r in range(rows):
                out_ref[f * rows + r, here, :] = state[f, MARGIN + r, :, 0:cols]
        return carry

    lax.fori_loop(0, members // 8, group, 0)


def forecast(place, states, above, below, left, right, cabove, cbelow, keep):
    members, cols = states.shape[1:]
    rows = states.shape[0] // 3
    total = rows + 2 * MARGIN
    return pl.pallas_call(
        functools.partial(forecast_kernel, members, rows),
        out_shape=jax.ShapeDtypeStruct(states.shape, F32),
        in_specs=[SSPEC] + [VSPEC] * 8,
        out_specs=VSPEC,
        scratch_shapes=[
            pltpu.VMEM((3, total, 8, 2 * cols), F32),
            pltpu.VMEM((total, 8, 2 * cols), F32),
            pltpu.VMEM((total, 8, 2 * cols), F32),
        ],
        compiler_params=pltpu.CompilerParams(vmem_limit_bytes=VMEM_LIMIT),
        cost_estimate=pl.CostEstimate(flops=60_000_000, bytes_accessed=30_000_000, transcendentals=0),
    )(place, states, above, below, left, right, cabove, cbelow, keep)


def localize(distance, reach, taper_ref):
    picked = jnp.zeros(distance.shape, F32)
    levels = taper_ref.shape[0]
    capped = jnp.minimum(distance, levels - 1)
    for d in range(levels):
        picked = jnp.where(capped == d, taper_ref[d], picked)
    return jnp.where(distance <= reach, picked, 0.0)


def assimilate_kernel(
    members, rows,
    place_ref, order_ref, owner_ref, reach_ref, value_ref, error_ref, taper_ref,
    prior_ref, forecast_ref,
    out_ref,
):
    n_obs = order_ref.shape[0]
    cols = prior_ref.shape[1]
    size_y = place_ref[5]
    lane1 = lanes_of((1, cols))
    lane = lanes_of((n_obs, cols))
    sub = sublanes_of((n_obs, cols))

    tile_row = jnp.zeros((1, cols), jnp.int32)
    tile_col = jnp.zeros((n_obs, cols), jnp.int32)
    reach_row = jnp.zeros((1, cols), jnp.int32)
    reach_col = jnp.zeros((n_obs, cols), jnp.int32)
    which = [order_ref[i] for i in range(n_obs)]
    for i, k in enumerate(which):
        tile_row = jnp.where(lane1 == i, owner_ref[k], tile_row)
        tile_col = jnp.where(sub == i, owner_ref[k], tile_col)
        reach_row = jnp.where(lane1 == i, reach_ref[k], reach_row)
        reach_col = jnp.where(sub == i, reach_ref[k], reach_col)
    rx, ry = tile_row // size_y, tile_row % size_y
    cx, cy = tile_col // size_y, tile_col % size_y
    distance = jnp.maximum(jnp.abs(cx - rx), jnp.abs(cy - ry))
    onto = localize(distance, reach_row, taper_ref)
    onto_t = localize(distance, reach_col, taper_ref)
    mine = place_ref[0]
    own = localize(
        jnp.maximum(jnp.abs(mine // size_y - rx), jnp.abs(mine % size_y - ry)), reach_row, taper_ref
    )

    priors = prior_ref[...]
    inside = lane < members
    mean_col = jnp.sum(jnp.where(inside, priors, 0.0), axis=1, keepdims=True) / members
    anomalies = jnp.where(inside, priors - mean_col, 0.0)
    padded = jnp.concatenate([anomalies, jnp.zeros((cols - n_obs, cols), F32)], axis=0)
    unit = jnp.where(lanes_of((members, cols)) == sublanes_of((members, cols)), 1.0, 0.0)
    table = lax.dot_general(
        jnp.concatenate([anomalies, unit], axis=0), padded, NT, precision=HIGHEST, preferred_element_type=F32
    )
    mean = jnp.zeros((1, cols), F32)
    for i in range(n_obs):
        mean = jnp.where(lane1 == i, mean_col[i : i + 1, :], mean)

    scales = jnp.zeros((1, cols), F32)
    increments = []
    for i, k in enumerate(which):
        error = error_ref[k]
        row = table[i : i + 1, :]
        column = table[:, i : i + 1]
        power = row[:, i : i + 1]
        variance = power / (members - 1) + EPS
        inverse = 1.0 / (variance + error)
        scaled = 1.0 / ((members - 1) * variance)
        shift = variance * (value_ref[k] - mean[:, i : i + 1]) * inverse
        shrink = jnp.sqrt(error * inverse) - 1.0
        weight = scaled * own[:, i : i + 1]
        alpha_row = onto_t[i : i + 1, :] * row * scaled
        later = lane1 > i
        h = jnp.where(later, shrink * alpha_row, 0.0)
        q = jnp.where(later, shrink * (row + h * power), 0.0)
        alpha = jnp.concatenate(
            [onto[:, i : i + 1] * column[:n_obs] * scaled, column[n_obs:] * weight], axis=0
        )
        table = table + column * h + alpha * q
        mean = mean + alpha_row * shift
        now = anomalies[i : i + 1, :]
        increments.append(shift + shrink * now)
        anomalies = anomalies + jnp.where(sub > i, shrink * alpha[:n_obs], 0.0) * now
        scales = jnp.where(lane1 == i, weight, scales)
    left = table[n_obs:, :] * scales
    right = jnp.where(inside, jnp.concatenate(increments, axis=0), 0.0)
    right = jnp.concatenate([right, jnp.zeros((cols - n_obs, cols), F32)], axis=0)
    change = jnp.dot(left, right, precision=HIGHEST, preferred_element_type=F32)
    change = jnp.concatenate([change, jnp.zeros((cols - members, cols), F32)], axis=0)
    change = jnp.transpose(change)[:members, :]
    high = change.astype(BF16).astype(F32)
    low = change - high
    zero = jnp.zeros((members, cols), F32)
    high = jnp.concatenate([high, zero], axis=1)
    low = jnp.concatenate([low, zero], axis=1)
    factor = (high + roll_lanes(high, members) + roll_lanes(low, 2 * members)).astype(BF16)

    block = 4
    for at in range(0, 3 * rows, block):
        x = jnp.concatenate([forecast_ref[at + b] for b in range(block)], axis=1)
        xh = x.astype(BF16)
        xl = (x - xh.astype(F32)).astype(BF16)
        stack = jnp.concatenate([xh, xl, xh, jnp.zeros((2 * cols - 3 * members, block * cols), BF16)], axis=0)
        y = x + jnp.dot(factor, stack, preferred_element_type=F32)
        for b in range(block):
            f, r = divmod(at + b, rows)
            out_ref[pl.ds(f * members * rows + r, members, stride=rows), :] = y[:, b * cols : (b + 1) * cols]


def assimilate(place, order, owner, reach, value, error, taper, priors, states, members, rows):
    cols = priors.shape[1]
    return pl.pallas_call(
        functools.partial(assimilate_kernel, members, rows),
        out_shape=jax.ShapeDtypeStruct((3 * members * rows, cols), F32),
        in_specs=[SSPEC] * 7 + [VSPEC] * 2,
        out_specs=VSPEC,
        compiler_params=pltpu.CompilerParams(vmem_limit_bytes=VMEM_LIMIT),
    )(place, order, owner, reach, value, error, taper, priors, states)


def to_neighbours(axis, lower, upper):
    count = lax.axis_size(axis)
    forward = [(i, i + 1) for i in range(count - 1)]
    backward = [(target, source) for source, target in forward]
    return lax.ppermute(upper, axis, forward), lax.ppermute(lower, axis, backward)


def swap_pairs(x, axis, start):
    pairs = [(i, i + 1) for i in range(start, lax.axis_size(axis) - 1, 2)]
    return lax.ppermute(x, axis, pairs + [(b, a) for a, b in pairs])


def add_over(x, axes):
    for axis in axes:
        count = lax.axis_size(axis)
        if count & (count - 1):
            x = lax.psum(x, axis)
            continue
        span = 1
        while span < count:
            x = x + lax.ppermute(x, axis, [(i, i ^ span) for i in range(count)])
            span *= 2
    return x


def body(status, drag, value, error, taper, order, owner, cell, reach):
    members, rows, cols = status.shape[1:]
    ix, iy = lax.axis_index("gx"), lax.axis_index("gy")
    size_x, size_y = lax.axis_size("gx"), lax.axis_size("gy")
    place = jnp.stack(
        [
            ix * size_y + iy,
            (ix == 0).astype(jnp.int32),
            (ix == size_x - 1).astype(jnp.int32),
            (iy == 0).astype(jnp.int32),
            (iy == size_y - 1).astype(jnp.int32),
            jnp.int32(size_y),
        ]
    ).astype(jnp.int32)
    flat = status.reshape(3 * members * rows, cols)
    states, lower, upper, first, last = arrange(flat, members, rows)
    drag, lower = lax.optimization_barrier((drag, lower))
    even, odd = swap_pairs(drag, "gy", 0), swap_pairs(drag, "gy", 1)
    even, odd, lower, upper = lax.optimization_barrier((even, odd, lower, upper))
    above, below = to_neighbours("gy", lower, upper)
    drag, even, odd = extend(place, drag, even, odd, first, last)
    even = swap_pairs(even, "gx", 0)
    odd = swap_pairs(odd, "gx", 1)
    keep, priors = share(place, order, owner, cell, states, drag, even, odd, members, rows)
    left, right, even, odd = corner(place, even, odd, 3 * members)
    even, odd, priors = lax.optimization_barrier((even, odd, priors))
    cabove = swap_pairs(even, "gy", 0)
    cbelow = swap_pairs(odd, "gy", 1)
    states = forecast(place, states, above, below, left, right, cabove, cbelow, keep)
    priors = add_over(priors, ("gx", "gy"))
    result = assimilate(place, order, owner, reach, value, error, taper, priors, states, members, rows)
    return result.reshape(status.shape)


def solution(mesh):
    in_specs = (P(None, None, "gy", "gx"), P("gy", "gx"), P(), P(), P(), P(), P(), P(), P())
    out_specs = P(None, None, "gy", "gx")
    return jax.shard_map(body, mesh=mesh, in_specs=in_specs, out_specs=out_specs, check_vma=False)
```

```python
import functools

import jax
import jax.numpy as jnp
from jax import lax
from jax.experimental import pallas as pl
from jax.experimental.pallas import tpu as pltpu
from jax.sharding import PartitionSpec as P

STEPS = 4
MARGIN = 2 * STEPS
EPS = 1e-06
NT = (((1,), (1,)), ((), ()))
HIGHEST = lax.Precision.HIGHEST
F32 = jnp.float32
BF16 = jnp.bfloat16
VMEM_LIMIT = 16 * 1024 * 1024
GROUP = 40

VSPEC = pl.BlockSpec(memory_space=pltpu.VMEM)
SSPEC = pl.BlockSpec(memory_space=pltpu.SMEM)


def lanes_of(shape):
    return lax.broadcasted_iota(jnp.int32, shape, len(shape) - 1)


def sublanes_of(shape):
    return lax.broadcasted_iota(jnp.int32, shape, len(shape) - 2)


def roll_lanes(x, shift):
    size = x.shape[-1]
    shift = shift % size
    return x if shift == 0 else pltpu.roll(x, shift, x.ndim - 1)


def arrange_kernel(members, rows, place_ref, x_ref, drag_ref, out_ref, lower_ref, upper_ref, even_ref, odd_ref):
    cols = x_ref.shape[1]
    lane = lanes_of((8, cols))
    odd_x = place_ref[0] // place_ref[5] % 2 == 1

    def group(g, carry):
        here = pl.ds(pl.multiple_of(g * 8, 8), 8)
        for f in range(3):
            left = jnp.zeros((8, cols), F32)
            right = jnp.zeros((8, cols), F32)
            depth = MARGIN if f == 2 else MARGIN - 1
            for r in range(rows):
                row = x_ref[pl.ds((f * members + g * 8) * rows + r, 8, stride=rows), :]
                out_ref[f * rows + r, here, :] = row
                if r < depth:
                    lower_ref[f * (MARGIN - 1) + r, here, :] = row
                if r >= rows - depth:
                    upper_ref[f * (MARGIN - 1) + r - rows + depth, here, :] = row
                there = (lane >= MARGIN * r) & (lane < MARGIN * (r + 1))
                left = jnp.where(there, roll_lanes(row, MARGIN * r), left)
                right = jnp.where(there, roll_lanes(row, MARGIN * (r + 1)), right)
            at = pl.ds(pl.multiple_of(f * members + g * 8, 8), 8)
            even_ref[at, :] = jnp.where(odd_x, left, right)
            odd_ref[at, :] = jnp.where(odd_x, right, left)
        return carry

    lax.fori_loop(0, members // 8, group, 0)
    even_ref[3 * members :, :] = drag_ref[...]
    odd_ref[3 * members :, :] = drag_ref[...]


def arrange(place, x, drag, members):
    rows, cols = drag.shape
    message = jax.ShapeDtypeStruct((3 * members + rows, cols), F32)
    band = jax.ShapeDtypeStruct((3 * MARGIN - 2, members, cols), F32)
    return pl.pallas_call(
        functools.partial(arrange_kernel, members, rows),
        out_shape=(jax.ShapeDtypeStruct((3 * rows, members, cols), F32), band, band, message, message),
        in_specs=[SSPEC, VSPEC, VSPEC],
        out_specs=(VSPEC,) * 5,
        compiler_params=pltpu.CompilerParams(vmem_limit_bytes=VMEM_LIMIT),
        cost_estimate=pl.CostEstimate(flops=4_000_000, bytes_accessed=6_000_000, transcendentals=0),
    )(place, x, drag)


def corner_kernel(place_ref, drag_ref, even_ref, odd_ref, left_ref, right_ref, margin_ref, even_out, odd_out):
    count, cols = left_ref.shape
    rows = drag_ref.shape[0]
    half = cols // 2
    odd_y = place_ref[0] % place_ref[5] % 2 == 1
    odd_x = place_ref[0] // place_ref[5] % 2 == 1
    even, odd = even_ref[...], odd_ref[...]
    left, right = jnp.where(odd_x, even, odd), jnp.where(odd_x, odd, even)
    margin = jnp.where(lanes_of((rows, cols)) < half, right[count:], left[count:])
    margin_ref[...] = margin
    left, right = left[:count], right[:count]
    left_ref[...] = left
    right_ref[...] = right
    first_half = lanes_of((count, cols)) < half
    lower = jnp.where(first_half, left, roll_lanes(right, half))
    upper = jnp.where(first_half, roll_lanes(left, half), right)
    even_out[:count, :] = jnp.where(odd_y, lower, upper)
    odd_out[:count, :] = jnp.where(odd_y, upper, lower)
    drag = drag_ref[...]
    for at, part in ((count, drag), (count + MARGIN, margin)):
        lower, upper = part[:MARGIN], part[rows - MARGIN :]
        even_out[at : at + MARGIN, :] = jnp.where(odd_y, lower, upper)
        odd_out[at : at + MARGIN, :] = jnp.where(odd_y, upper, lower)


def corner(place, drag, even, odd):
    rows, cols = drag.shape
    count = even.shape[0] - rows
    edge = jax.ShapeDtypeStruct((count, cols), F32)
    message = jax.ShapeDtypeStruct((count + 2 * MARGIN, cols), F32)
    return pl.pallas_call(
        corner_kernel,
        out_shape=(edge, edge, jax.ShapeDtypeStruct((rows, cols), F32), message, message),
        in_specs=[SSPEC] + [VSPEC] * 3,
        out_specs=(VSPEC,) * 5,
        compiler_params=pltpu.CompilerParams(vmem_limit_bytes=VMEM_LIMIT),
    )(place, drag, even, odd)


def grid_factor(place_ref, shape, rows, cols):
    row, col = sublanes_of(shape), lanes_of(shape)
    wide = 2 * cols
    low, high = jnp.where(place_ref[3] == 1, MARGIN, 0), jnp.where(place_ref[4] == 1, MARGIN + rows, rows + 2 * MARGIN)
    first, last = jnp.where(place_ref[1] == 1, wide, wide - MARGIN), jnp.where(place_ref[2] == 1, cols, cols + MARGIN)
    ok = (row >= low) & (row < high) & ((col < last) | (col >= first))
    return jnp.where(ok, 1.0, 0.0)


def wide_row(lane, main, left, left_at, right, right_at):
    cols = main.shape[1]
    halo = jnp.where(lane >= cols - MARGIN, roll_lanes(left, cols - MARGIN - left_at), 0.0)
    halo = jnp.where(lane < MARGIN, roll_lanes(right, -right_at), halo)
    return jnp.concatenate([main, halo], axis=1)


def forecast_kernel(
    members, rows,
    place_ref, order_ref, owner_ref, cell_ref,
    state_ref, above_ref, below_ref, left_ref, right_ref, ceven_ref, codd_ref, drag_ref, margin_ref,
    out_ref, prior_ref,
    state, keep, slope, across,
):
    cols = state_ref.shape[2]
    wide = 2 * cols
    total = rows + 2 * MARGIN
    lane = lanes_of((GROUP, cols))
    half = cols // 2
    factor = -0.2 * grid_factor(place_ref, (total, wide), rows, cols)
    odd_y = place_ref[0] % place_ref[5] % 2 == 1
    source, target = sublanes_of((wide, wide)), lanes_of((wide, wide))
    shift = jnp.where(source == (target + 1) % wide, 1.0, jnp.where(target == (source + 1) % wide, -1.0, 0.0)).astype(BF16)
    count = 3 * members
    parts = []
    for here, own in ((count, drag_ref), (count + MARGIN, margin_ref)):
        even, odd = ceven_ref[here : here + MARGIN, :], codd_ref[here : here + MARGIN, :]
        above, below = jnp.where(odd_y, even, odd), jnp.where(odd_y, odd, even)
        parts.append(jnp.concatenate([above, own[...], below], axis=0))
    kept = 1.0 - jnp.concatenate(parts, axis=1)
    for r in range(total):
        keep[r] = jnp.broadcast_to(kept[r : r + 1, :], (GROUP, wide))
        slope[r] = jnp.broadcast_to(factor[r : r + 1, :], (GROUP, wide))

    def group(g, carry):
        here = pl.ds(pl.multiple_of(g * GROUP, GROUP), GROUP)
        for f in range(3):
            at = pl.ds(pl.multiple_of(f * members + g * GROUP, GROUP), GROUP)
            ledge, redge = left_ref[at, :], right_ref[at, :]
            ceven, codd = ceven_ref[at, :], codd_ref[at, :]
            cab, cbe = jnp.where(odd_y, ceven, codd), jnp.where(odd_y, codd, ceven)
            depth = MARGIN if f == 2 else MARGIN - 1
            for r in range(MARGIN - depth, MARGIN + rows + depth):
                if r < MARGIN:
                    main = above_ref[f * (MARGIN - 1) + r - MARGIN + depth, here, :]
                    value = wide_row(lane, main, cab, MARGIN * r, cab, half + MARGIN * r)
                elif r < MARGIN + rows:
                    q = r - MARGIN
                    main = state_ref[f * rows + q, here, :]
                    value = wide_row(lane, main, ledge, MARGIN * q, redge, MARGIN * q)
                else:
                    q = r - MARGIN - rows
                    main = below_ref[f * (MARGIN - 1) + q, here, :]
                    value = wide_row(lane, main, cbe, MARGIN * q, cbe, half + MARGIN * q)
                state[f, r] = value
        def column_slope(f, low, high):
            x = state[f, low:high].reshape((high - low) * GROUP, wide)
            top = x.astype(BF16)
            rest = (x - top.astype(F32)).astype(BF16)
            n = (high - low) * GROUP
            cut = n // 2 // 16 * 16
            parts = []
            for p, q in ((0, cut), (cut, n)):
                parts.append(jnp.dot(top[p:q], shift, preferred_element_type=F32))
                parts.append(jnp.dot(rest[p:q], shift, preferred_element_type=F32))
            d = jnp.concatenate([parts[0] + parts[1], parts[2] + parts[3]], axis=0)
            across[low:high] = d.reshape(high - low, GROUP, wide)

        for step in range(STEPS):
            reach = 2 * (STEPS - step) - 1
            low, high = MARGIN - reach, MARGIN + rows + reach
            column_slope(1, low, high)
            for r in range(low, high):
                div = across[r] + (state[2, r + 1] - state[2, r - 1])
                state[0, r] = state[0, r] + slope[r] * div
            low, high = low + 1, high - 1
            column_slope(0, low, high)
            for r in range(low, high):
                u, v = state[1, r], state[2, r]
                k, c = keep[r], slope[r]
                state[1, r] = k * u + c * across[r] + 0.1 * v
                state[2, r] = k * v + c * (state[0, r + 1] - state[0, r - 1]) - 0.1 * u
        for f in range(3):
            for r in range(rows):
                out_ref[f * rows + r, here, :] = state[f, MARGIN + r, :, 0:cols]
        return carry

    lax.fori_loop(0, members // GROUP, group, 0)

    prior_ref[...] = jnp.zeros_like(prior_ref)
    eight = lanes_of((8, cols))
    for i in range(order_ref.shape[0]):
        which = order_ref[i]

        @pl.when(owner_ref[which] == place_ref[0])
        def _():
            cell = cell_ref[which]
            one = jnp.where(eight == cell % cols, 1.0, 0.0)
            prior_ref[i : i + 1, 0:members] = lax.dot_general(
                one, out_ref[cell // cols], NT, precision=HIGHEST, preferred_element_type=F32
            )[0:1]


def forecast(place, order, owner, cell, states, *arrays):
    members, cols = states.shape[1:]
    rows = states.shape[0] // 3
    total = rows + 2 * MARGIN
    return pl.pallas_call(
        functools.partial(forecast_kernel, members, rows),
        out_shape=(jax.ShapeDtypeStruct(states.shape, F32), jax.ShapeDtypeStruct((order.shape[0], cols), F32)),
        in_specs=[SSPEC] * 4 + [VSPEC] * (1 + len(arrays)),
        out_specs=(VSPEC, VSPEC),
        scratch_shapes=[pltpu.VMEM((3, total, GROUP, 2 * cols), F32)] + [pltpu.VMEM((total, GROUP, 2 * cols), F32)] * 3,
        compiler_params=pltpu.CompilerParams(vmem_limit_bytes=VMEM_LIMIT),
        cost_estimate=pl.CostEstimate(flops=60_000_000, bytes_accessed=30_000_000, transcendentals=0),
    )(place, order, owner, cell, states, *arrays)


def localize(distance, reach, taper_ref):
    picked = jnp.zeros(distance.shape, F32)
    levels = taper_ref.shape[0]
    capped = jnp.minimum(distance, levels - 1)
    for d in range(levels):
        picked = jnp.where(capped == d, taper_ref[d], picked)
    return jnp.where(distance <= reach, picked, 0.0)


def assimilate_kernel(
    members, rows,
    place_ref, order_ref, owner_ref, reach_ref, value_ref, error_ref, taper_ref,
    prior_ref, forecast_ref,
    out_ref,
):
    n_obs = order_ref.shape[0]
    cols = prior_ref.shape[1]
    size_y = place_ref[5]
    lane1 = lanes_of((1, cols))
    lane = lanes_of((n_obs, cols))
    sub = sublanes_of((n_obs, cols))

    tile_row = jnp.zeros((1, cols), jnp.int32)
    tile_col = jnp.zeros((n_obs, cols), jnp.int32)
    reach_row = jnp.zeros((1, cols), jnp.int32)
    reach_col = jnp.zeros((n_obs, cols), jnp.int32)
    which = [order_ref[i] for i in range(n_obs)]
    for i, k in enumerate(which):
        tile_row = jnp.where(lane1 == i, owner_ref[k], tile_row)
        tile_col = jnp.where(sub == i, owner_ref[k], tile_col)
        reach_row = jnp.where(lane1 == i, reach_ref[k], reach_row)
        reach_col = jnp.where(sub == i, reach_ref[k], reach_col)
    rx, ry = tile_row // size_y, tile_row % size_y
    cx, cy = tile_col // size_y, tile_col % size_y
    distance = jnp.maximum(jnp.abs(cx - rx), jnp.abs(cy - ry))
    onto = localize(distance, reach_row, taper_ref)
    onto_t = localize(distance, reach_col, taper_ref)
    mine = place_ref[0]
    own = localize(
        jnp.maximum(jnp.abs(mine // size_y - rx), jnp.abs(mine % size_y - ry)), reach_row, taper_ref
    )

    priors = prior_ref[...]
    inside = lane < members
    mean_col = jnp.sum(jnp.where(inside, priors, 0.0), axis=1, keepdims=True) / members
    anomalies = jnp.where(inside, priors - mean_col, 0.0)
    padded = jnp.concatenate([anomalies, jnp.zeros((cols - n_obs, cols), F32)], axis=0)
    unit = jnp.where(lanes_of((members, cols)) == sublanes_of((members, cols)), 1.0, 0.0)
    table = lax.dot_general(
        jnp.concatenate([anomalies, unit], axis=0), padded, NT, precision=HIGHEST, preferred_element_type=F32
    )
    mean = jnp.zeros((1, cols), F32)
    for i in range(n_obs):
        mean = jnp.where(lane1 == i, mean_col[i : i + 1, :], mean)

    scales = jnp.zeros((1, cols), F32)
    increments = []
    for i, k in enumerate(which):
        error = error_ref[k]
        row = table[i : i + 1, :]
        column = table[:, i : i + 1]
        power = row[:, i : i + 1]
        variance = power / (members - 1) + EPS
        inverse = 1.0 / (variance + error)
        scaled = 1.0 / ((members - 1) * variance)
        shift = variance * (value_ref[k] - mean[:, i : i + 1]) * inverse
        shrink = jnp.sqrt(error * inverse) - 1.0
        weight = scaled * own[:, i : i + 1]
        alpha_row = onto_t[i : i + 1, :] * row * scaled
        later = lane1 > i
        h = jnp.where(later, shrink * alpha_row, 0.0)
        q = jnp.where(later, shrink * (row + h * power), 0.0)
        alpha = jnp.concatenate(
            [onto[:, i : i + 1] * column[:n_obs] * scaled, column[n_obs:] * weight], axis=0
        )
        table = table + column * h + alpha * q
        mean = mean + alpha_row * shift
        now = anomalies[i : i + 1, :]
        increments.append(shift + shrink * now)
        anomalies = anomalies + jnp.where(sub > i, shrink * alpha[:n_obs], 0.0) * now
        scales = jnp.where(lane1 == i, weight, scales)
    left = table[n_obs:, :] * scales
    right = jnp.where(inside, jnp.concatenate(increments, axis=0), 0.0)
    right = jnp.concatenate([right, jnp.zeros((cols - n_obs, cols), F32)], axis=0)
    change = jnp.dot(left, right, precision=HIGHEST, preferred_element_type=F32)
    change = jnp.concatenate([change, jnp.zeros((cols - members, cols), F32)], axis=0)
    change = jnp.transpose(change)[:members, :]
    high = change.astype(BF16).astype(F32)
    low = change - high
    zero = jnp.zeros((members, cols), F32)
    high = jnp.concatenate([high, zero], axis=1)
    low = jnp.concatenate([low, zero], axis=1)
    factor = (high + roll_lanes(high, members) + roll_lanes(low, 2 * members)).astype(BF16)

    block = 4
    for at in range(0, 3 * rows, block):
        x = jnp.concatenate([forecast_ref[at + b] for b in range(block)], axis=1)
        xh = x.astype(BF16)
        xl = (x - xh.astype(F32)).astype(BF16)
        stack = jnp.concatenate([xh, xl, xh, jnp.zeros((2 * cols - 3 * members, block * cols), BF16)], axis=0)
        y = x + jnp.dot(factor, stack, preferred_element_type=F32)
        for b in range(block):
            f, r = divmod(at + b, rows)
            out_ref[pl.ds(f * members * rows + r, members, stride=rows), :] = y[:, b * cols : (b + 1) * cols]


def assimilate(place, order, owner, reach, value, error, taper, priors, states, members, rows):
    cols = priors.shape[1]
    return pl.pallas_call(
        functools.partial(assimilate_kernel, members, rows),
        out_shape=jax.ShapeDtypeStruct((3 * members * rows, cols), F32),
        in_specs=[SSPEC] * 7 + [VSPEC] * 2,
        out_specs=VSPEC,
        compiler_params=pltpu.CompilerParams(vmem_limit_bytes=VMEM_LIMIT),
    )(place, order, owner, reach, value, error, taper, priors, states)


def to_neighbours(axis, lower, upper):
    count = lax.axis_size(axis)
    forward = [(i, i + 1) for i in range(count - 1)]
    backward = [(target, source) for source, target in forward]
    return lax.ppermute(upper, axis, forward), lax.ppermute(lower, axis, backward)


def swap_pairs(x, axis, start):
    pairs = [(i, i + 1) for i in range(start, lax.axis_size(axis) - 1, 2)]
    return lax.ppermute(x, axis, pairs + [(b, a) for a, b in pairs])


def add_over(x, axes):
    for axis in axes:
        count = lax.axis_size(axis)
        if count & (count - 1):
            x = lax.psum(x, axis)
            continue
        span = 1
        while span < count:
            x = x + lax.ppermute(x, axis, [(i, i ^ span) for i in range(count)])
            span *= 2
    return x


def body(status, drag, value, error, taper, order, owner, cell, reach):
    members, rows, cols = status.shape[1:]
    ix, iy = lax.axis_index("gx"), lax.axis_index("gy")
    size_x, size_y = lax.axis_size("gx"), lax.axis_size("gy")
    place = jnp.stack(
        [
            ix * size_y + iy,
            (ix == 0).astype(jnp.int32),
            (ix == size_x - 1).astype(jnp.int32),
            (iy == 0).astype(jnp.int32),
            (iy == size_y - 1).astype(jnp.int32),
            jnp.int32(size_y),
        ]
    ).astype(jnp.int32)
    flat = status.reshape(3 * members * rows, cols)
    states, lower, upper, even, odd = arrange(place, flat, drag, members)
    above, below = to_neighbours("gy", lower, upper)
    even, odd = swap_pairs(even, "gx", 0), swap_pairs(odd, "gx", 1)
    left, right, margin, even, odd = corner(place, drag, even, odd)
    even, odd = swap_pairs(even, "gy", 0), swap_pairs(odd, "gy", 1)
    states, priors = forecast(
        place, order, owner, cell, states, above, below, left, right, even, odd, drag, margin
    )
    priors = add_over(priors, ("gx", "gy"))
    result = assimilate(place, order, owner, reach, value, error, taper, priors, states, members, rows)
    return result.reshape(status.shape)


def solution(mesh):
    in_specs = (P(None, None, "gy", "gx"), P("gy", "gx"), P(), P(), P(), P(), P(), P(), P())
    out_specs = P(None, None, "gy", "gx")
    return jax.shard_map(body, mesh=mesh, in_specs=in_specs, out_specs=out_specs, check_vma=False)
```

```python
import functools

import jax
import jax.numpy as jnp
from jax import lax
from jax.experimental import pallas as pl
from jax.experimental.pallas import tpu as pltpu
from jax.sharding import PartitionSpec as P

STEPS = 4
MARGIN = 2 * STEPS
EPS = 1e-06
NT = (((1,), (1,)), ((), ()))
HIGHEST = lax.Precision.HIGHEST
F32 = jnp.float32
BF16 = jnp.bfloat16
VMEM_LIMIT = 16 * 1024 * 1024
GROUP = 40

VSPEC = pl.BlockSpec(memory_space=pltpu.VMEM)
SSPEC = pl.BlockSpec(memory_space=pltpu.SMEM)


def lanes_of(shape):
    return lax.broadcasted_iota(jnp.int32, shape, len(shape) - 1)


def sublanes_of(shape):
    return lax.broadcasted_iota(jnp.int32, shape, len(shape) - 2)


def roll_lanes(x, shift):
    size = x.shape[-1]
    shift = shift % size
    return x if shift == 0 else pltpu.roll(x, shift, x.ndim - 1)


def band_kernel(members, rows, x_ref, lower_ref, upper_ref):
    def group(g, carry):
        here = pl.ds(pl.multiple_of(g * 8, 8), 8)
        for f in range(3):
            depth = MARGIN if f == 2 else MARGIN - 1
            for d in range(depth):
                at = (f * members + g * 8) * rows
                lower_ref[f * (MARGIN - 1) + d, here, :] = x_ref[pl.ds(at + d, 8, stride=rows), :]
                upper_ref[f * (MARGIN - 1) + d, here, :] = x_ref[pl.ds(at + rows - depth + d, 8, stride=rows), :]
        return carry

    lax.fori_loop(0, members // 8, group, 0)


def bands(x, members, rows):
    band = jax.ShapeDtypeStruct((3 * MARGIN - 2, members, x.shape[1]), F32)
    return pl.pallas_call(
        functools.partial(band_kernel, members, rows),
        out_shape=(band, band),
        in_specs=[VSPEC],
        out_specs=(VSPEC,) * 2,
        compiler_params=pltpu.CompilerParams(vmem_limit_bytes=VMEM_LIMIT),
        cost_estimate=pl.CostEstimate(flops=1_000_000, bytes_accessed=4_000_000, transcendentals=0),
    )(x)


def pack_kernel(members, rows, place_ref, x_ref, drag_ref, even_ref, odd_ref):
    cols = x_ref.shape[1]
    lane = lanes_of((8, cols))
    odd_x = place_ref[0] // place_ref[5] % 2 == 1

    def group(g, carry):
        for f in range(3):
            left = jnp.zeros((8, cols), F32)
            right = jnp.zeros((8, cols), F32)
            for r in range(rows):
                row = x_ref[pl.ds((f * members + g * 8) * rows + r, 8, stride=rows), :]
                there = (lane >= MARGIN * r) & (lane < MARGIN * (r + 1))
                left = jnp.where(there, roll_lanes(row, MARGIN * r), left)
                right = jnp.where(there, roll_lanes(row, MARGIN * (r + 1)), right)
            at = pl.ds(pl.multiple_of(f * members + g * 8, 8), 8)
            even_ref[at, :] = jnp.where(odd_x, left, right)
            odd_ref[at, :] = jnp.where(odd_x, right, left)
        return carry

    lax.fori_loop(0, members // 8, group, 0)
    even_ref[3 * members :, :] = drag_ref[...]
    odd_ref[3 * members :, :] = drag_ref[...]


def pack(place, x, drag, members):
    rows, cols = drag.shape
    message = jax.ShapeDtypeStruct((3 * members + rows, cols), F32)
    return pl.pallas_call(
        functools.partial(pack_kernel, members, rows),
        out_shape=(message, message),
        in_specs=[SSPEC, VSPEC, VSPEC],
        out_specs=(VSPEC,) * 2,
        compiler_params=pltpu.CompilerParams(vmem_limit_bytes=VMEM_LIMIT),
        cost_estimate=pl.CostEstimate(flops=1_000_000, bytes_accessed=4_000_000, transcendentals=0),
    )(place, x, drag)


def corner_kernel(place_ref, drag_ref, even_ref, odd_ref, left_ref, right_ref, margin_ref, even_out, odd_out):
    count, cols = left_ref.shape
    rows = drag_ref.shape[0]
    half = cols // 2
    odd_y = place_ref[0] % place_ref[5] % 2 == 1
    odd_x = place_ref[0] // place_ref[5] % 2 == 1
    even, odd = even_ref[...], odd_ref[...]
    left, right = jnp.where(odd_x, even, odd), jnp.where(odd_x, odd, even)
    margin = jnp.where(lanes_of((rows, cols)) < half, right[count:], left[count:])
    margin_ref[...] = margin
    left, right = left[:count], right[:count]
    left_ref[...] = left
    right_ref[...] = right
    first_half = lanes_of((count, cols)) < half
    lower = jnp.where(first_half, left, roll_lanes(right, half))
    upper = jnp.where(first_half, roll_lanes(left, half), right)
    even_out[:count, :] = jnp.where(odd_y, lower, upper)
    odd_out[:count, :] = jnp.where(odd_y, upper, lower)
    drag = drag_ref[...]
    for at, part in ((count, drag), (count + MARGIN, margin)):
        lower, upper = part[:MARGIN], part[rows - MARGIN :]
        even_out[at : at + MARGIN, :] = jnp.where(odd_y, lower, upper)
        odd_out[at : at + MARGIN, :] = jnp.where(odd_y, upper, lower)


def corner(place, drag, even, odd):
    rows, cols = drag.shape
    count = even.shape[0] - rows
    edge = jax.ShapeDtypeStruct((count, cols), F32)
    message = jax.ShapeDtypeStruct((count + 2 * MARGIN, cols), F32)
    return pl.pallas_call(
        corner_kernel,
        out_shape=(edge, edge, jax.ShapeDtypeStruct((rows, cols), F32), message, message),
        in_specs=[SSPEC] + [VSPEC] * 3,
        out_specs=(VSPEC,) * 5,
        compiler_params=pltpu.CompilerParams(vmem_limit_bytes=VMEM_LIMIT),
    )(place, drag, even, odd)


def grid_factor(place_ref, shape, rows, cols):
    row, col = sublanes_of(shape), lanes_of(shape)
    wide = 2 * cols
    low, high = jnp.where(place_ref[3] == 1, MARGIN, 0), jnp.where(place_ref[4] == 1, MARGIN + rows, rows + 2 * MARGIN)
    first, last = jnp.where(place_ref[1] == 1, wide, wide - MARGIN), jnp.where(place_ref[2] == 1, cols, cols + MARGIN)
    ok = (row >= low) & (row < high) & ((col < last) | (col >= first))
    return jnp.where(ok, 1.0, 0.0)


def wide_row(lane, main, left, left_at, right, right_at):
    cols = main.shape[1]
    halo = jnp.where(lane >= cols - MARGIN, roll_lanes(left, cols - MARGIN - left_at), 0.0)
    halo = jnp.where(lane < MARGIN, roll_lanes(right, -right_at), halo)
    return jnp.concatenate([main, halo], axis=1)


def shift_matrix(wide):
    source, target = sublanes_of((wide, wide)), lanes_of((wide, wide))
    after, before = source == (target + 1) % wide, target == (source + 1) % wide
    return jnp.where(after, 1.0, jnp.where(before, -1.0, 0.0)).astype(BF16)


def column_slope(x, shift):
    rows, group, wide = x.shape
    x = x.reshape(rows * group, wide)
    top = x.astype(BF16)
    rest = (x - top.astype(F32)).astype(BF16)
    slope = jnp.dot(top, shift, preferred_element_type=F32) + jnp.dot(rest, shift, preferred_element_type=F32)
    return slope.reshape(rows, group, wide)


def interior_kernel(members, rows, place_ref, x_ref, left_ref, right_ref, drag_ref, margin_ref, state, keep, slope, across):
    cols = x_ref.shape[1]
    wide = 2 * cols
    lane = lanes_of((8, cols))
    factor = -0.2 * grid_factor(place_ref, (rows + 2 * MARGIN, wide), rows, cols)
    shift = shift_matrix(wide)
    kept = 1.0 - jnp.concatenate([drag_ref[...], margin_ref[...]], axis=1)
    for r in range(rows):
        keep[r] = jnp.broadcast_to(kept[r : r + 1, :], (GROUP, wide))
        slope[r] = jnp.broadcast_to(factor[MARGIN + r : MARGIN + r + 1, :], (GROUP, wide))

    def first(g, carry):
        here = pl.ds(pl.multiple_of(g * 8, 8), 8)
        for f in range(3):
            at = pl.ds(pl.multiple_of(f * members + g * 8, 8), 8)
            left, right = left_ref[at, :], right_ref[at, :]
            for r in range(rows):
                main = x_ref[pl.ds((f * members + g * 8) * rows + r, 8, stride=rows), :]
                state[f, r, here, :] = wide_row(lane, main, left, MARGIN * r, right, MARGIN * r)
        return carry

    lax.fori_loop(0, members // 8, first, 0)

    def group(g, carry):
        here = pl.ds(pl.multiple_of(g * GROUP, GROUP), GROUP)
        for step in range(STEPS):
            low, high = 1 + 2 * step, rows - 1 - 2 * step
            if low >= high:
                break
            across[low:high] = column_slope(state[1, low:high, here, :], shift)
            for r in range(low, high):
                div = across[r] + (state[2, r + 1, here, :] - state[2, r - 1, here, :])
                state[0, r, here, :] = state[0, r, here, :] + slope[r] * div
            low, high = low + 1, high - 1
            if low >= high:
                break
            across[low:high] = column_slope(state[0, low:high, here, :], shift)
            for r in range(low, high):
                u, v = state[1, r, here, :], state[2, r, here, :]
                k, c = keep[r], slope[r]
                state[1, r, here, :] = k * u + c * across[r] + 0.1 * v
                state[2, r, here, :] = k * v + c * (state[0, r + 1, here, :] - state[0, r - 1, here, :]) - 0.1 * u
        return carry

    lax.fori_loop(0, members // GROUP, group, 0)


def interior(place, x, left, right, drag, margin, members):
    rows, cols = drag.shape
    return pl.pallas_call(
        functools.partial(interior_kernel, members, rows),
        out_shape=jax.ShapeDtypeStruct((3, rows, members, 2 * cols), F32),
        in_specs=[SSPEC] + [VSPEC] * 5,
        out_specs=VSPEC,
        scratch_shapes=[pltpu.VMEM((rows, GROUP, 2 * cols), F32)] * 3,
        compiler_params=pltpu.CompilerParams(vmem_limit_bytes=VMEM_LIMIT),
        cost_estimate=pl.CostEstimate(flops=30_000_000, bytes_accessed=10_000_000, transcendentals=0),
    )(place, x, left, right, drag, margin)


def forecast_kernel(
    members, rows,
    place_ref, order_ref, owner_ref, cell_ref,
    inner_ref, above_ref, below_ref, ceven_ref, codd_ref, drag_ref, margin_ref,
    out_ref, prior_ref,
    state, keep, slope, across,
):
    cols = above_ref.shape[2]
    wide = 2 * cols
    total = rows + 2 * MARGIN
    half = cols // 2
    lane = lanes_of((GROUP, cols))
    factor = -0.2 * grid_factor(place_ref, (total, wide), rows, cols)
    odd_y = place_ref[0] % place_ref[5] % 2 == 1
    shift = shift_matrix(wide)
    count = 3 * members
    parts = []
    for here, own in ((count, drag_ref), (count + MARGIN, margin_ref)):
        even, odd = ceven_ref[here : here + MARGIN, :], codd_ref[here : here + MARGIN, :]
        above, below = jnp.where(odd_y, even, odd), jnp.where(odd_y, odd, even)
        parts.append(jnp.concatenate([above, own[...], below], axis=0))
    kept = 1.0 - jnp.concatenate(parts, axis=1)
    for r in range(total):
        keep[r] = jnp.broadcast_to(kept[r : r + 1, :], (GROUP, wide))
        slope[r] = jnp.broadcast_to(factor[r : r + 1, :], (GROUP, wide))

    def group(g, carry):
        here = pl.ds(pl.multiple_of(g * GROUP, GROUP), GROUP)
        for f in range(3):
            at = pl.ds(pl.multiple_of(f * members + g * GROUP, 8), GROUP)
            ceven, codd = ceven_ref[at, :], codd_ref[at, :]
            cab, cbe = jnp.where(odd_y, ceven, codd), jnp.where(odd_y, codd, ceven)
            depth = MARGIN if f == 2 else MARGIN - 1
            for d in range(depth):
                r = MARGIN - depth + d
                main = above_ref[f * (MARGIN - 1) + d, here, :]
                state[f, r] = wide_row(lane, main, cab, MARGIN * r, cab, half + MARGIN * r)
                main = below_ref[f * (MARGIN - 1) + d, here, :]
                state[f, MARGIN + rows + d] = wide_row(lane, main, cbe, MARGIN * d, cbe, half + MARGIN * d)
            for r in range(rows):
                state[f, MARGIN + r] = inner_ref[f, r, here, :]
        for step in range(STEPS):
            first, last = MARGIN - MARGIN + 1 + 2 * step, MARGIN + rows + MARGIN - 1 - 2 * step
            done, still = MARGIN + 1 + 2 * step, MARGIN + rows - 1 - 2 * step
            spans = ((first, min(done, still)), (max(done, still), last)) if done < still else ((first, last),)
            for low, high in spans:
                across[low:high] = column_slope(state[1, low:high], shift)
            for low, high in spans:
                for r in range(low, high):
                    div = across[r] + (state[2, r + 1] - state[2, r - 1])
                    state[0, r] = state[0, r] + slope[r] * div
            first, last, done, still = first + 1, last - 1, done + 1, still - 1
            spans = ((first, done), (still, last)) if done < still else ((first, MARGIN + rows // 2), (MARGIN + rows // 2, last))
            for low, high in spans:
                across[low:high] = column_slope(state[0, low:high], shift)
            for low, high in spans:
                for r in range(low, high):
                    u, v = state[1, r], state[2, r]
                    k, c = keep[r], slope[r]
                    u, v = (
                        k * u + c * across[r] + 0.1 * v,
                        k * v + c * (state[0, r + 1] - state[0, r - 1]) - 0.1 * u,
                    )
                    state[1, r] = u
                    state[2, r] = v
        for f in range(3):
            for r in range(rows):
                out_ref[f * rows + r, here, :] = state[f, MARGIN + r, :, 0:cols]
        return carry

    lax.fori_loop(0, members // GROUP, group, 0)

    prior_ref[...] = jnp.zeros_like(prior_ref)
    eight = lanes_of((8, cols))
    for i in range(order_ref.shape[0]):
        which = order_ref[i]

        @pl.when(owner_ref[which] == place_ref[0])
        def _():
            cell = cell_ref[which]
            one = jnp.where(eight == cell % cols, 1.0, 0.0)
            prior_ref[i : i + 1, 0:members] = lax.dot_general(
                one, out_ref[cell // cols], NT, precision=HIGHEST, preferred_element_type=F32
            )[0:1]


def forecast(place, order, owner, cell, inner, *arrays):
    _, rows, members, wide = inner.shape
    cols = wide // 2
    total = rows + 2 * MARGIN
    return pl.pallas_call(
        functools.partial(forecast_kernel, members, rows),
        out_shape=(
            jax.ShapeDtypeStruct((3 * rows, members, cols), F32),
            jax.ShapeDtypeStruct((order.shape[0], cols), F32),
        ),
        in_specs=[SSPEC] * 4 + [VSPEC] * (1 + len(arrays)),
        out_specs=(VSPEC, VSPEC),
        scratch_shapes=[pltpu.VMEM((3, total, GROUP, wide), F32)] + [pltpu.VMEM((total, GROUP, wide), F32)] * 3,
        compiler_params=pltpu.CompilerParams(vmem_limit_bytes=VMEM_LIMIT),
        cost_estimate=pl.CostEstimate(flops=60_000_000, bytes_accessed=30_000_000, transcendentals=0),
    )(place, order, owner, cell, inner, *arrays)


def localize(distance, reach, taper_ref):
    picked = jnp.zeros(distance.shape, F32)
    levels = taper_ref.shape[0]
    capped = jnp.minimum(distance, levels - 1)
    for d in range(levels):
        picked = jnp.where(capped == d, taper_ref[d], picked)
    return jnp.where(distance <= reach, picked, 0.0)


def assimilate_kernel(
    members, rows,
    place_ref, order_ref, owner_ref, reach_ref, value_ref, error_ref, taper_ref,
    prior_ref, forecast_ref,
    out_ref,
):
    n_obs = order_ref.shape[0]
    cols = prior_ref.shape[1]
    size_y = place_ref[5]
    lane1 = lanes_of((1, cols))
    lane = lanes_of((n_obs, cols))
    sub = sublanes_of((n_obs, cols))

    tile_row = jnp.zeros((1, cols), jnp.int32)
    tile_col = jnp.zeros((n_obs, cols), jnp.int32)
    reach_row = jnp.zeros((1, cols), jnp.int32)
    reach_col = jnp.zeros((n_obs, cols), jnp.int32)
    which = [order_ref[i] for i in range(n_obs)]
    for i, k in enumerate(which):
        tile_row = jnp.where(lane1 == i, owner_ref[k], tile_row)
        tile_col = jnp.where(sub == i, owner_ref[k], tile_col)
        reach_row = jnp.where(lane1 == i, reach_ref[k], reach_row)
        reach_col = jnp.where(sub == i, reach_ref[k], reach_col)
    rx, ry = tile_row // size_y, tile_row % size_y
    cx, cy = tile_col // size_y, tile_col % size_y
    distance = jnp.maximum(jnp.abs(cx - rx), jnp.abs(cy - ry))
    onto = localize(distance, reach_row, taper_ref)
    onto_t = localize(distance, reach_col, taper_ref)
    mine = place_ref[0]
    own = localize(
        jnp.maximum(jnp.abs(mine // size_y - rx), jnp.abs(mine % size_y - ry)), reach_row, taper_ref
    )

    priors = prior_ref[...]
    inside = lane < members
    mean_col = jnp.sum(jnp.where(inside, priors, 0.0), axis=1, keepdims=True) / members
    anomalies = jnp.where(inside, priors - mean_col, 0.0)
    padded = jnp.concatenate([anomalies, jnp.zeros((cols - n_obs, cols), F32)], axis=0)
    unit = jnp.where(lanes_of((members, cols)) == sublanes_of((members, cols)), 1.0, 0.0)
    table = lax.dot_general(
        jnp.concatenate([anomalies, unit], axis=0), padded, NT, precision=HIGHEST, preferred_element_type=F32
    )
    mean = jnp.zeros((1, cols), F32)
    for i in range(n_obs):
        mean = jnp.where(lane1 == i, mean_col[i : i + 1, :], mean)

    scales = jnp.zeros((1, cols), F32)
    increments = []
    for i, k in enumerate(which):
        error = error_ref[k]
        row = table[i : i + 1, :]
        column = table[:, i : i + 1]
        power = row[:, i : i + 1]
        variance = power / (members - 1) + EPS
        inverse = 1.0 / (variance + error)
        scaled = 1.0 / ((members - 1) * variance)
        shift = variance * (value_ref[k] - mean[:, i : i + 1]) * inverse
        shrink = jnp.sqrt(error * inverse) - 1.0
        weight = scaled * own[:, i : i + 1]
        alpha_row = onto_t[i : i + 1, :] * row * scaled
        later = lane1 > i
        h = jnp.where(later, shrink * alpha_row, 0.0)
        q = jnp.where(later, shrink * (row + h * power), 0.0)
        alpha = jnp.concatenate(
            [onto[:, i : i + 1] * column[:n_obs] * scaled, column[n_obs:] * weight], axis=0
        )
        table = table + column * h + alpha * q
        mean = mean + alpha_row * shift
        now = anomalies[i : i + 1, :]
        increments.append(shift + shrink * now)
        anomalies = anomalies + jnp.where(sub > i, shrink * alpha[:n_obs], 0.0) * now
        scales = jnp.where(lane1 == i, weight, scales)
    left = table[n_obs:, :] * scales
    right = jnp.where(inside, jnp.concatenate(increments, axis=0), 0.0)
    right = jnp.concatenate([right, jnp.zeros((cols - n_obs, cols), F32)], axis=0)
    change = jnp.dot(left, right, precision=HIGHEST, preferred_element_type=F32)
    change = jnp.concatenate([change, jnp.zeros((cols - members, cols), F32)], axis=0)
    change = jnp.transpose(change)[:members, :]
    high = change.astype(BF16).astype(F32)
    low = change - high
    zero = jnp.zeros((members, cols), F32)
    high = jnp.concatenate([high, zero], axis=1)
    low = jnp.concatenate([low, zero], axis=1)
    factor = (high + roll_lanes(high, members) + roll_lanes(low, 2 * members)).astype(BF16)

    block = 4
    for at in range(0, 3 * rows, block):
        x = jnp.concatenate([forecast_ref[at + b] for b in range(block)], axis=1)
        xh = x.astype(BF16)
        xl = (x - xh.astype(F32)).astype(BF16)
        stack = jnp.concatenate([xh, xl, xh, jnp.zeros((2 * cols - 3 * members, block * cols), BF16)], axis=0)
        y = x + jnp.dot(factor, stack, preferred_element_type=F32)
        for b in range(block):
            f, r = divmod(at + b, rows)
            out_ref[pl.ds(f * members * rows + r, members, stride=rows), :] = y[:, b * cols : (b + 1) * cols]


def assimilate(place, order, owner, reach, value, error, taper, priors, states, members, rows):
    cols = priors.shape[1]
    return pl.pallas_call(
        functools.partial(assimilate_kernel, members, rows),
        out_shape=jax.ShapeDtypeStruct((3 * members * rows, cols), F32),
        in_specs=[SSPEC] * 7 + [VSPEC] * 2,
        out_specs=VSPEC,
        compiler_params=pltpu.CompilerParams(vmem_limit_bytes=VMEM_LIMIT),
    )(place, order, owner, reach, value, error, taper, priors, states)


def to_neighbours(axis, lower, upper):
    count = lax.axis_size(axis)
    forward = [(i, i + 1) for i in range(count - 1)]
    backward = [(target, source) for source, target in forward]
    return lax.ppermute(upper, axis, forward), lax.ppermute(lower, axis, backward)


def swap_pairs(x, axis, start):
    pairs = [(i, i + 1) for i in range(start, lax.axis_size(axis) - 1, 2)]
    return lax.ppermute(x, axis, pairs + [(b, a) for a, b in pairs])


def add_over(x, axes):
    for axis in axes:
        count = lax.axis_size(axis)
        if count & (count - 1):
            x = lax.psum(x, axis)
            continue
        span = 1
        while span < count:
            x = x + lax.ppermute(x, axis, [(i, i ^ span) for i in range(count)])
            span *= 2
    return x


def body(status, drag, value, error, taper, order, owner, cell, reach):
    members, rows, cols = status.shape[1:]
    ix, iy = lax.axis_index("gx"), lax.axis_index("gy")
    size_x, size_y = lax.axis_size("gx"), lax.axis_size("gy")
    place = jnp.stack(
        [
            ix * size_y + iy,
            (ix == 0).astype(jnp.int32),
            (ix == size_x - 1).astype(jnp.int32),
            (iy == 0).astype(jnp.int32),
            (iy == size_y - 1).astype(jnp.int32),
            jnp.int32(size_y),
        ]
    ).astype(jnp.int32)
    flat = status.reshape(3 * members * rows, cols)
    lower, upper = bands(flat, members, rows)
    above, below = to_neighbours("gy", lower, upper)
    even, odd = pack(place, flat, drag, members)
    even, odd = swap_pairs(even, "gx", 0), swap_pairs(odd, "gx", 1)
    left, right, margin, even, odd = corner(place, drag, even, odd)
    even, odd = swap_pairs(even, "gy", 0), swap_pairs(odd, "gy", 1)
    inner = interior(place, flat, left, right, drag, margin, members)
    states, priors = forecast(place, order, owner, cell, inner, above, below, even, odd, drag, margin)
    priors = add_over(priors, ("gx", "gy"))
    result = assimilate(place, order, owner, reach, value, error, taper, priors, states, members, rows)
    return result.reshape(status.shape)


def solution(mesh):
    in_specs = (P(None, None, "gy", "gx"), P("gy", "gx"), P(), P(), P(), P(), P(), P(), P())
    out_specs = P(None, None, "gy", "gx")
    return jax.shard_map(body, mesh=mesh, in_specs=in_specs, out_specs=out_specs, check_vma=False)
```

```python
import functools

import jax
import jax.numpy as jnp
from jax import lax
from jax.experimental import pallas as pl
from jax.experimental.pallas import tpu as pltpu
from jax.sharding import PartitionSpec as P

STEPS = 4
MARGIN = 2 * STEPS
EPS = 1e-06
NT = (((1,), (1,)), ((), ()))
HIGHEST = lax.Precision.HIGHEST
F32 = jnp.float32
BF16 = jnp.bfloat16
VMEM_LIMIT = 24 * 1024 * 1024
GROUP = 40

VSPEC = pl.BlockSpec(memory_space=pltpu.VMEM)
SSPEC = pl.BlockSpec(memory_space=pltpu.SMEM)


def lanes_of(shape):
    return lax.broadcasted_iota(jnp.int32, shape, len(shape) - 1)


def sublanes_of(shape):
    return lax.broadcasted_iota(jnp.int32, shape, len(shape) - 2)


def roll_lanes(x, shift):
    size = x.shape[-1]
    shift = shift % size
    return x if shift == 0 else pltpu.roll(x, shift, x.ndim - 1)


def band_kernel(members, rows, x_hbm, lower_hbm, upper_hbm, x_ref, lower_ref, upper_ref, sems):
    def arrive(f):
        field = pl.ds(f * members * rows, members * rows)
        return pltpu.make_async_copy(x_hbm.at[field], x_ref.at[field], sems.at[0, f])

    def leave(f, side):
        source, target = ((lower_ref, lower_hbm), (upper_ref, upper_hbm))[side]
        here = pl.ds(f * (MARGIN - 1), MARGIN if f == 2 else MARGIN - 1)
        return pltpu.make_async_copy(source.at[here], target.at[here], sems.at[1 + side, f])

    for f in range(3):
        arrive(f).start()
    for f in range(3):
        arrive(f).wait()
        depth = MARGIN if f == 2 else MARGIN - 1
        for d in range(depth):
            at = f * members * rows + d
            lower_ref[f * (MARGIN - 1) + d] = x_ref[pl.ds(at, members, stride=rows), :]
            upper_ref[f * (MARGIN - 1) + d] = x_ref[pl.ds(at + rows - depth, members, stride=rows), :]
        leave(f, 0).start()
        leave(f, 1).start()
    for f in range(3):
        leave(f, 0).wait()
        leave(f, 1).wait()


def bands(x, members, rows):
    cols = x.shape[1]
    shape = (3 * MARGIN - 2, members, cols)
    return pl.pallas_call(
        functools.partial(band_kernel, members, rows),
        out_shape=(jax.ShapeDtypeStruct(shape, F32),) * 2,
        in_specs=[pl.BlockSpec(memory_space=pltpu.HBM)],
        out_specs=(pl.BlockSpec(memory_space=pl.ANY),) * 2,
        scratch_shapes=[pltpu.VMEM(x.shape, F32)] + [pltpu.VMEM(shape, F32)] * 2 + [pltpu.SemaphoreType.DMA((3, 3))],
        compiler_params=pltpu.CompilerParams(vmem_limit_bytes=60 * 1024 * 1024),
        cost_estimate=pl.CostEstimate(flops=1_000_000, bytes_accessed=4_000_000, transcendentals=0),
    )(x)


def pack_kernel(members, rows, place_ref, x_ref, drag_ref, even_ref, odd_ref):
    cols = x_ref.shape[1]
    lane = lanes_of((8, cols))
    odd_x = place_ref[0] // place_ref[5] % 2 == 1

    def group(g, carry):
        for f in range(3):
            left = jnp.zeros((8, cols), F32)
            right = jnp.zeros((8, cols), F32)
            for r in range(rows):
                row = x_ref[pl.ds((f * members + g * 8) * rows + r, 8, stride=rows), :]
                there = (lane >= MARGIN * r) & (lane < MARGIN * (r + 1))
                left = jnp.where(there, roll_lanes(row, MARGIN * r), left)
                right = jnp.where(there, roll_lanes(row, MARGIN * (r + 1)), right)
            at = pl.ds(pl.multiple_of(f * members + g * 8, 8), 8)
            even_ref[at, :] = jnp.where(odd_x, left, right)
            odd_ref[at, :] = jnp.where(odd_x, right, left)
        return carry

    lax.fori_loop(0, members // 8, group, 0)
    even_ref[3 * members :, :] = drag_ref[...]
    odd_ref[3 * members :, :] = drag_ref[...]


def pack(place, x, drag, members):
    rows, cols = drag.shape
    message = jax.ShapeDtypeStruct((3 * members + rows, cols), F32)
    return pl.pallas_call(
        functools.partial(pack_kernel, members, rows),
        out_shape=(message, message),
        in_specs=[SSPEC, VSPEC, VSPEC],
        out_specs=(VSPEC,) * 2,
        compiler_params=pltpu.CompilerParams(vmem_limit_bytes=VMEM_LIMIT),
        cost_estimate=pl.CostEstimate(flops=1_000_000, bytes_accessed=4_000_000, transcendentals=0),
    )(place, x, drag)


def corner_kernel(place_ref, drag_ref, even_ref, odd_ref, left_ref, right_ref, margin_ref, even_out, odd_out):
    count, cols = left_ref.shape
    rows = drag_ref.shape[0]
    half = cols // 2
    odd_y = place_ref[0] % place_ref[5] % 2 == 1
    odd_x = place_ref[0] // place_ref[5] % 2 == 1
    even, odd = even_ref[...], odd_ref[...]
    left, right = jnp.where(odd_x, even, odd), jnp.where(odd_x, odd, even)
    margin = jnp.where(lanes_of((rows, cols)) < half, right[count:], left[count:])
    margin_ref[...] = margin
    left, right = left[:count], right[:count]
    left_ref[...] = left
    right_ref[...] = right
    first_half = lanes_of((count, cols)) < half
    lower = jnp.where(first_half, left, roll_lanes(right, half))
    upper = jnp.where(first_half, roll_lanes(left, half), right)
    even_out[:count, :] = jnp.where(odd_y, lower, upper)
    odd_out[:count, :] = jnp.where(odd_y, upper, lower)
    drag = drag_ref[...]
    for at, part in ((count, drag), (count + MARGIN, margin)):
        lower, upper = part[:MARGIN], part[rows - MARGIN :]
        even_out[at : at + MARGIN, :] = jnp.where(odd_y, lower, upper)
        odd_out[at : at + MARGIN, :] = jnp.where(odd_y, upper, lower)


def corner(place, drag, even, odd):
    rows, cols = drag.shape
    count = even.shape[0] - rows
    edge = jax.ShapeDtypeStruct((count, cols), F32)
    message = jax.ShapeDtypeStruct((count + 2 * MARGIN, cols), F32)
    return pl.pallas_call(
        corner_kernel,
        out_shape=(edge, edge, jax.ShapeDtypeStruct((rows, cols), F32), message, message),
        in_specs=[SSPEC] + [VSPEC] * 3,
        out_specs=(VSPEC,) * 5,
        compiler_params=pltpu.CompilerParams(vmem_limit_bytes=VMEM_LIMIT),
    )(place, drag, even, odd)


def grid_factor(place_ref, shape, rows, cols):
    row, col = sublanes_of(shape), lanes_of(shape)
    wide = 2 * cols
    low, high = jnp.where(place_ref[3] == 1, MARGIN, 0), jnp.where(place_ref[4] == 1, MARGIN + rows, rows + 2 * MARGIN)
    first, last = jnp.where(place_ref[1] == 1, wide, wide - MARGIN), jnp.where(place_ref[2] == 1, cols, cols + MARGIN)
    ok = (row >= low) & (row < high) & ((col < last) | (col >= first))
    return jnp.where(ok, 1.0, 0.0)


def wide_row(lane, main, left, left_at, right, right_at):
    cols = main.shape[1]
    halo = jnp.where(lane >= cols - MARGIN, roll_lanes(left, cols - MARGIN - left_at), 0.0)
    halo = jnp.where(lane < MARGIN, roll_lanes(right, -right_at), halo)
    return jnp.concatenate([main, halo], axis=1)


def shift_matrix(wide):
    source, target = sublanes_of((wide, wide)), lanes_of((wide, wide))
    after, before = source == (target + 1) % wide, target == (source + 1) % wide
    return jnp.where(after, 1.0, jnp.where(before, -1.0, 0.0)).astype(BF16)


def tall(x):
    return jnp.concatenate([x] * (GROUP // 8), axis=0)


def column_slope(x, shift):
    rows, group, wide = x.shape
    x = x.reshape(rows * group, wide)
    top = x.astype(BF16)
    rest = (x - top.astype(F32)).astype(BF16)
    slope = jnp.dot(top, shift, preferred_element_type=F32) + jnp.dot(rest, shift, preferred_element_type=F32)
    return slope.reshape(rows, group, wide)


def interior_kernel(members, rows, place_ref, x_ref, left_ref, right_ref, drag_ref, margin_ref, state, keep, slope):
    cols = x_ref.shape[1]
    wide = 2 * cols
    lane = lanes_of((8, cols))
    factor = -0.2 * grid_factor(place_ref, (rows + 2 * MARGIN, wide), rows, cols)
    shift = shift_matrix(wide)
    kept = 1.0 - jnp.concatenate([drag_ref[...], margin_ref[...]], axis=1)
    for r in range(rows):
        keep[r] = jnp.broadcast_to(kept[r : r + 1, :], (8, wide))
        slope[r] = jnp.broadcast_to(factor[MARGIN + r : MARGIN + r + 1, :], (8, wide))

    def first(g, carry):
        here = pl.ds(pl.multiple_of(g * 8, 8), 8)
        for f in range(3):
            at = pl.ds(pl.multiple_of(f * members + g * 8, 8), 8)
            left, right = left_ref[at, :], right_ref[at, :]
            for r in range(rows):
                main = x_ref[pl.ds((f * members + g * 8) * rows + r, 8, stride=rows), :]
                state[f, r, here, :] = wide_row(lane, main, left, MARGIN * r, right, MARGIN * r)
        return carry

    lax.fori_loop(0, members // 8, first, 0)

    groups = [pl.ds(m, GROUP) for m in range(0, members, GROUP)]
    for step in range(STEPS):
        low, high = 1 + 2 * step, rows - 1 - 2 * step
        if low >= high:
            break
        for here in groups:
            d = column_slope(state[1, low:high, here, :], shift)
            for r in range(low, high):
                div = d[r - low] + (state[2, r + 1, here, :] - state[2, r - 1, here, :])
                state[0, r, here, :] = state[0, r, here, :] + tall(slope[r]) * div
        low, high = low + 1, high - 1
        if low >= high:
            break
        for here in groups:
            d = column_slope(state[0, low:high, here, :], shift)
            for r in range(low, high):
                u, v = state[1, r, here, :], state[2, r, here, :]
                k, c = tall(keep[r]), tall(slope[r])
                state[1, r, here, :] = k * u + c * d[r - low] + 0.1 * v
                state[2, r, here, :] = k * v + c * (state[0, r + 1, here, :] - state[0, r - 1, here, :]) - 0.1 * u


def interior(place, x, left, right, drag, margin, members):
    rows, cols = drag.shape
    return pl.pallas_call(
        functools.partial(interior_kernel, members, rows),
        out_shape=jax.ShapeDtypeStruct((3, rows, members, 2 * cols), F32),
        in_specs=[SSPEC] + [VSPEC] * 5,
        out_specs=VSPEC,
        scratch_shapes=[pltpu.VMEM((rows, 8, 2 * cols), F32)] * 2,
        compiler_params=pltpu.CompilerParams(vmem_limit_bytes=VMEM_LIMIT),
        cost_estimate=pl.CostEstimate(flops=30_000_000, bytes_accessed=10_000_000, transcendentals=0),
    )(place, x, left, right, drag, margin)


def forecast_kernel(
    members, rows,
    place_ref, order_ref, owner_ref, cell_ref,
    inner_ref, above_ref, below_ref, ceven_ref, codd_ref, drag_ref, margin_ref,
    out_ref, prior_ref,
    state, keep, slope,
):
    cols = above_ref.shape[2]
    wide = 2 * cols
    total = rows + 2 * MARGIN
    half = cols // 2
    lane = lanes_of((GROUP, cols))
    factor = -0.2 * grid_factor(place_ref, (total, wide), rows, cols)
    odd_y = place_ref[0] % place_ref[5] % 2 == 1
    shift = shift_matrix(wide)
    count = 3 * members
    parts = []
    for here, own in ((count, drag_ref), (count + MARGIN, margin_ref)):
        even, odd = ceven_ref[here : here + MARGIN, :], codd_ref[here : here + MARGIN, :]
        above, below = jnp.where(odd_y, even, odd), jnp.where(odd_y, odd, even)
        parts.append(jnp.concatenate([above, own[...], below], axis=0))
    kept = 1.0 - jnp.concatenate(parts, axis=1)
    for r in range(total):
        keep[r] = jnp.broadcast_to(kept[r : r + 1, :], (8, wide))
        slope[r] = jnp.broadcast_to(factor[r : r + 1, :], (8, wide))

    groups = range(members // GROUP)
    for g in groups:
        here = pl.ds(g * GROUP, GROUP)
        for f in range(3):
            at = pl.ds(f * members + g * GROUP, GROUP)
            ceven, codd = ceven_ref[at, :], codd_ref[at, :]
            cab, cbe = jnp.where(odd_y, ceven, codd), jnp.where(odd_y, codd, ceven)
            depth = MARGIN if f == 2 else MARGIN - 1
            for d in range(depth):
                r = MARGIN - depth + d
                main = above_ref[f * (MARGIN - 1) + d, here, :]
                state[g, f, r] = wide_row(lane, main, cab, MARGIN * r, cab, half + MARGIN * r)
                main = below_ref[f * (MARGIN - 1) + d, here, :]
                state[g, f, MARGIN + rows + d] = wide_row(lane, main, cbe, MARGIN * d, cbe, half + MARGIN * d)
            for r in range(rows):
                state[g, f, MARGIN + r] = inner_ref[f, r, here, :]

    def heights(g, spans):
        for low, high in spans:
            d = column_slope(state[g, 1, low:high], shift)
            for r in range(low, high):
                div = d[r - low] + (state[g, 2, r + 1] - state[g, 2, r - 1])
                state[g, 0, r] = state[g, 0, r] + tall(slope[r]) * div

    def flows(g, spans):
        for low, high in spans:
            d = column_slope(state[g, 0, low:high], shift)
            for r in range(low, high):
                u, v = state[g, 1, r], state[g, 2, r]
                k, c = tall(keep[r]), tall(slope[r])
                state[g, 1, r] = k * u + c * d[r - low] + 0.1 * v
                state[g, 2, r] = k * v + c * (state[g, 0, r + 1] - state[g, 0, r - 1]) - 0.1 * u

    for step in range(STEPS):
        first, last = MARGIN - MARGIN + 1 + 2 * step, MARGIN + rows + MARGIN - 1 - 2 * step
        done, still = MARGIN + 1 + 2 * step, MARGIN + rows - 1 - 2 * step
        for g in groups:
            heights(g, ((first, done), (still, last)))
        for g in groups:
            flows(g, ((first + 1, done + 1), (still - 1, last - 1)))
    for g in groups:
        here = pl.ds(g * GROUP, GROUP)
        for f in range(3):
            for r in range(rows):
                out_ref[f * rows + r, here, :] = state[g, f, MARGIN + r, :, 0:cols]

    prior_ref[...] = jnp.zeros_like(prior_ref)
    eight = lanes_of((8, cols))
    for i in range(order_ref.shape[0]):
        which = order_ref[i]

        @pl.when(owner_ref[which] == place_ref[0])
        def _():
            cell = cell_ref[which]
            one = jnp.where(eight == cell % cols, 1.0, 0.0)
            prior_ref[i : i + 1, 0:members] = lax.dot_general(
                one, out_ref[cell // cols], NT, precision=HIGHEST, preferred_element_type=F32
            )[0:1]


def forecast(place, order, owner, cell, inner, *arrays):
    _, rows, members, wide = inner.shape
    cols = wide // 2
    total = rows + 2 * MARGIN
    return pl.pallas_call(
        functools.partial(forecast_kernel, members, rows),
        out_shape=(
            jax.ShapeDtypeStruct((3 * rows, members, cols), F32),
            jax.ShapeDtypeStruct((order.shape[0], cols), F32),
        ),
        in_specs=[SSPEC] * 4 + [VSPEC] * (1 + len(arrays)),
        out_specs=(VSPEC, VSPEC),
        scratch_shapes=[pltpu.VMEM((members // GROUP, 3, total, GROUP, wide), F32)] + [pltpu.VMEM((total, 8, wide), F32)] * 2,
        compiler_params=pltpu.CompilerParams(vmem_limit_bytes=VMEM_LIMIT),
        cost_estimate=pl.CostEstimate(flops=60_000_000, bytes_accessed=30_000_000, transcendentals=0),
    )(place, order, owner, cell, inner, *arrays)


def localize(distance, reach, taper_ref):
    picked = jnp.zeros(distance.shape, F32)
    levels = taper_ref.shape[0]
    capped = jnp.minimum(distance, levels - 1)
    for d in range(levels):
        picked = jnp.where(capped == d, taper_ref[d], picked)
    return jnp.where(distance <= reach, picked, 0.0)


def assimilate_kernel(
    members, rows,
    place_ref, order_ref, owner_ref, reach_ref, value_ref, error_ref, taper_ref,
    prior_ref, forecast_ref,
    result_ref,
    out_ref, sems,
):
    n_obs = order_ref.shape[0]
    cols = prior_ref.shape[1]
    size_y = place_ref[5]
    lane1 = lanes_of((1, cols))
    lane = lanes_of((n_obs, cols))
    sub = sublanes_of((n_obs, cols))

    tile_row = jnp.zeros((1, cols), jnp.int32)
    tile_col = jnp.zeros((n_obs, cols), jnp.int32)
    reach_row = jnp.zeros((1, cols), jnp.int32)
    reach_col = jnp.zeros((n_obs, cols), jnp.int32)
    which = [order_ref[i] for i in range(n_obs)]
    for i, k in enumerate(which):
        tile_row = jnp.where(lane1 == i, owner_ref[k], tile_row)
        tile_col = jnp.where(sub == i, owner_ref[k], tile_col)
        reach_row = jnp.where(lane1 == i, reach_ref[k], reach_row)
        reach_col = jnp.where(sub == i, reach_ref[k], reach_col)
    rx, ry = tile_row // size_y, tile_row % size_y
    cx, cy = tile_col // size_y, tile_col % size_y
    distance = jnp.maximum(jnp.abs(cx - rx), jnp.abs(cy - ry))
    onto = localize(distance, reach_row, taper_ref)
    onto_t = localize(distance, reach_col, taper_ref)
    mine = place_ref[0]
    own = localize(
        jnp.maximum(jnp.abs(mine // size_y - rx), jnp.abs(mine % size_y - ry)), reach_row, taper_ref
    )

    priors = prior_ref[...]
    inside = lane < members
    mean_col = jnp.sum(jnp.where(inside, priors, 0.0), axis=1, keepdims=True) / members
    anomalies = jnp.where(inside, priors - mean_col, 0.0)
    padded = jnp.concatenate([anomalies, jnp.zeros((cols - n_obs, cols), F32)], axis=0)
    unit = jnp.where(lanes_of((members, cols)) == sublanes_of((members, cols)), 1.0, 0.0)
    table = lax.dot_general(
        jnp.concatenate([anomalies, unit], axis=0), padded, NT, precision=HIGHEST, preferred_element_type=F32
    )
    mean = jnp.zeros((1, cols), F32)
    for i in range(n_obs):
        mean = jnp.where(lane1 == i, mean_col[i : i + 1, :], mean)

    scales = jnp.zeros((1, cols), F32)
    increments = []
    for i, k in enumerate(which):
        error = error_ref[k]
        row = table[i : i + 1, :]
        column = table[:, i : i + 1]
        power = row[:, i : i + 1]
        variance = power / (members - 1) + EPS
        inverse = 1.0 / (variance + error)
        scaled = 1.0 / ((members - 1) * variance)
        shift = variance * (value_ref[k] - mean[:, i : i + 1]) * inverse
        shrink = jnp.sqrt(error * inverse) - 1.0
        weight = scaled * own[:, i : i + 1]
        alpha_row = onto_t[i : i + 1, :] * row * scaled
        later = lane1 > i
        h = jnp.where(later, shrink * alpha_row, 0.0)
        q = jnp.where(later, shrink * (row + h * power), 0.0)
        alpha = jnp.concatenate(
            [onto[:, i : i + 1] * column[:n_obs] * scaled, column[n_obs:] * weight], axis=0
        )
        table = table + column * h + alpha * q
        mean = mean + alpha_row * shift
        now = anomalies[i : i + 1, :]
        increments.append(shift + shrink * now)
        anomalies = anomalies + jnp.where(sub > i, shrink * alpha[:n_obs], 0.0) * now
        scales = jnp.where(lane1 == i, weight, scales)
    left = table[n_obs:, :] * scales
    right = jnp.where(inside, jnp.concatenate(increments, axis=0), 0.0)
    right = jnp.concatenate([right, jnp.zeros((cols - n_obs, cols), F32)], axis=0)
    change = jnp.dot(left, right, precision=HIGHEST, preferred_element_type=F32)
    change = jnp.concatenate([change, jnp.zeros((cols - members, cols), F32)], axis=0)
    change = jnp.transpose(change)[:members, :]
    high = change.astype(BF16).astype(F32)
    low = change - high
    zero = jnp.zeros((members, cols), F32)
    high = jnp.concatenate([high, zero], axis=1)
    low = jnp.concatenate([low, zero], axis=1)
    factor = (high + roll_lanes(high, members) + roll_lanes(low, 2 * members)).astype(BF16)

    block = 4
    for at in range(0, 3 * rows, block):
        x = jnp.concatenate([forecast_ref[at + b] for b in range(block)], axis=1)
        xh = x.astype(BF16)
        xl = (x - xh.astype(F32)).astype(BF16)
        stack = jnp.concatenate([xh, xl, xh, jnp.zeros((2 * cols - 3 * members, block * cols), BF16)], axis=0)
        y = x + jnp.dot(factor, stack, preferred_element_type=F32)
        for b in range(block):
            f, r = divmod(at + b, rows)
            out_ref[pl.ds(f * members * rows + r, members, stride=rows), :] = y[:, b * cols : (b + 1) * cols]
        if (at + block) % rows == 0:
            field = pl.ds(at // rows * members * rows, members * rows)
            pltpu.make_async_copy(out_ref.at[field], result_ref.at[field], sems.at[at // rows]).start()
    for f in range(3):
        field = pl.ds(f * members * rows, members * rows)
        pltpu.make_async_copy(out_ref.at[field], result_ref.at[field], sems.at[f]).wait()


def assimilate(place, order, owner, reach, value, error, taper, priors, states, members, rows):
    cols = priors.shape[1]
    return pl.pallas_call(
        functools.partial(assimilate_kernel, members, rows),
        out_shape=jax.ShapeDtypeStruct((3 * members * rows, cols), F32),
        in_specs=[SSPEC] * 7 + [VSPEC] * 2,
        out_specs=pl.BlockSpec(memory_space=pl.ANY),
        scratch_shapes=[pltpu.VMEM((3 * members * rows, cols), F32), pltpu.SemaphoreType.DMA((3,))],
        compiler_params=pltpu.CompilerParams(vmem_limit_bytes=VMEM_LIMIT),
    )(place, order, owner, reach, value, error, taper, priors, states)


def to_neighbours(axis, lower, upper):
    count = lax.axis_size(axis)
    forward = [(i, i + 1) for i in range(count - 1)]
    backward = [(target, source) for source, target in forward]
    return lax.ppermute(upper, axis, forward), lax.ppermute(lower, axis, backward)


def swap_pairs(x, axis, start):
    pairs = [(i, i + 1) for i in range(start, lax.axis_size(axis) - 1, 2)]
    return lax.ppermute(x, axis, pairs + [(b, a) for a, b in pairs])


def add_over(x, axes):
    for axis in axes:
        count = lax.axis_size(axis)
        if count & (count - 1):
            x = lax.psum(x, axis)
            continue
        span = 1
        while span < count:
            x = x + lax.ppermute(x, axis, [(i, i ^ span) for i in range(count)])
            span *= 2
    return x


def body(status, drag, value, error, taper, order, owner, cell, reach):
    members, rows, cols = status.shape[1:]
    ix, iy = lax.axis_index("gx"), lax.axis_index("gy")
    size_x, size_y = lax.axis_size("gx"), lax.axis_size("gy")
    place = jnp.stack(
        [
            ix * size_y + iy,
            (ix == 0).astype(jnp.int32),
            (ix == size_x - 1).astype(jnp.int32),
            (iy == 0).astype(jnp.int32),
            (iy == size_y - 1).astype(jnp.int32),
            jnp.int32(size_y),
        ]
    ).astype(jnp.int32)
    flat = status.reshape(3 * members * rows, cols)
    lower, upper = bands(flat, members, rows)
    above, below = to_neighbours("gy", lower, upper)
    even, odd = pack(place, flat, drag, members)
    even, odd = swap_pairs(even, "gx", 0), swap_pairs(odd, "gx", 1)
    left, right, margin, even, odd = corner(place, drag, even, odd)
    even, odd = swap_pairs(even, "gy", 0), swap_pairs(odd, "gy", 1)
    inner = interior(place, flat, left, right, drag, margin, members)
    states, priors = forecast(place, order, owner, cell, inner, above, below, even, odd, drag, margin)
    priors = add_over(priors, ("gx", "gy"))
    result = assimilate(place, order, owner, reach, value, error, taper, priors, states, members, rows)
    return result.reshape(status.shape)


def solution(mesh):
    in_specs = (P(None, None, "gy", "gx"), P("gy", "gx"), P(), P(), P(), P(), P(), P(), P())
    out_specs = P(None, None, "gy", "gx")
    return jax.shard_map(body, mesh=mesh, in_specs=in_specs, out_specs=out_specs, check_vma=False)
```

```python
import functools

import jax
import jax.numpy as jnp
from jax import lax
from jax.experimental import pallas as pl
from jax.experimental.pallas import tpu as pltpu
from jax.sharding import PartitionSpec as P

STEPS = 4
MARGIN = 2 * STEPS
EPS = 1e-06
NT = (((1,), (1,)), ((), ()))
HIGHEST = lax.Precision.HIGHEST
F32 = jnp.float32
BF16 = jnp.bfloat16
VMEM_LIMIT = 24 * 1024 * 1024
GROUP = 40

VSPEC = pl.BlockSpec(memory_space=pltpu.VMEM)
SSPEC = pl.BlockSpec(memory_space=pltpu.SMEM)


def lanes_of(shape):
    return lax.broadcasted_iota(jnp.int32, shape, len(shape) - 1)


def sublanes_of(shape):
    return lax.broadcasted_iota(jnp.int32, shape, len(shape) - 2)


def roll_lanes(x, shift):
    size = x.shape[-1]
    shift = shift % size
    return x if shift == 0 else pltpu.roll(x, shift, x.ndim - 1)


def band_kernel(members, rows, x_hbm, lower_hbm, upper_hbm, x_ref, lower_ref, upper_ref, sems):
    def arrive(f):
        field = pl.ds(f * members * rows, members * rows)
        return pltpu.make_async_copy(x_hbm.at[field], x_ref.at[field], sems.at[0, f])

    def leave(f, side):
        source, target = ((lower_ref, lower_hbm), (upper_ref, upper_hbm))[side]
        here = pl.ds(f * (MARGIN - 1), MARGIN if f == 2 else MARGIN - 1)
        return pltpu.make_async_copy(source.at[here], target.at[here], sems.at[1 + side, f])

    for f in range(3):
        arrive(f).start()
    for f in range(3):
        arrive(f).wait()
        depth = MARGIN if f == 2 else MARGIN - 1
        for d in range(depth):
            at = f * members * rows + d
            lower_ref[f * (MARGIN - 1) + d] = x_ref[pl.ds(at, members, stride=rows), :]
            upper_ref[f * (MARGIN - 1) + d] = x_ref[pl.ds(at + rows - depth, members, stride=rows), :]
        leave(f, 0).start()
        leave(f, 1).start()
    for f in range(3):
        leave(f, 0).wait()
        leave(f, 1).wait()


def bands(x, members, rows):
    cols = x.shape[1]
    shape = (3 * MARGIN - 2, members, cols)
    return pl.pallas_call(
        functools.partial(band_kernel, members, rows),
        out_shape=(jax.ShapeDtypeStruct(shape, F32),) * 2,
        in_specs=[pl.BlockSpec(memory_space=pltpu.HBM)],
        out_specs=(pl.BlockSpec(memory_space=pl.ANY),) * 2,
        scratch_shapes=[pltpu.VMEM(x.shape, F32)] + [pltpu.VMEM(shape, F32)] * 2 + [pltpu.SemaphoreType.DMA((3, 3))],
        compiler_params=pltpu.CompilerParams(vmem_limit_bytes=60 * 1024 * 1024),
        cost_estimate=pl.CostEstimate(flops=1_000_000, bytes_accessed=4_000_000, transcendentals=0),
    )(x)


def pack_kernel(members, rows, place_ref, x_ref, drag_ref, even_ref, odd_ref):
    cols = x_ref.shape[1]
    lane = lanes_of((8, cols))
    odd_x = place_ref[0] // place_ref[5] % 2 == 1

    def group(g, carry):
        for f in range(3):
            left = jnp.zeros((8, cols), F32)
            right = jnp.zeros((8, cols), F32)
            for r in range(rows):
                row = x_ref[pl.ds((f * members + g * 8) * rows + r, 8, stride=rows), :]
                slot = lane // MARGIN
                left = jnp.where(slot == rows - 1 - r, roll_lanes(row, MARGIN * (rows - 1 - r)), left)
                right = jnp.where(slot == r, roll_lanes(row, MARGIN * (r + 1)), right)
            at = pl.ds(pl.multiple_of(f * members + g * 8, 8), 8)
            even_ref[at, :] = jnp.where(odd_x, left, right)
            odd_ref[at, :] = jnp.where(odd_x, right, left)
        return carry

    lax.fori_loop(0, members // 8, group, 0)
    even_ref[3 * members :, :] = drag_ref[...]
    odd_ref[3 * members :, :] = drag_ref[...]


def pack(place, x, drag, members):
    rows, cols = drag.shape
    message = jax.ShapeDtypeStruct((3 * members + rows, cols), F32)
    return pl.pallas_call(
        functools.partial(pack_kernel, members, rows),
        out_shape=(message, message),
        in_specs=[SSPEC, VSPEC, VSPEC],
        out_specs=(VSPEC,) * 2,
        compiler_params=pltpu.CompilerParams(vmem_limit_bytes=VMEM_LIMIT),
        cost_estimate=pl.CostEstimate(flops=1_000_000, bytes_accessed=4_000_000, transcendentals=0),
    )(place, x, drag)


def corner_kernel(place_ref, drag_ref, even_ref, odd_ref, left_ref, right_ref, margin_ref, even_out, odd_out):
    count, cols = left_ref.shape
    rows = drag_ref.shape[0]
    half = cols // 2
    odd_y = place_ref[0] % place_ref[5] % 2 == 1
    odd_x = place_ref[0] // place_ref[5] % 2 == 1
    even, odd = even_ref[...], odd_ref[...]
    left, right = jnp.where(odd_x, even, odd), jnp.where(odd_x, odd, even)
    margin = jnp.where(lanes_of((rows, cols)) < half, right[count:], left[count:])
    margin_ref[...] = margin
    left, right = left[:count], right[:count]
    left_ref[...] = left
    right_ref[...] = right
    lane = lanes_of((count, cols))
    slot, column = lane % half // MARGIN, lane % MARGIN
    mine = column > jnp.where(lane < half, slot, MARGIN - 1 - slot)
    both = jnp.where(mine, left, roll_lanes(right, half))
    count = count // 2
    head, tail = both[:count], both[count:]
    first_half = lanes_of((count, cols)) < half
    lower = jnp.where(first_half, head, roll_lanes(tail, half))
    upper = jnp.where(first_half, roll_lanes(head, half), tail)
    even_out[:count, :] = jnp.where(odd_y, lower, upper)
    odd_out[:count, :] = jnp.where(odd_y, upper, lower)
    drag = drag_ref[...]
    for at, part in ((count, drag), (count + MARGIN, margin)):
        lower, upper = part[:MARGIN], part[rows - MARGIN :]
        even_out[at : at + MARGIN, :] = jnp.where(odd_y, lower, upper)
        odd_out[at : at + MARGIN, :] = jnp.where(odd_y, upper, lower)


def corner(place, drag, even, odd):
    rows, cols = drag.shape
    count = even.shape[0] - rows
    edge = jax.ShapeDtypeStruct((count, cols), F32)
    message = jax.ShapeDtypeStruct((count // 2 + 2 * MARGIN, cols), F32)
    return pl.pallas_call(
        corner_kernel,
        out_shape=(edge, edge, jax.ShapeDtypeStruct((rows, cols), F32), message, message),
        in_specs=[SSPEC] + [VSPEC] * 3,
        out_specs=(VSPEC,) * 5,
        compiler_params=pltpu.CompilerParams(vmem_limit_bytes=VMEM_LIMIT),
    )(place, drag, even, odd)


def grid_factor(place_ref, shape, rows, cols):
    row, col = sublanes_of(shape), lanes_of(shape)
    wide = 2 * cols
    low, high = jnp.where(place_ref[3] == 1, MARGIN, 0), jnp.where(place_ref[4] == 1, MARGIN + rows, rows + 2 * MARGIN)
    first, last = jnp.where(place_ref[1] == 1, wide, wide - MARGIN), jnp.where(place_ref[2] == 1, cols, cols + MARGIN)
    ok = (row >= low) & (row < high) & ((col < last) | (col >= first))
    return jnp.where(ok, 1.0, 0.0)


def wide_row(lane, main, left, left_at, right, right_at):
    cols = main.shape[1]
    halo = jnp.where(lane >= cols - MARGIN, roll_lanes(left, cols - MARGIN - left_at), 0.0)
    halo = jnp.where(lane < MARGIN, roll_lanes(right, -right_at), halo)
    return jnp.concatenate([main, halo], axis=1)


def shift_matrix(wide):
    source, target = sublanes_of((wide, wide)), lanes_of((wide, wide))
    after, before = source == (target + 1) % wide, target == (source + 1) % wide
    return jnp.where(after, 1.0, jnp.where(before, -1.0, 0.0)).astype(BF16)


def tall(x):
    return jnp.concatenate([x] * (GROUP // 8), axis=0)


def column_slope(x, shift):
    rows, group, wide = x.shape
    x = x.reshape(rows * group, wide)
    top = x.astype(BF16)
    rest = (x - top.astype(F32)).astype(BF16)
    slope = jnp.dot(top, shift, preferred_element_type=F32) + jnp.dot(rest, shift, preferred_element_type=F32)
    return slope.reshape(rows, group, wide)


def interior_kernel(members, rows, place_ref, x_ref, left_ref, right_ref, drag_ref, margin_ref, state, keep, slope):
    cols = x_ref.shape[1]
    wide = 2 * cols
    lane = lanes_of((8, cols))
    factor = -0.2 * grid_factor(place_ref, (rows + 2 * MARGIN, wide), rows, cols)
    shift = shift_matrix(wide)
    kept = 1.0 - jnp.concatenate([drag_ref[...], margin_ref[...]], axis=1)
    for r in range(rows):
        keep[r] = jnp.broadcast_to(kept[r : r + 1, :], (8, wide))
        slope[r] = jnp.broadcast_to(factor[MARGIN + r : MARGIN + r + 1, :], (8, wide))

    def first(g, carry):
        here = pl.ds(pl.multiple_of(g * 8, 8), 8)
        for f in range(3):
            at = pl.ds(pl.multiple_of(f * members + g * 8, 8), 8)
            left, right = left_ref[at, :], right_ref[at, :]
            for r in range(rows):
                main = x_ref[pl.ds((f * members + g * 8) * rows + r, 8, stride=rows), :]
                state[f, r, here, :] = wide_row(lane, main, left, MARGIN * r, right, MARGIN * (rows - 1 - r))
        return carry

    lax.fori_loop(0, members // 8, first, 0)

    groups = [pl.ds(m, GROUP) for m in range(0, members, GROUP)]
    for step in range(STEPS):
        low, high = 1 + 2 * step, rows - 1 - 2 * step
        if low >= high:
            break
        for here in groups:
            d = column_slope(state[1, low:high, here, :], shift)
            for r in range(low, high):
                div = d[r - low] + (state[2, r + 1, here, :] - state[2, r - 1, here, :])
                state[0, r, here, :] = state[0, r, here, :] + tall(slope[r]) * div
        low, high = low + 1, high - 1
        if low >= high:
            break
        for here in groups:
            d = column_slope(state[0, low:high, here, :], shift)
            for r in range(low, high):
                u, v = state[1, r, here, :], state[2, r, here, :]
                k, c = tall(keep[r]), tall(slope[r])
                state[1, r, here, :] = k * u + c * d[r - low] + 0.1 * v
                state[2, r, here, :] = k * v + c * (state[0, r + 1, here, :] - state[0, r - 1, here, :]) - 0.1 * u


def interior(place, x, left, right, drag, margin, members):
    rows, cols = drag.shape
    return pl.pallas_call(
        functools.partial(interior_kernel, members, rows),
        out_shape=jax.ShapeDtypeStruct((3, rows, members, 2 * cols), F32),
        in_specs=[SSPEC] + [VSPEC] * 5,
        out_specs=VSPEC,
        scratch_shapes=[pltpu.VMEM((rows, 8, 2 * cols), F32)] * 2,
        compiler_params=pltpu.CompilerParams(vmem_limit_bytes=VMEM_LIMIT),
        cost_estimate=pl.CostEstimate(flops=30_000_000, bytes_accessed=10_000_000, transcendentals=0),
    )(place, x, left, right, drag, margin)


def forecast_kernel(
    members, rows,
    place_ref, order_ref, owner_ref, cell_ref,
    inner_ref, above_ref, below_ref, ceven_ref, codd_ref, drag_ref, margin_ref,
    out_ref, prior_ref,
    state, keep, slope,
):
    cols = above_ref.shape[2]
    wide = 2 * cols
    total = rows + 2 * MARGIN
    half = cols // 2
    lane = lanes_of((GROUP, cols))
    factor = -0.2 * grid_factor(place_ref, (total, wide), rows, cols)
    odd_y = place_ref[0] % place_ref[5] % 2 == 1
    shift = shift_matrix(wide)
    count = 3 * members // 2
    parts = []
    for here, own in ((count, drag_ref), (count + MARGIN, margin_ref)):
        even, odd = ceven_ref[here : here + MARGIN, :], codd_ref[here : here + MARGIN, :]
        above, below = jnp.where(odd_y, even, odd), jnp.where(odd_y, odd, even)
        parts.append(jnp.concatenate([above, own[...], below], axis=0))
    kept = 1.0 - jnp.concatenate(parts, axis=1)
    for r in range(total):
        keep[r] = jnp.broadcast_to(kept[r : r + 1, :], (8, wide))
        slope[r] = jnp.broadcast_to(factor[r : r + 1, :], (8, wide))

    groups = range(members // GROUP)
    for g in groups:
        here = pl.ds(g * GROUP, GROUP)
        for f in range(3):
            at = f * members + g * GROUP
            base = half if at >= count else 0
            at = pl.ds(at % count, GROUP)
            ceven, codd = ceven_ref[at, :], codd_ref[at, :]
            cab, cbe = jnp.where(odd_y, ceven, codd), jnp.where(odd_y, codd, ceven)
            depth = MARGIN if f == 2 else MARGIN - 1
            for d in range(depth):
                r = MARGIN - depth + d
                main = above_ref[f * (MARGIN - 1) + d, here, :]
                state[g, f, r] = wide_row(lane, main, cab, base + MARGIN * r, cab, base + MARGIN * (MARGIN - 1 - r))
                main = below_ref[f * (MARGIN - 1) + d, here, :]
                state[g, f, MARGIN + rows + d] = wide_row(
                    lane, main, cbe, base + MARGIN * d, cbe, base + MARGIN * (MARGIN - 1 - d)
                )
            for r in range(rows):
                state[g, f, MARGIN + r] = inner_ref[f, r, here, :]

    def heights(g, spans):
        for low, high in spans:
            d = column_slope(state[g, 1, low:high], shift)
            for r in range(low, high):
                div = d[r - low] + (state[g, 2, r + 1] - state[g, 2, r - 1])
                state[g, 0, r] = state[g, 0, r] + tall(slope[r]) * div

    def flows(g, spans, final):
        here = pl.ds(g * GROUP, GROUP)
        for low, high in spans:
            d = column_slope(state[g, 0, low:high], shift)
            for r in range(low, high):
                u, v = state[g, 1, r], state[g, 2, r]
                k, c = tall(keep[r]), tall(slope[r])
                u, v = (
                    k * u + c * d[r - low] + 0.1 * v,
                    k * v + c * (state[g, 0, r + 1] - state[g, 0, r - 1]) - 0.1 * u,
                )
                if final:
                    for f, value in enumerate((state[g, 0, r], u, v)):
                        out_ref[f * rows + r - MARGIN, here, :] = value[:, 0:cols]
                else:
                    state[g, 1, r] = u
                    state[g, 2, r] = v

    for step in range(STEPS):
        first, last = MARGIN - MARGIN + 1 + 2 * step, MARGIN + rows + MARGIN - 1 - 2 * step
        done, still = MARGIN + 1 + 2 * step, MARGIN + rows - 1 - 2 * step
        for g in groups:
            heights(g, ((first, done), (still, last)))
        for g in groups:
            flows(g, ((first + 1, done + 1), (still - 1, last - 1)), step == STEPS - 1)
    prior_ref[...] = jnp.zeros_like(prior_ref)
    eight = lanes_of((8, cols))
    for i in range(order_ref.shape[0]):
        which = order_ref[i]

        @pl.when(owner_ref[which] == place_ref[0])
        def _():
            cell = cell_ref[which]
            one = jnp.where(eight == cell % cols, 1.0, 0.0)
            prior_ref[i : i + 1, 0:members] = lax.dot_general(
                one, out_ref[cell // cols], NT, precision=HIGHEST, preferred_element_type=F32
            )[0:1]


def forecast(place, order, owner, cell, inner, *arrays):
    _, rows, members, wide = inner.shape
    cols = wide // 2
    total = rows + 2 * MARGIN
    return pl.pallas_call(
        functools.partial(forecast_kernel, members, rows),
        out_shape=(
            jax.ShapeDtypeStruct((3 * rows, members, cols), F32),
            jax.ShapeDtypeStruct((order.shape[0], cols), F32),
        ),
        in_specs=[SSPEC] * 4 + [VSPEC] * (1 + len(arrays)),
        out_specs=(VSPEC, VSPEC),
        scratch_shapes=[pltpu.VMEM((members // GROUP, 3, total, GROUP, wide), F32)] + [pltpu.VMEM((total, 8, wide), F32)] * 2,
        compiler_params=pltpu.CompilerParams(vmem_limit_bytes=VMEM_LIMIT),
        cost_estimate=pl.CostEstimate(flops=60_000_000, bytes_accessed=30_000_000, transcendentals=0),
    )(place, order, owner, cell, inner, *arrays)


def localize(distance, reach, taper_ref):
    picked = jnp.zeros(distance.shape, F32)
    levels = taper_ref.shape[0]
    capped = jnp.minimum(distance, levels - 1)
    for d in range(levels):
        picked = jnp.where(capped == d, taper_ref[d], picked)
    return jnp.where(distance <= reach, picked, 0.0)


def assimilate_kernel(
    members, rows,
    place_ref, order_ref, owner_ref, reach_ref, value_ref, error_ref, taper_ref,
    prior_ref, forecast_ref,
    result_ref,
    out_ref, sems,
):
    n_obs = order_ref.shape[0]
    cols = prior_ref.shape[1]
    size_y = place_ref[5]
    lane1 = lanes_of((1, cols))
    lane = lanes_of((n_obs, cols))
    sub = sublanes_of((n_obs, cols))

    tile_row = jnp.zeros((1, cols), jnp.int32)
    tile_col = jnp.zeros((n_obs, cols), jnp.int32)
    reach_row = jnp.zeros((1, cols), jnp.int32)
    reach_col = jnp.zeros((n_obs, cols), jnp.int32)
    which = [order_ref[i] for i in range(n_obs)]
    for i, k in enumerate(which):
        tile_row = jnp.where(lane1 == i, owner_ref[k], tile_row)
        tile_col = jnp.where(sub == i, owner_ref[k], tile_col)
        reach_row = jnp.where(lane1 == i, reach_ref[k], reach_row)
        reach_col = jnp.where(sub == i, reach_ref[k], reach_col)
    rx, ry = tile_row // size_y, tile_row % size_y
    cx, cy = tile_col // size_y, tile_col % size_y
    distance = jnp.maximum(jnp.abs(cx - rx), jnp.abs(cy - ry))
    onto = localize(distance, reach_row, taper_ref)
    onto_t = localize(distance, reach_col, taper_ref)
    mine = place_ref[0]
    own = localize(
        jnp.maximum(jnp.abs(mine // size_y - rx), jnp.abs(mine % size_y - ry)), reach_row, taper_ref
    )

    priors = prior_ref[...]
    inside = lane < members
    mean_col = jnp.sum(jnp.where(inside, priors, 0.0), axis=1, keepdims=True) / members
    anomalies = jnp.where(inside, priors - mean_col, 0.0)
    padded = jnp.concatenate([anomalies, jnp.zeros((cols - n_obs, cols), F32)], axis=0)
    unit = jnp.where(lanes_of((members, cols)) == sublanes_of((members, cols)), 1.0, 0.0)
    table = lax.dot_general(
        jnp.concatenate([anomalies, unit], axis=0), padded, NT, precision=HIGHEST, preferred_element_type=F32
    )
    mean = jnp.zeros((1, cols), F32)
    for i in range(n_obs):
        mean = jnp.where(lane1 == i, mean_col[i : i + 1, :], mean)

    scales = jnp.zeros((1, cols), F32)
    increments = []
    for i, k in enumerate(which):
        error = error_ref[k]
        row = table[i : i + 1, :]
        column = table[:, i : i + 1]
        power = row[:, i : i + 1]
        variance = power / (members - 1) + EPS
        root = lax.rsqrt(1.0 + variance * (1.0 / error))
        scaled = 1.0 / ((members - 1) * variance)
        shift = variance * (value_ref[k] - mean[:, i : i + 1]) * (root * root * (1.0 / error))
        shrink = root - 1.0
        weight = scaled * own[:, i : i + 1]
        alpha_row = onto_t[i : i + 1, :] * row * scaled
        later = lane1 > i
        h = jnp.where(later, shrink * alpha_row, 0.0)
        q = jnp.where(later, shrink * (row + h * power), 0.0)
        alpha = jnp.concatenate(
            [onto[:, i : i + 1] * column[:n_obs] * scaled, column[n_obs:] * weight], axis=0
        )
        table = table + column * h + alpha * q
        mean = mean + alpha_row * shift
        now = anomalies[i : i + 1, :]
        increments.append(shift + shrink * now)
        anomalies = anomalies + jnp.where(sub > i, shrink * alpha[:n_obs], 0.0) * now
        scales = jnp.where(lane1 == i, weight, scales)
    left = table[n_obs:, :] * scales
    right = jnp.where(inside, jnp.concatenate(increments, axis=0), 0.0)
    right = jnp.concatenate([right, jnp.zeros((cols - n_obs, cols), F32)], axis=0)
    change = jnp.dot(left, right, precision=HIGHEST, preferred_element_type=F32)
    change = jnp.concatenate([change, jnp.zeros((cols - members, cols), F32)], axis=0)
    change = jnp.transpose(change)[:members, :]
    high = change.astype(BF16).astype(F32)
    low = change - high
    zero = jnp.zeros((members, cols), F32)
    high = jnp.concatenate([high, zero], axis=1)
    low = jnp.concatenate([low, zero], axis=1)
    factor = (high + roll_lanes(high, members) + roll_lanes(low, 2 * members)).astype(BF16)

    block = 4
    for at in range(0, 3 * rows, block):
        x = jnp.concatenate([forecast_ref[at + b] for b in range(block)], axis=1)
        xh = x.astype(BF16)
        xl = (x - xh.astype(F32)).astype(BF16)
        stack = jnp.concatenate([xh, xl, xh, jnp.zeros((2 * cols - 3 * members, block * cols), BF16)], axis=0)
        y = x + jnp.dot(factor, stack, preferred_element_type=F32)
        for b in range(block):
            f, r = divmod(at + b, rows)
            out_ref[pl.ds(f * members * rows + r, members, stride=rows), :] = y[:, b * cols : (b + 1) * cols]
        if (at + block) % rows == 0:
            field = pl.ds(at // rows * members * rows, members * rows)
            pltpu.make_async_copy(out_ref.at[field], result_ref.at[field], sems.at[at // rows]).start()
    for f in range(3):
        field = pl.ds(f * members * rows, members * rows)
        pltpu.make_async_copy(out_ref.at[field], result_ref.at[field], sems.at[f]).wait()


def assimilate(place, order, owner, reach, value, error, taper, priors, states, members, rows):
    cols = priors.shape[1]
    return pl.pallas_call(
        functools.partial(assimilate_kernel, members, rows),
        out_shape=jax.ShapeDtypeStruct((3 * members * rows, cols), F32),
        in_specs=[SSPEC] * 7 + [VSPEC] * 2,
        out_specs=pl.BlockSpec(memory_space=pl.ANY),
        scratch_shapes=[pltpu.VMEM((3 * members * rows, cols), F32), pltpu.SemaphoreType.DMA((3,))],
        compiler_params=pltpu.CompilerParams(vmem_limit_bytes=VMEM_LIMIT),
    )(place, order, owner, reach, value, error, taper, priors, states)


def to_neighbours(axis, lower, upper):
    count = lax.axis_size(axis)
    forward = [(i, i + 1) for i in range(count - 1)]
    backward = [(target, source) for source, target in forward]
    return lax.ppermute(upper, axis, forward), lax.ppermute(lower, axis, backward)


def swap_pairs(x, axis, start):
    pairs = [(i, i + 1) for i in range(start, lax.axis_size(axis) - 1, 2)]
    return lax.ppermute(x, axis, pairs + [(b, a) for a, b in pairs])


def add_over(x, axes):
    for axis in axes:
        count = lax.axis_size(axis)
        if count & (count - 1):
            x = lax.psum(x, axis)
            continue
        span = 1
        while span < count:
            x = x + lax.ppermute(x, axis, [(i, i ^ span) for i in range(count)])
            span *= 2
    return x


def body(status, drag, value, error, taper, order, owner, cell, reach):
    members, rows, cols = status.shape[1:]
    ix, iy = lax.axis_index("gx"), lax.axis_index("gy")
    size_x, size_y = lax.axis_size("gx"), lax.axis_size("gy")
    place = jnp.stack(
        [
            ix * size_y + iy,
            (ix == 0).astype(jnp.int32),
            (ix == size_x - 1).astype(jnp.int32),
            (iy == 0).astype(jnp.int32),
            (iy == size_y - 1).astype(jnp.int32),
            jnp.int32(size_y),
        ]
    ).astype(jnp.int32)
    flat = status.reshape(3 * members * rows, cols)
    lower, upper = bands(flat, members, rows)
    above, below = to_neighbours("gy", lower, upper)
    even, odd = pack(place, flat, drag, members)
    even, odd = swap_pairs(even, "gx", 0), swap_pairs(odd, "gx", 1)
    left, right, margin, even, odd = corner(place, drag, even, odd)
    even, odd = swap_pairs(even, "gy", 0), swap_pairs(odd, "gy", 1)
    inner = interior(place, flat, left, right, drag, margin, members)
    states, priors = forecast(place, order, owner, cell, inner, above, below, even, odd, drag, margin)
    priors = add_over(priors, ("gx", "gy"))
    result = assimilate(place, order, owner, reach, value, error, taper, priors, states, members, rows)
    return result.reshape(status.shape)


def solution(mesh):
    in_specs = (P(None, None, "gy", "gx"), P("gy", "gx"), P(), P(), P(), P(), P(), P(), P())
    out_specs = P(None, None, "gy", "gx")
    return jax.shard_map(body, mesh=mesh, in_specs=in_specs, out_specs=out_specs, check_vma=False)
```

```python
import functools

import jax
import jax.numpy as jnp
from jax import lax
from jax.experimental import pallas as pl
from jax.experimental.pallas import tpu as pltpu
from jax.sharding import PartitionSpec as P

STEPS = 4
MARGIN = 2 * STEPS
EPS = 1e-06
NT = (((1,), (1,)), ((), ()))
HIGHEST = lax.Precision.HIGHEST
F32 = jnp.float32
BF16 = jnp.bfloat16
VMEM_LIMIT = 24 * 1024 * 1024
GROUP = 40

VSPEC = pl.BlockSpec(memory_space=pltpu.VMEM)
SSPEC = pl.BlockSpec(memory_space=pltpu.SMEM)


def lanes_of(shape):
    return lax.broadcasted_iota(jnp.int32, shape, len(shape) - 1)


def sublanes_of(shape):
    return lax.broadcasted_iota(jnp.int32, shape, len(shape) - 2)


def roll_lanes(x, shift):
    size = x.shape[-1]
    shift = shift % size
    return x if shift == 0 else pltpu.roll(x, shift, x.ndim - 1)


def band_kernel(members, rows, x_hbm, lower_hbm, upper_hbm, x_ref, lower_ref, upper_ref, sems):
    def arrive(f):
        field = pl.ds(f * members * rows, members * rows)
        return pltpu.make_async_copy(x_hbm.at[field], x_ref.at[field], sems.at[0, f])

    def leave(f, side):
        source, target = ((lower_ref, lower_hbm), (upper_ref, upper_hbm))[side]
        here = pl.ds(f * (MARGIN - 1), MARGIN if f == 2 else MARGIN - 1)
        return pltpu.make_async_copy(source.at[here], target.at[here], sems.at[1 + side, f])

    for f in range(3):
        arrive(f).start()
    for f in range(3):
        arrive(f).wait()
        depth = MARGIN if f == 2 else MARGIN - 1
        for d in range(depth):
            at = f * members * rows + d
            lower_ref[f * (MARGIN - 1) + d] = x_ref[pl.ds(at, members, stride=rows), :]
            upper_ref[f * (MARGIN - 1) + d] = x_ref[pl.ds(at + rows - depth, members, stride=rows), :]
        leave(f, 0).start()
        leave(f, 1).start()
    for f in range(3):
        leave(f, 0).wait()
        leave(f, 1).wait()


def bands(x, members, rows):
    cols = x.shape[1]
    shape = (3 * MARGIN - 2, members, cols)
    return pl.pallas_call(
        functools.partial(band_kernel, members, rows),
        out_shape=(jax.ShapeDtypeStruct(shape, F32),) * 2,
        in_specs=[pl.BlockSpec(memory_space=pltpu.HBM)],
        out_specs=(pl.BlockSpec(memory_space=pl.ANY),) * 2,
        scratch_shapes=[pltpu.VMEM(x.shape, F32)] + [pltpu.VMEM(shape, F32)] * 2 + [pltpu.SemaphoreType.DMA((3, 3))],
        compiler_params=pltpu.CompilerParams(vmem_limit_bytes=60 * 1024 * 1024),
        cost_estimate=pl.CostEstimate(flops=1_000_000, bytes_accessed=4_000_000, transcendentals=0),
    )(x)


def pack_kernel(members, rows, place_ref, x_ref, drag_ref, even_ref, odd_ref):
    cols = x_ref.shape[1]
    lane = lanes_of((8, cols))
    odd_x = place_ref[0] // place_ref[5] % 2 == 1

    def group(g, carry):
        for f in range(3):
            left = jnp.zeros((8, cols), F32)
            right = jnp.zeros((8, cols), F32)
            for r in range(rows):
                row = x_ref[pl.ds((f * members + g * 8) * rows + r, 8, stride=rows), :]
                slot = lane // MARGIN
                left = jnp.where(slot == rows - 1 - r, roll_lanes(row, MARGIN * (rows - 1 - r)), left)
                right = jnp.where(slot == r, roll_lanes(row, MARGIN * (r + 1)), right)
            at = pl.ds(pl.multiple_of(f * members + g * 8, 8), 8)
            even_ref[at, :] = jnp.where(odd_x, left, right)
            odd_ref[at, :] = jnp.where(odd_x, right, left)
        return carry

    lax.fori_loop(0, members // 8, group, 0)
    even_ref[3 * members :, :] = drag_ref[...]
    odd_ref[3 * members :, :] = drag_ref[...]


def pack(place, x, drag, members):
    rows, cols = drag.shape
    message = jax.ShapeDtypeStruct((3 * members + rows, cols), F32)
    return pl.pallas_call(
        functools.partial(pack_kernel, members, rows),
        out_shape=(message, message),
        in_specs=[SSPEC, VSPEC, VSPEC],
        out_specs=(VSPEC,) * 2,
        compiler_params=pltpu.CompilerParams(vmem_limit_bytes=VMEM_LIMIT),
        cost_estimate=pl.CostEstimate(flops=1_000_000, bytes_accessed=4_000_000, transcendentals=0),
    )(place, x, drag)


def corner_kernel(place_ref, drag_ref, even_ref, odd_ref, left_ref, right_ref, margin_ref, even_out, odd_out):
    count, cols = left_ref.shape
    rows = drag_ref.shape[0]
    half = cols // 2
    odd_y = place_ref[0] % place_ref[5] % 2 == 1
    odd_x = place_ref[0] // place_ref[5] % 2 == 1
    even, odd = even_ref[...], odd_ref[...]
    left, right = jnp.where(odd_x, even, odd), jnp.where(odd_x, odd, even)
    margin = jnp.where(lanes_of((rows, cols)) < half, right[count:], left[count:])
    margin_ref[...] = margin
    left, right = left[:count], right[:count]
    left_ref[...] = left
    right_ref[...] = right
    lane = lanes_of((count, cols))
    slot, column = lane % half // MARGIN, lane % MARGIN
    mine = column > jnp.where(lane < half, slot, MARGIN - 1 - slot)
    both = jnp.where(mine, left, roll_lanes(right, half))
    count = count // 2
    head, tail = both[:count], both[count:]
    first_half = lanes_of((count, cols)) < half
    lower = jnp.where(first_half, head, roll_lanes(tail, half))
    upper = jnp.where(first_half, roll_lanes(head, half), tail)
    even_out[:count, :] = jnp.where(odd_y, lower, upper)
    odd_out[:count, :] = jnp.where(odd_y, upper, lower)
    drag = drag_ref[...]
    for at, part in ((count, drag), (count + MARGIN, margin)):
        lower, upper = part[:MARGIN], part[rows - MARGIN :]
        even_out[at : at + MARGIN, :] = jnp.where(odd_y, lower, upper)
        odd_out[at : at + MARGIN, :] = jnp.where(odd_y, upper, lower)


def corner(place, drag, even, odd):
    rows, cols = drag.shape
    count = even.shape[0] - rows
    edge = jax.ShapeDtypeStruct((count, cols), F32)
    message = jax.ShapeDtypeStruct((count // 2 + 2 * MARGIN, cols), F32)
    return pl.pallas_call(
        corner_kernel,
        out_shape=(edge, edge, jax.ShapeDtypeStruct((rows, cols), F32), message, message),
        in_specs=[SSPEC] + [VSPEC] * 3,
        out_specs=(VSPEC,) * 5,
        compiler_params=pltpu.CompilerParams(vmem_limit_bytes=VMEM_LIMIT),
    )(place, drag, even, odd)


def grid_factor(place_ref, shape, rows, cols):
    row, col = sublanes_of(shape), lanes_of(shape)
    wide = 2 * cols
    low, high = jnp.where(place_ref[3] == 1, MARGIN, 0), jnp.where(place_ref[4] == 1, MARGIN + rows, rows + 2 * MARGIN)
    first, last = jnp.where(place_ref[1] == 1, wide, wide - MARGIN), jnp.where(place_ref[2] == 1, cols, cols + MARGIN)
    ok = (row >= low) & (row < high) & ((col < last) | (col >= first))
    return jnp.where(ok, 1.0, 0.0)


def wide_row(lane, main, left, left_at, right, right_at):
    cols = main.shape[1]
    halo = jnp.where(lane >= cols - MARGIN, roll_lanes(left, cols - MARGIN - left_at), 0.0)
    halo = jnp.where(lane < MARGIN, roll_lanes(right, -right_at), halo)
    return jnp.concatenate([main, halo], axis=1)


def shift_matrix(wide):
    source, target = sublanes_of((wide, wide)), lanes_of((wide, wide))
    after, before = source == (target + 1) % wide, target == (source + 1) % wide
    return jnp.where(after, 1.0, jnp.where(before, -1.0, 0.0)).astype(BF16)


def tall(x):
    return jnp.concatenate([x] * (GROUP // 8), axis=0)


def column_slope(x, shift):
    rows, group, wide = x.shape
    x = x.reshape(rows * group, wide)
    top = x.astype(BF16)
    rest = (x - top.astype(F32)).astype(BF16)
    slope = jnp.dot(top, shift, preferred_element_type=F32) + jnp.dot(rest, shift, preferred_element_type=F32)
    return slope.reshape(rows, group, wide)


def interior_kernel(members, rows, place_ref, x_ref, left_ref, right_ref, drag_ref, margin_ref, state, keep, slope):
    cols = x_ref.shape[1]
    wide = 2 * cols
    lane = lanes_of((8, cols))
    factor = -0.2 * grid_factor(place_ref, (rows + 2 * MARGIN, wide), rows, cols)
    shift = shift_matrix(wide)
    kept = 1.0 - jnp.concatenate([drag_ref[...], margin_ref[...]], axis=1)
    for r in range(rows):
        keep[r] = jnp.broadcast_to(kept[r : r + 1, :], (8, wide))
        slope[r] = jnp.broadcast_to(factor[MARGIN + r : MARGIN + r + 1, :], (8, wide))

    def first(g, carry):
        here = pl.ds(pl.multiple_of(g * 8, 8), 8)
        for f in range(3):
            at = pl.ds(pl.multiple_of(f * members + g * 8, 8), 8)
            left, right = left_ref[at, :], right_ref[at, :]
            for r in range(rows):
                main = x_ref[pl.ds((f * members + g * 8) * rows + r, 8, stride=rows), :]
                state[f, r, here, :] = wide_row(lane, main, left, MARGIN * r, right, MARGIN * (rows - 1 - r))
        return carry

    lax.fori_loop(0, members // 8, first, 0)

    groups = [pl.ds(m, GROUP) for m in range(0, members, GROUP)]
    for step in range(STEPS):
        low, high = 1 + 2 * step, rows - 1 - 2 * step
        if low >= high:
            break
        for here in groups:
            d = column_slope(state[1, low:high, here, :], shift)
            for r in range(low, high):
                div = d[r - low] + (state[2, r + 1, here, :] - state[2, r - 1, here, :])
                state[0, r, here, :] = state[0, r, here, :] + tall(slope[r]) * div
        low, high = low + 1, high - 1
        if low >= high:
            break
        for here in groups:
            d = column_slope(state[0, low:high, here, :], shift)
            for r in range(low, high):
                u, v = state[1, r, here, :], state[2, r, here, :]
                k, c = tall(keep[r]), tall(slope[r])
                state[1, r, here, :] = k * u + c * d[r - low] + 0.1 * v
                state[2, r, here, :] = k * v + c * (state[0, r + 1, here, :] - state[0, r - 1, here, :]) - 0.1 * u


def interior(place, x, left, right, drag, margin, members):
    rows, cols = drag.shape
    return pl.pallas_call(
        functools.partial(interior_kernel, members, rows),
        out_shape=jax.ShapeDtypeStruct((3, rows, members, 2 * cols), F32),
        in_specs=[SSPEC] + [VSPEC] * 5,
        out_specs=VSPEC,
        scratch_shapes=[pltpu.VMEM((rows, 8, 2 * cols), F32)] * 2,
        compiler_params=pltpu.CompilerParams(vmem_limit_bytes=VMEM_LIMIT),
        cost_estimate=pl.CostEstimate(flops=30_000_000, bytes_accessed=10_000_000, transcendentals=0),
    )(place, x, left, right, drag, margin)


def forecast_kernel(
    members, rows,
    place_ref, order_ref, owner_ref, cell_ref,
    inner_ref, above_ref, below_ref, ceven_ref, codd_ref, drag_ref, margin_ref,
    out_ref, prior_ref,
    state, keep, slope,
):
    cols = above_ref.shape[2]
    wide = 2 * cols
    total = rows + 2 * MARGIN
    half = cols // 2
    lane = lanes_of((GROUP, cols))
    factor = -0.2 * grid_factor(place_ref, (total, wide), rows, cols)
    odd_y = place_ref[0] % place_ref[5] % 2 == 1
    shift = shift_matrix(wide)
    count = 3 * members // 2
    parts = []
    for here, own in ((count, drag_ref), (count + MARGIN, margin_ref)):
        even, odd = ceven_ref[here : here + MARGIN, :], codd_ref[here : here + MARGIN, :]
        above, below = jnp.where(odd_y, even, odd), jnp.where(odd_y, odd, even)
        parts.append(jnp.concatenate([above, own[...], below], axis=0))
    kept = 1.0 - jnp.concatenate(parts, axis=1)
    for r in range(total):
        keep[r] = jnp.broadcast_to(kept[r : r + 1, :], (8, wide))
        slope[r] = jnp.broadcast_to(factor[r : r + 1, :], (8, wide))

    groups = range(members // GROUP)
    for g in groups:
        here = pl.ds(g * GROUP, GROUP)
        for f in range(3):
            at = f * members + g * GROUP
            base = half if at >= count else 0
            at = pl.ds(at % count, GROUP)
            ceven, codd = ceven_ref[at, :], codd_ref[at, :]
            cab, cbe = jnp.where(odd_y, ceven, codd), jnp.where(odd_y, codd, ceven)
            depth = MARGIN if f == 2 else MARGIN - 1
            for d in range(depth):
                r = MARGIN - depth + d
                main = above_ref[f * (MARGIN - 1) + d, here, :]
                state[g, f, r] = wide_row(lane, main, cab, base + MARGIN * r, cab, base + MARGIN * (MARGIN - 1 - r))
                main = below_ref[f * (MARGIN - 1) + d, here, :]
                state[g, f, MARGIN + rows + d] = wide_row(
                    lane, main, cbe, base + MARGIN * d, cbe, base + MARGIN * (MARGIN - 1 - d)
                )
            for r in range(rows):
                state[g, f, MARGIN + r] = inner_ref[f, r, here, :]

    def heights(g, spans):
        for low, high in spans:
            d = column_slope(state[g, 1, low:high], shift)
            for r in range(low, high):
                div = d[r - low] + (state[g, 2, r + 1] - state[g, 2, r - 1])
                state[g, 0, r] = state[g, 0, r] + tall(slope[r]) * div

    def flows(g, spans, final):
        here = pl.ds(g * GROUP, GROUP)
        for low, high in spans:
            d = column_slope(state[g, 0, low:high], shift)
            for r in range(low, high):
                u, v = state[g, 1, r], state[g, 2, r]
                k, c = tall(keep[r]), tall(slope[r])
                u, v = (
                    k * u + c * d[r - low] + 0.1 * v,
                    k * v + c * (state[g, 0, r + 1] - state[g, 0, r - 1]) - 0.1 * u,
                )
                if final:
                    for f, value in enumerate((state[g, 0, r], u, v)):
                        out_ref[f * rows + r - MARGIN, here, :] = value[:, 0:cols]
                else:
                    state[g, 1, r] = u
                    state[g, 2, r] = v

    for step in range(STEPS):
        first, last = MARGIN - MARGIN + 1 + 2 * step, MARGIN + rows + MARGIN - 1 - 2 * step
        done, still = MARGIN + 1 + 2 * step, MARGIN + rows - 1 - 2 * step
        for g in groups:
            heights(g, ((first, done), (still, last)))
        for g in groups:
            flows(g, ((first + 1, done + 1), (still - 1, last - 1)), step == STEPS - 1)
    prior_ref[...] = jnp.zeros_like(prior_ref)
    eight = lanes_of((8, cols))
    for i in range(order_ref.shape[0]):
        which = order_ref[i]

        @pl.when(owner_ref[which] == place_ref[0])
        def _():
            cell = cell_ref[which]
            one = jnp.where(eight == cell % cols, 1.0, 0.0)
            prior_ref[i : i + 1, 0:members] = lax.dot_general(
                one, out_ref[cell // cols], NT, precision=HIGHEST, preferred_element_type=F32
            )[0:1]


def forecast(place, order, owner, cell, inner, *arrays):
    _, rows, members, wide = inner.shape
    cols = wide // 2
    total = rows + 2 * MARGIN
    return pl.pallas_call(
        functools.partial(forecast_kernel, members, rows),
        out_shape=(
            jax.ShapeDtypeStruct((3 * rows, members, cols), F32),
            jax.ShapeDtypeStruct((order.shape[0], cols), F32),
        ),
        in_specs=[SSPEC] * 4 + [VSPEC] * (1 + len(arrays)),
        out_specs=(VSPEC, VSPEC),
        scratch_shapes=[pltpu.VMEM((members // GROUP, 3, total, GROUP, wide), F32)] + [pltpu.VMEM((total, 8, wide), F32)] * 2,
        compiler_params=pltpu.CompilerParams(vmem_limit_bytes=VMEM_LIMIT),
        cost_estimate=pl.CostEstimate(flops=60_000_000, bytes_accessed=30_000_000, transcendentals=0),
    )(place, order, owner, cell, inner, *arrays)


def localize(distance, reach, taper_ref):
    picked = jnp.zeros(distance.shape, F32)
    levels = taper_ref.shape[0]
    capped = jnp.minimum(distance, levels - 1)
    for d in range(levels):
        picked = jnp.where(capped == d, taper_ref[d], picked)
    return jnp.where(distance <= reach, picked, 0.0)


def assimilate_kernel(
    members, rows,
    place_ref, order_ref, owner_ref, reach_ref, value_ref, error_ref, taper_ref,
    prior_ref, forecast_ref,
    result_ref,
    out_ref, sems,
):
    n_obs = order_ref.shape[0]
    cols = prior_ref.shape[1]
    size_y = place_ref[5]
    lane1 = lanes_of((1, cols))
    lane = lanes_of((n_obs, cols))
    sub = sublanes_of((n_obs, cols))

    tile_row = jnp.zeros((1, cols), jnp.int32)
    tile_col = jnp.zeros((n_obs, cols), jnp.int32)
    reach_row = jnp.zeros((1, cols), jnp.int32)
    reach_col = jnp.zeros((n_obs, cols), jnp.int32)
    which = [order_ref[i] for i in range(n_obs)]
    for i, k in enumerate(which):
        tile_row = jnp.where(lane1 == i, owner_ref[k], tile_row)
        tile_col = jnp.where(sub == i, owner_ref[k], tile_col)
        reach_row = jnp.where(lane1 == i, reach_ref[k], reach_row)
        reach_col = jnp.where(sub == i, reach_ref[k], reach_col)
    rx, ry = tile_row // size_y, tile_row % size_y
    cx, cy = tile_col // size_y, tile_col % size_y
    distance = jnp.maximum(jnp.abs(cx - rx), jnp.abs(cy - ry))
    onto = localize(distance, reach_row, taper_ref)
    onto_t = localize(distance, reach_col, taper_ref)
    mine = place_ref[0]
    own = localize(
        jnp.maximum(jnp.abs(mine // size_y - rx), jnp.abs(mine % size_y - ry)), reach_row, taper_ref
    )

    priors = prior_ref[...]
    inside = lane < members
    mean_col = jnp.sum(jnp.where(inside, priors, 0.0), axis=1, keepdims=True) / members
    anomalies = jnp.where(inside, priors - mean_col, 0.0)
    padded = jnp.concatenate([anomalies, jnp.zeros((cols - n_obs, cols), F32)], axis=0)
    table = lax.dot_general(anomalies, padded, NT, precision=HIGHEST, preferred_element_type=F32)
    table = jnp.concatenate([table, jnp.transpose(padded)[:members]], axis=0)
    mean = jnp.zeros((1, cols), F32)
    for i in range(n_obs):
        mean = jnp.where(lane1 == i, mean_col[i : i + 1, :], mean)

    scales = jnp.zeros((1, cols), F32)
    increments = []
    power = jnp.broadcast_to(table[0:1, 0:1], (1, cols))
    for i, k in enumerate(which):
        error = error_ref[k]
        row = table[i : i + 1, :]
        column = jnp.broadcast_to(table[:, i : i + 1], table.shape)
        variance = power / (members - 1) + EPS
        root = lax.rsqrt(1.0 + variance * (1.0 / error))
        scaled = 1.0 / ((members - 1) * variance)
        shift = variance * (value_ref[k] - jnp.broadcast_to(mean[:, i : i + 1], row.shape)) * (root * root * (1.0 / error))
        shrink = root - 1.0
        weight = scaled * jnp.broadcast_to(own[:, i : i + 1], row.shape)
        alpha_row = onto_t[i : i + 1, :] * row * scaled
        later = lane1 > i
        h = jnp.where(later, shrink * alpha_row, 0.0)
        q = jnp.where(later, shrink * (row + h * power), 0.0)
        alpha = jnp.concatenate(
            [jnp.broadcast_to(onto[:, i : i + 1], onto.shape) * column[:n_obs] * scaled, column[n_obs:] * weight], axis=0
        )
        if i + 1 < n_obs:
            beside, ahead, reach_on = (
                jnp.broadcast_to(x[:, i + 1 : i + 2], row.shape)
                for x in (row, table[i + 1 : i + 2, :], onto_t[i : i + 1, :])
            )
            step = reach_on * beside * scaled
            power = ahead + beside * (shrink * step) + step * (shrink * (beside + shrink * step * power))
        table = table + column * h + alpha * q
        mean = mean + alpha_row * shift
        now = anomalies[i : i + 1, :]
        increments.append(shift + shrink * now)
        anomalies = anomalies + jnp.where(sub > i, shrink * alpha[:n_obs], 0.0) * now
        scales = jnp.where(lane1 == i, weight, scales)
    left = table[n_obs:, :] * scales
    right = jnp.where(inside, jnp.concatenate(increments, axis=0), 0.0)
    right = jnp.concatenate([right, jnp.zeros((cols - n_obs, cols), F32)], axis=0)
    change = jnp.dot(left, right, precision=HIGHEST, preferred_element_type=F32)
    change = jnp.concatenate([change, jnp.zeros((cols - members, cols), F32)], axis=0)
    change = jnp.transpose(change)[:members, :]
    high = change.astype(BF16).astype(F32)
    low = change - high
    zero = jnp.zeros((members, cols), F32)
    high = jnp.concatenate([high, zero], axis=1)
    low = jnp.concatenate([low, zero], axis=1)
    factor = (high + roll_lanes(high, members) + roll_lanes(low, 2 * members)).astype(BF16)

    block = 4
    for at in range(0, 3 * rows, block):
        x = jnp.concatenate([forecast_ref[at + b] for b in range(block)], axis=1)
        xh = x.astype(BF16)
        xl = (x - xh.astype(F32)).astype(BF16)
        stack = jnp.concatenate([xh, xl, xh, jnp.zeros((2 * cols - 3 * members, block * cols), BF16)], axis=0)
        y = x + jnp.dot(factor, stack, preferred_element_type=F32)
        for b in range(block):
            f, r = divmod(at + b, rows)
            out_ref[pl.ds(f * members * rows + r, members, stride=rows), :] = y[:, b * cols : (b + 1) * cols]
        if (at + block) % rows == 0:
            field = pl.ds(at // rows * members * rows, members * rows)
            pltpu.make_async_copy(out_ref.at[field], result_ref.at[field], sems.at[at // rows]).start()
    for f in range(3):
        field = pl.ds(f * members * rows, members * rows)
        pltpu.make_async_copy(out_ref.at[field], result_ref.at[field], sems.at[f]).wait()


def assimilate(place, order, owner, reach, value, error, taper, priors, states, members, rows):
    cols = priors.shape[1]
    return pl.pallas_call(
        functools.partial(assimilate_kernel, members, rows),
        out_shape=jax.ShapeDtypeStruct((3 * members * rows, cols), F32),
        in_specs=[SSPEC] * 7 + [VSPEC] * 2,
        out_specs=pl.BlockSpec(memory_space=pl.ANY),
        scratch_shapes=[pltpu.VMEM((3 * members * rows, cols), F32), pltpu.SemaphoreType.DMA((3,))],
        compiler_params=pltpu.CompilerParams(vmem_limit_bytes=VMEM_LIMIT),
    )(place, order, owner, reach, value, error, taper, priors, states)


def to_neighbours(axis, lower, upper):
    count = lax.axis_size(axis)
    forward = [(i, i + 1) for i in range(count - 1)]
    backward = [(target, source) for source, target in forward]
    return lax.ppermute(upper, axis, forward), lax.ppermute(lower, axis, backward)


def swap_pairs(x, axis, start):
    pairs = [(i, i + 1) for i in range(start, lax.axis_size(axis) - 1, 2)]
    return lax.ppermute(x, axis, pairs + [(b, a) for a, b in pairs])


def add_over(x, axes):
    for axis in axes:
        count = lax.axis_size(axis)
        if count & (count - 1):
            x = lax.psum(x, axis)
            continue
        span = 1
        while span < count:
            x = x + lax.ppermute(x, axis, [(i, i ^ span) for i in range(count)])
            span *= 2
    return x


def body(status, drag, value, error, taper, order, owner, cell, reach):
    members, rows, cols = status.shape[1:]
    ix, iy = lax.axis_index("gx"), lax.axis_index("gy")
    size_x, size_y = lax.axis_size("gx"), lax.axis_size("gy")
    place = jnp.stack(
        [
            ix * size_y + iy,
            (ix == 0).astype(jnp.int32),
            (ix == size_x - 1).astype(jnp.int32),
            (iy == 0).astype(jnp.int32),
            (iy == size_y - 1).astype(jnp.int32),
            jnp.int32(size_y),
        ]
    ).astype(jnp.int32)
    flat = status.reshape(3 * members * rows, cols)
    lower, upper = bands(flat, members, rows)
    above, below = to_neighbours("gy", lower, upper)
    even, odd = pack(place, flat, drag, members)
    even, odd = swap_pairs(even, "gx", 0), swap_pairs(odd, "gx", 1)
    left, right, margin, even, odd = corner(place, drag, even, odd)
    even, odd = swap_pairs(even, "gy", 0), swap_pairs(odd, "gy", 1)
    inner = interior(place, flat, left, right, drag, margin, members)
    states, priors = forecast(place, order, owner, cell, inner, above, below, even, odd, drag, margin)
    priors = add_over(priors, ("gx", "gy"))
    result = assimilate(place, order, owner, reach, value, error, taper, priors, states, members, rows)
    return result.reshape(status.shape)


def solution(mesh):
    in_specs = (P(None, None, "gy", "gx"), P("gy", "gx"), P(), P(), P(), P(), P(), P(), P())
    out_specs = P(None, None, "gy", "gx")
    return jax.shard_map(body, mesh=mesh, in_specs=in_specs, out_specs=out_specs, check_vma=False)
```

```python
import functools

import jax
import jax.numpy as jnp
from jax import lax
from jax.experimental import pallas as pl
from jax.experimental.pallas import tpu as pltpu
from jax.sharding import PartitionSpec as P

STEPS = 4
MARGIN = 2 * STEPS
EPS = 1e-06
NT = (((1,), (1,)), ((), ()))
HIGHEST = lax.Precision.HIGHEST
F32 = jnp.float32
BF16 = jnp.bfloat16
VMEM_LIMIT = 24 * 1024 * 1024
GROUP = 40

VSPEC = pl.BlockSpec(memory_space=pltpu.VMEM)
SSPEC = pl.BlockSpec(memory_space=pltpu.SMEM)


def lanes_of(shape):
    return lax.broadcasted_iota(jnp.int32, shape, len(shape) - 1)


def sublanes_of(shape):
    return lax.broadcasted_iota(jnp.int32, shape, len(shape) - 2)


def roll_lanes(x, shift):
    size = x.shape[-1]
    shift = shift % size
    return x if shift == 0 else pltpu.roll(x, shift, x.ndim - 1)


def band_kernel(members, rows, x_hbm, lower_hbm, upper_hbm, x_ref, lower_ref, upper_ref, sems):
    def arrive(f):
        field = pl.ds(f * members * rows, members * rows)
        return pltpu.make_async_copy(x_hbm.at[field], x_ref.at[field], sems.at[0, f])

    def leave(f, side):
        source, target = ((lower_ref, lower_hbm), (upper_ref, upper_hbm))[side]
        here = pl.ds(f * (MARGIN - 1), MARGIN if f == 2 else MARGIN - 1)
        return pltpu.make_async_copy(source.at[here], target.at[here], sems.at[1 + side, f])

    for f in range(3):
        arrive(f).start()
    for f in range(3):
        arrive(f).wait()
        depth = MARGIN if f == 2 else MARGIN - 1
        for d in range(depth):
            at = f * members * rows + d
            lower_ref[f * (MARGIN - 1) + d] = x_ref[pl.ds(at, members, stride=rows), :]
            upper_ref[f * (MARGIN - 1) + d] = x_ref[pl.ds(at + rows - depth, members, stride=rows), :]
        leave(f, 0).start()
        leave(f, 1).start()
    for f in range(3):
        leave(f, 0).wait()
        leave(f, 1).wait()


def bands(x, members, rows):
    cols = x.shape[1]
    shape = (3 * MARGIN - 2, members, cols)
    return pl.pallas_call(
        functools.partial(band_kernel, members, rows),
        out_shape=(jax.ShapeDtypeStruct(shape, F32),) * 2,
        in_specs=[pl.BlockSpec(memory_space=pltpu.HBM)],
        out_specs=(pl.BlockSpec(memory_space=pl.ANY),) * 2,
        scratch_shapes=[pltpu.VMEM(x.shape, F32)] + [pltpu.VMEM(shape, F32)] * 2 + [pltpu.SemaphoreType.DMA((3, 3))],
        compiler_params=pltpu.CompilerParams(vmem_limit_bytes=60 * 1024 * 1024),
        cost_estimate=pl.CostEstimate(flops=1_000_000, bytes_accessed=4_000_000, transcendentals=0),
    )(x)


def pack_kernel(members, rows, place_ref, x_ref, drag_ref, even_ref, odd_ref):
    cols = x_ref.shape[1]
    lane = lanes_of((8, cols))
    slot = lane // MARGIN
    odd_x = place_ref[0] // place_ref[5] % 2 == 1

    def group(g, carry):
        for f in range(3):
            row = [x_ref[pl.ds((f * members + g * 8) * rows + r, 8, stride=rows), :] for r in range(rows)]
            left, right = row[rows - 1], roll_lanes(row[rows - 1], MARGIN * rows)
            for r in range(rows - 1):
                both = roll_lanes(jnp.where(lane < cols // 2, row[rows - 2 - r], row[r]), MARGIN * (r + 1))
                left = jnp.where(slot == r + 1, both, left)
                right = jnp.where(slot == r, both, right)
            at = pl.ds(pl.multiple_of(f * members + g * 8, 8), 8)
            even_ref[at, :] = jnp.where(odd_x, left, right)
            odd_ref[at, :] = jnp.where(odd_x, right, left)
        return carry

    lax.fori_loop(0, members // 8, group, 0)
    even_ref[3 * members :, :] = drag_ref[...]
    odd_ref[3 * members :, :] = drag_ref[...]


def pack(place, x, drag, members):
    rows, cols = drag.shape
    message = jax.ShapeDtypeStruct((3 * members + rows, cols), F32)
    return pl.pallas_call(
        functools.partial(pack_kernel, members, rows),
        out_shape=(message, message),
        in_specs=[SSPEC, VSPEC, VSPEC],
        out_specs=(VSPEC,) * 2,
        compiler_params=pltpu.CompilerParams(vmem_limit_bytes=VMEM_LIMIT),
        cost_estimate=pl.CostEstimate(flops=1_000_000, bytes_accessed=4_000_000, transcendentals=0),
    )(place, x, drag)


def corner_kernel(place_ref, drag_ref, even_ref, odd_ref, left_ref, right_ref, margin_ref, even_out, odd_out):
    count, cols = left_ref.shape
    rows = drag_ref.shape[0]
    half = cols // 2
    odd_y = place_ref[0] % place_ref[5] % 2 == 1
    odd_x = place_ref[0] // place_ref[5] % 2 == 1
    even, odd = even_ref[...], odd_ref[...]
    left, right = jnp.where(odd_x, even, odd), jnp.where(odd_x, odd, even)
    margin = jnp.where(lanes_of((rows, cols)) < half, right[count:], left[count:])
    margin_ref[...] = margin
    left, right = left[:count], right[:count]
    left_ref[...] = left
    right_ref[...] = right
    lane = lanes_of((count, cols))
    slot, column = lane % half // MARGIN, lane % MARGIN
    mine = column > jnp.where(lane < half, slot, MARGIN - 1 - slot)
    both = jnp.where(mine, left, roll_lanes(right, half))
    count = count // 2
    head, tail = both[:count], both[count:]
    first_half = lanes_of((count, cols)) < half
    lower = jnp.where(first_half, head, roll_lanes(tail, half))
    upper = jnp.where(first_half, roll_lanes(head, half), tail)
    even_out[:count, :] = jnp.where(odd_y, lower, upper)
    odd_out[:count, :] = jnp.where(odd_y, upper, lower)
    drag = drag_ref[...]
    for at, part in ((count, drag), (count + MARGIN, margin)):
        lower, upper = part[:MARGIN], part[rows - MARGIN :]
        even_out[at : at + MARGIN, :] = jnp.where(odd_y, lower, upper)
        odd_out[at : at + MARGIN, :] = jnp.where(odd_y, upper, lower)


def corner(place, drag, even, odd):
    rows, cols = drag.shape
    count = even.shape[0] - rows
    edge = jax.ShapeDtypeStruct((count, cols), F32)
    message = jax.ShapeDtypeStruct((count // 2 + 2 * MARGIN, cols), F32)
    return pl.pallas_call(
        corner_kernel,
        out_shape=(edge, edge, jax.ShapeDtypeStruct((rows, cols), F32), message, message),
        in_specs=[SSPEC] + [VSPEC] * 3,
        out_specs=(VSPEC,) * 5,
        compiler_params=pltpu.CompilerParams(vmem_limit_bytes=VMEM_LIMIT),
    )(place, drag, even, odd)


def grid_factor(place_ref, shape, rows, cols):
    row, col = sublanes_of(shape), lanes_of(shape)
    wide = 2 * cols
    low, high = jnp.where(place_ref[3] == 1, MARGIN, 0), jnp.where(place_ref[4] == 1, MARGIN + rows, rows + 2 * MARGIN)
    first, last = jnp.where(place_ref[1] == 1, wide, wide - MARGIN), jnp.where(place_ref[2] == 1, cols, cols + MARGIN)
    ok = (row >= low) & (row < high) & ((col < last) | (col >= first))
    return jnp.where(ok, 1.0, 0.0)


def wide_row(lane, main, left, left_at, right, right_at):
    cols = main.shape[1]
    halo = jnp.where(lane >= cols - MARGIN, roll_lanes(left, cols - MARGIN - left_at), 0.0)
    halo = jnp.where(lane < MARGIN, roll_lanes(right, -right_at), halo)
    return jnp.concatenate([main, halo], axis=1)


def shift_matrix(wide):
    source, target = sublanes_of((wide, wide)), lanes_of((wide, wide))
    after, before = source == (target + 1) % wide, target == (source + 1) % wide
    return jnp.where(after, 1.0, jnp.where(before, -1.0, 0.0)).astype(BF16)


def tall(x):
    return jnp.concatenate([x] * (GROUP // 8), axis=0)


def column_slope(x, shift):
    rows, group, wide = x.shape
    x = x.reshape(rows * group, wide)
    top = x.astype(BF16)
    rest = (x - top.astype(F32)).astype(BF16)
    slope = jnp.dot(top, shift, preferred_element_type=F32) + jnp.dot(rest, shift, preferred_element_type=F32)
    return slope.reshape(rows, group, wide)


def interior_kernel(members, rows, place_ref, x_ref, left_ref, right_ref, drag_ref, margin_ref, state, keep, slope):
    cols = x_ref.shape[1]
    wide = 2 * cols
    lane = lanes_of((8, cols))
    factor = -0.2 * grid_factor(place_ref, (rows + 2 * MARGIN, wide), rows, cols)
    shift = shift_matrix(wide)
    kept = 1.0 - jnp.concatenate([drag_ref[...], margin_ref[...]], axis=1)
    for r in range(rows):
        keep[r] = jnp.broadcast_to(kept[r : r + 1, :], (8, wide))
        slope[r] = jnp.broadcast_to(factor[MARGIN + r : MARGIN + r + 1, :], (8, wide))

    def first(g, carry):
        here = pl.ds(pl.multiple_of(g * 8, 8), 8)
        for f in range(3):
            at = pl.ds(pl.multiple_of(f * members + g * 8, 8), 8)
            left, right = left_ref[at, :], right_ref[at, :]
            for r in range(rows):
                main = x_ref[pl.ds((f * members + g * 8) * rows + r, 8, stride=rows), :]
                state[f, r, here, :] = wide_row(lane, main, left, MARGIN * r, right, MARGIN * (rows - 1 - r))
        return carry

    lax.fori_loop(0, members // 8, first, 0)

    groups = [pl.ds(m, GROUP) for m in range(0, members, GROUP)]
    for step in range(STEPS):
        low, high = 1 + 2 * step, rows - 1 - 2 * step
        if low >= high:
            break
        for here in groups:
            d = column_slope(state[1, low:high, here, :], shift)
            for r in range(low, high):
                div = d[r - low] + (state[2, r + 1, here, :] - state[2, r - 1, here, :])
                state[0, r, here, :] = state[0, r, here, :] + tall(slope[r]) * div
        low, high = low + 1, high - 1
        if low >= high:
            break
        for here in groups:
            d = column_slope(state[0, low:high, here, :], shift)
            for r in range(low, high):
                u, v = state[1, r, here, :], state[2, r, here, :]
                k, c = tall(keep[r]), tall(slope[r])
                state[1, r, here, :] = k * u + c * d[r - low] + 0.1 * v
                state[2, r, here, :] = k * v + c * (state[0, r + 1, here, :] - state[0, r - 1, here, :]) - 0.1 * u


def interior(place, x, left, right, drag, margin, members):
    rows, cols = drag.shape
    return pl.pallas_call(
        functools.partial(interior_kernel, members, rows),
        out_shape=jax.ShapeDtypeStruct((3, rows, members, 2 * cols), F32),
        in_specs=[SSPEC] + [VSPEC] * 5,
        out_specs=VSPEC,
        scratch_shapes=[pltpu.VMEM((rows, 8, 2 * cols), F32)] * 2,
        compiler_params=pltpu.CompilerParams(vmem_limit_bytes=VMEM_LIMIT),
        cost_estimate=pl.CostEstimate(flops=30_000_000, bytes_accessed=10_000_000, transcendentals=0),
    )(place, x, left, right, drag, margin)


def forecast_kernel(
    members, rows,
    place_ref, order_ref, owner_ref, cell_ref,
    inner_ref, above_ref, below_ref, ceven_ref, codd_ref, drag_ref, margin_ref,
    out_ref, prior_ref,
    state, keep, slope,
):
    cols = above_ref.shape[2]
    wide = 2 * cols
    total = rows + 2 * MARGIN
    half = cols // 2
    lane = lanes_of((GROUP, cols))
    factor = -0.2 * grid_factor(place_ref, (total, wide), rows, cols)
    odd_y = place_ref[0] % place_ref[5] % 2 == 1
    shift = shift_matrix(wide)
    count = 3 * members // 2
    parts = []
    for here, own in ((count, drag_ref), (count + MARGIN, margin_ref)):
        even, odd = ceven_ref[here : here + MARGIN, :], codd_ref[here : here + MARGIN, :]
        above, below = jnp.where(odd_y, even, odd), jnp.where(odd_y, odd, even)
        parts.append(jnp.concatenate([above, own[...], below], axis=0))
    kept = 1.0 - jnp.concatenate(parts, axis=1)
    for r in range(total):
        keep[r] = jnp.broadcast_to(kept[r : r + 1, :], (8, wide))
        slope[r] = jnp.broadcast_to(factor[r : r + 1, :], (8, wide))

    groups = range(members // GROUP)
    for g in groups:
        here = pl.ds(g * GROUP, GROUP)
        for f in range(3):
            at = f * members + g * GROUP
            base = half if at >= count else 0
            at = pl.ds(at % count, GROUP)
            ceven, codd = ceven_ref[at, :], codd_ref[at, :]
            cab, cbe = jnp.where(odd_y, ceven, codd), jnp.where(odd_y, codd, ceven)
            depth = MARGIN if f == 2 else MARGIN - 1
            for d in range(depth):
                r = MARGIN - depth + d
                main = above_ref[f * (MARGIN - 1) + d, here, :]
                state[g, f, r] = wide_row(lane, main, cab, base + MARGIN * r, cab, base + MARGIN * (MARGIN - 1 - r))
                main = below_ref[f * (MARGIN - 1) + d, here, :]
                state[g, f, MARGIN + rows + d] = wide_row(
                    lane, main, cbe, base + MARGIN * d, cbe, base + MARGIN * (MARGIN - 1 - d)
                )
            for r in range(rows):
                state[g, f, MARGIN + r] = inner_ref[f, r, here, :]

    def heights(g, spans):
        for low, high in spans:
            d = column_slope(state[g, 1, low:high], shift)
            for r in range(low, high):
                div = d[r - low] + (state[g, 2, r + 1] - state[g, 2, r - 1])
                state[g, 0, r] = state[g, 0, r] + tall(slope[r]) * div

    def flows(g, spans, final):
        here = pl.ds(g * GROUP, GROUP)
        for low, high in spans:
            d = column_slope(state[g, 0, low:high], shift)
            for r in range(low, high):
                u, v = state[g, 1, r], state[g, 2, r]
                k, c = tall(keep[r]), tall(slope[r])
                u, v = (
                    k * u + c * d[r - low] + 0.1 * v,
                    k * v + c * (state[g, 0, r + 1] - state[g, 0, r - 1]) - 0.1 * u,
                )
                if final:
                    for f, value in enumerate((state[g, 0, r], u, v)):
                        out_ref[f * rows + r - MARGIN, here, :] = value[:, 0:cols]
                else:
                    state[g, 1, r] = u
                    state[g, 2, r] = v

    for step in range(STEPS):
        first, last = MARGIN - MARGIN + 1 + 2 * step, MARGIN + rows + MARGIN - 1 - 2 * step
        done, still = MARGIN + 1 + 2 * step, MARGIN + rows - 1 - 2 * step
        for g in groups:
            heights(g, ((first, done), (still, last)))
        for g in groups:
            flows(g, ((first + 1, done + 1), (still - 1, last - 1)), step == STEPS - 1)
    prior_ref[...] = jnp.zeros_like(prior_ref)
    eight = lanes_of((8, cols))
    for i in range(order_ref.shape[0]):
        which = order_ref[i]

        @pl.when(owner_ref[which] == place_ref[0])
        def _():
            cell = cell_ref[which]
            one = jnp.where(eight == cell % cols, 1.0, 0.0)
            prior_ref[i : i + 1, 0:members] = lax.dot_general(
                one, out_ref[cell // cols], NT, precision=HIGHEST, preferred_element_type=F32
            )[0:1]


def forecast(place, order, owner, cell, inner, *arrays):
    _, rows, members, wide = inner.shape
    cols = wide // 2
    total = rows + 2 * MARGIN
    return pl.pallas_call(
        functools.partial(forecast_kernel, members, rows),
        out_shape=(
            jax.ShapeDtypeStruct((3 * rows, members, cols), F32),
            jax.ShapeDtypeStruct((order.shape[0], cols), F32),
        ),
        in_specs=[SSPEC] * 4 + [VSPEC] * (1 + len(arrays)),
        out_specs=(VSPEC, VSPEC),
        scratch_shapes=[pltpu.VMEM((members // GROUP, 3, total, GROUP, wide), F32)] + [pltpu.VMEM((total, 8, wide), F32)] * 2,
        compiler_params=pltpu.CompilerParams(vmem_limit_bytes=VMEM_LIMIT),
        cost_estimate=pl.CostEstimate(flops=60_000_000, bytes_accessed=30_000_000, transcendentals=0),
    )(place, order, owner, cell, inner, *arrays)


def localize(distance, reach, taper_ref):
    picked = jnp.zeros(distance.shape, F32)
    levels = taper_ref.shape[0]
    capped = jnp.minimum(distance, levels - 1)
    for d in range(levels):
        picked = jnp.where(capped == d, taper_ref[d], picked)
    return jnp.where(distance <= reach, picked, 0.0)


def assimilate_kernel(
    members, rows,
    place_ref, order_ref, owner_ref, reach_ref, value_ref, error_ref, taper_ref,
    prior_ref, forecast_ref,
    result_ref,
    out_ref, sems,
):
    n_obs = order_ref.shape[0]
    cols = prior_ref.shape[1]
    size_y = place_ref[5]
    lane1 = lanes_of((1, cols))
    lane = lanes_of((n_obs, cols))
    sub = sublanes_of((n_obs, cols))

    tile_row = jnp.zeros((1, cols), jnp.int32)
    tile_col = jnp.zeros((n_obs, cols), jnp.int32)
    reach_row = jnp.zeros((1, cols), jnp.int32)
    reach_col = jnp.zeros((n_obs, cols), jnp.int32)
    which = [order_ref[i] for i in range(n_obs)]
    for i, k in enumerate(which):
        tile_row = jnp.where(lane1 == i, owner_ref[k], tile_row)
        tile_col = jnp.where(sub == i, owner_ref[k], tile_col)
        reach_row = jnp.where(lane1 == i, reach_ref[k], reach_row)
        reach_col = jnp.where(sub == i, reach_ref[k], reach_col)
    rx, ry = tile_row // size_y, tile_row % size_y
    cx, cy = tile_col // size_y, tile_col % size_y
    distance = jnp.maximum(jnp.abs(cx - rx), jnp.abs(cy - ry))
    onto = localize(distance, reach_row, taper_ref)
    onto_t = localize(distance, reach_col, taper_ref)
    mine = place_ref[0]
    own = localize(
        jnp.maximum(jnp.abs(mine // size_y - rx), jnp.abs(mine % size_y - ry)), reach_row, taper_ref
    )

    priors = prior_ref[...]
    inside = lane < members
    mean_col = jnp.sum(jnp.where(inside, priors, 0.0), axis=1, keepdims=True) / members
    anomalies = jnp.where(inside, priors - mean_col, 0.0)
    padded = jnp.concatenate([anomalies, jnp.zeros((cols - n_obs, cols), F32)], axis=0)
    table = lax.dot_general(anomalies, padded, NT, precision=HIGHEST, preferred_element_type=F32)
    table = jnp.concatenate([table, jnp.transpose(padded)[:members]], axis=0)
    mean = jnp.zeros((1, cols), F32)
    for i in range(n_obs):
        mean = jnp.where(lane1 == i, mean_col[i : i + 1, :], mean)

    scales = jnp.zeros((1, cols), F32)
    increments = []
    power = jnp.broadcast_to(table[0:1, 0:1], (1, cols))
    for i, k in enumerate(which):
        error = error_ref[k]
        row = table[i : i + 1, :]
        column = jnp.broadcast_to(table[:, i : i + 1], table.shape)
        variance = power / (members - 1) + EPS
        root = lax.rsqrt(1.0 + variance * (1.0 / error))
        scaled = 1.0 / ((members - 1) * variance)
        shift = variance * (value_ref[k] - jnp.broadcast_to(mean[:, i : i + 1], row.shape)) * (root * root * (1.0 / error))
        shrink = root - 1.0
        weight = scaled * jnp.broadcast_to(own[:, i : i + 1], row.shape)
        alpha_row = onto_t[i : i + 1, :] * row * scaled
        later = lane1 > i
        h = jnp.where(later, shrink * alpha_row, 0.0)
        q = jnp.where(later, shrink * (row + h * power), 0.0)
        alpha = jnp.concatenate(
            [jnp.broadcast_to(onto[:, i : i + 1], onto.shape) * column[:n_obs] * scaled, column[n_obs:] * weight], axis=0
        )
        if i + 1 < n_obs:
            beside, ahead, reach_on = (
                jnp.broadcast_to(x[:, i + 1 : i + 2], row.shape)
                for x in (row, table[i + 1 : i + 2, :], onto_t[i : i + 1, :])
            )
            step = reach_on * beside * scaled
            power = ahead + beside * (shrink * step) + step * (shrink * (beside + shrink * step * power))
        table = table + column * h + alpha * q
        mean = mean + alpha_row * shift
        now = anomalies[i : i + 1, :]
        increments.append(shift + shrink * now)
        anomalies = anomalies + jnp.where(sub > i, shrink * alpha[:n_obs], 0.0) * now
        scales = jnp.where(lane1 == i, weight, scales)
    left = table[n_obs:, :] * scales
    right = jnp.where(inside, jnp.concatenate(increments, axis=0), 0.0)
    right = jnp.concatenate([right, jnp.zeros((cols - n_obs, cols), F32)], axis=0)
    change = jnp.dot(left, right, precision=HIGHEST, preferred_element_type=F32)
    change = jnp.concatenate([change, jnp.zeros((cols - members, cols), F32)], axis=0)
    change = jnp.transpose(change)[:members, :]
    high = change.astype(BF16).astype(F32)
    low = change - high
    zero = jnp.zeros((members, cols), F32)
    high = jnp.concatenate([high, zero], axis=1)
    low = jnp.concatenate([low, zero], axis=1)
    factor = (high + roll_lanes(high, members) + roll_lanes(low, 2 * members)).astype(BF16)

    block = 4
    for at in range(0, 3 * rows, block):
        x = jnp.concatenate([forecast_ref[at + b] for b in range(block)], axis=1)
        xh = x.astype(BF16)
        xl = (x - xh.astype(F32)).astype(BF16)
        stack = jnp.concatenate([xh, xl, xh, jnp.zeros((2 * cols - 3 * members, block * cols), BF16)], axis=0)
        y = x + jnp.dot(factor, stack, preferred_element_type=F32)
        for b in range(block):
            f, r = divmod(at + b, rows)
            out_ref[pl.ds(f * members * rows + r, members, stride=rows), :] = y[:, b * cols : (b + 1) * cols]
        if (at + block) % rows == 0:
            field = pl.ds(at // rows * members * rows, members * rows)
            pltpu.make_async_copy(out_ref.at[field], result_ref.at[field], sems.at[at // rows]).start()
    for f in range(3):
        field = pl.ds(f * members * rows, members * rows)
        pltpu.make_async_copy(out_ref.at[field], result_ref.at[field], sems.at[f]).wait()


def assimilate(place, order, owner, reach, value, error, taper, priors, states, members, rows):
    cols = priors.shape[1]
    return pl.pallas_call(
        functools.partial(assimilate_kernel, members, rows),
        out_shape=jax.ShapeDtypeStruct((3 * members * rows, cols), F32),
        in_specs=[SSPEC] * 7 + [VSPEC] * 2,
        out_specs=pl.BlockSpec(memory_space=pl.ANY),
        scratch_shapes=[pltpu.VMEM((3 * members * rows, cols), F32), pltpu.SemaphoreType.DMA((3,))],
        compiler_params=pltpu.CompilerParams(vmem_limit_bytes=VMEM_LIMIT),
    )(place, order, owner, reach, value, error, taper, priors, states)


def to_neighbours(axis, lower, upper):
    count = lax.axis_size(axis)
    forward = [(i, i + 1) for i in range(count - 1)]
    backward = [(target, source) for source, target in forward]
    return lax.ppermute(upper, axis, forward), lax.ppermute(lower, axis, backward)


def swap_pairs(x, axis, start):
    pairs = [(i, i + 1) for i in range(start, lax.axis_size(axis) - 1, 2)]
    return lax.ppermute(x, axis, pairs + [(b, a) for a, b in pairs])


def add_over(x, axes):
    for axis in axes:
        count = lax.axis_size(axis)
        if count & (count - 1):
            x = lax.psum(x, axis)
            continue
        span = 1
        while span < count:
            x = x + lax.ppermute(x, axis, [(i, i ^ span) for i in range(count)])
            span *= 2
    return x


def body(status, drag, value, error, taper, order, owner, cell, reach):
    members, rows, cols = status.shape[1:]
    ix, iy = lax.axis_index("gx"), lax.axis_index("gy")
    size_x, size_y = lax.axis_size("gx"), lax.axis_size("gy")
    place = jnp.stack(
        [
            ix * size_y + iy,
            (ix == 0).astype(jnp.int32),
            (ix == size_x - 1).astype(jnp.int32),
            (iy == 0).astype(jnp.int32),
            (iy == size_y - 1).astype(jnp.int32),
            jnp.int32(size_y),
        ]
    ).astype(jnp.int32)
    flat = status.reshape(3 * members * rows, cols)
    lower, upper = bands(flat, members, rows)
    above, below = to_neighbours("gy", lower, upper)
    even, odd = pack(place, flat, drag, members)
    even, odd = swap_pairs(even, "gx", 0), swap_pairs(odd, "gx", 1)
    left, right, margin, even, odd = corner(place, drag, even, odd)
    even, odd = swap_pairs(even, "gy", 0), swap_pairs(odd, "gy", 1)
    inner = interior(place, flat, left, right, drag, margin, members)
    states, priors = forecast(place, order, owner, cell, inner, above, below, even, odd, drag, margin)
    priors = add_over(priors, ("gy", "gx"))
    result = assimilate(place, order, owner, reach, value, error, taper, priors, states, members, rows)
    return result.reshape(status.shape)


def solution(mesh):
    in_specs = (P(None, None, "gy", "gx"), P("gy", "gx"), P(), P(), P(), P(), P(), P(), P())
    out_specs = P(None, None, "gy", "gx")
    return jax.shard_map(body, mesh=mesh, in_specs=in_specs, out_specs=out_specs, check_vma=False)
```

```python
import functools

import jax
import jax.numpy as jnp
from jax import lax
from jax.experimental import pallas as pl
from jax.experimental.pallas import tpu as pltpu
from jax.sharding import PartitionSpec as P

STEPS = 4
MARGIN = 2 * STEPS
EPS = 1e-06
NT = (((1,), (1,)), ((), ()))
HIGHEST = lax.Precision.HIGHEST
F32 = jnp.float32
BF16 = jnp.bfloat16
VMEM_LIMIT = 24 * 1024 * 1024
GROUP = 40

VSPEC = pl.BlockSpec(memory_space=pltpu.VMEM)
SSPEC = pl.BlockSpec(memory_space=pltpu.SMEM)


def lanes_of(shape):
    return lax.broadcasted_iota(jnp.int32, shape, len(shape) - 1)


def sublanes_of(shape):
    return lax.broadcasted_iota(jnp.int32, shape, len(shape) - 2)


def roll_lanes(x, shift):
    size = x.shape[-1]
    shift = shift % size
    return x if shift == 0 else pltpu.roll(x, shift, x.ndim - 1)


def band_kernel(members, rows, x_hbm, lower_hbm, upper_hbm, x_ref, lower_ref, upper_ref, sems):
    def arrive(f):
        field = pl.ds(f * members * rows, members * rows)
        return pltpu.make_async_copy(x_hbm.at[field], x_ref.at[field], sems.at[0, f])

    def leave(f, side):
        source, target = ((lower_ref, lower_hbm), (upper_ref, upper_hbm))[side]
        here = pl.ds(f * (MARGIN - 1), MARGIN if f == 2 else MARGIN - 1)
        return pltpu.make_async_copy(source.at[here], target.at[here], sems.at[1 + side, f])

    for f in range(3):
        arrive(f).start()
    for f in range(3):
        arrive(f).wait()
        depth = MARGIN if f == 2 else MARGIN - 1
        for d in range(depth):
            at = f * members * rows + d
            lower_ref[f * (MARGIN - 1) + d] = x_ref[pl.ds(at, members, stride=rows), :]
            upper_ref[f * (MARGIN - 1) + d] = x_ref[pl.ds(at + rows - depth, members, stride=rows), :]
        leave(f, 0).start()
        leave(f, 1).start()
    for f in range(3):
        leave(f, 0).wait()
        leave(f, 1).wait()


def bands(x, members, rows):
    cols = x.shape[1]
    shape = (3 * MARGIN - 2, members, cols)
    return pl.pallas_call(
        functools.partial(band_kernel, members, rows),
        out_shape=(jax.ShapeDtypeStruct(shape, F32),) * 2,
        in_specs=[pl.BlockSpec(memory_space=pltpu.HBM)],
        out_specs=(pl.BlockSpec(memory_space=pl.ANY),) * 2,
        scratch_shapes=[pltpu.VMEM(x.shape, F32)] + [pltpu.VMEM(shape, F32)] * 2 + [pltpu.SemaphoreType.DMA((3, 3))],
        compiler_params=pltpu.CompilerParams(vmem_limit_bytes=60 * 1024 * 1024),
        cost_estimate=pl.CostEstimate(flops=1_000_000, bytes_accessed=4_000_000, transcendentals=0),
    )(x)


def pack_kernel(members, rows, place_ref, x_ref, drag_ref, even_ref, odd_ref):
    cols = x_ref.shape[1]
    lane = lanes_of((8, cols))
    slot = lane // MARGIN
    odd_x = place_ref[0] // place_ref[5] % 2 == 1

    def group(g, carry):
        for f in range(3):
            row = [x_ref[pl.ds((f * members + g * 8) * rows + r, 8, stride=rows), :] for r in range(rows)]
            left, right = row[rows - 1], roll_lanes(row[rows - 1], MARGIN * rows)
            for r in range(rows - 1):
                both = roll_lanes(jnp.where(lane < cols // 2, row[rows - 2 - r], row[r]), MARGIN * (r + 1))
                left = jnp.where(slot == r + 1, both, left)
                right = jnp.where(slot == r, both, right)
            at = pl.ds(pl.multiple_of(f * members + g * 8, 8), 8)
            even_ref[at, :] = jnp.where(odd_x, left, right)
            odd_ref[at, :] = jnp.where(odd_x, right, left)
        return carry

    lax.fori_loop(0, members // 8, group, 0)
    even_ref[3 * members :, :] = drag_ref[...]
    odd_ref[3 * members :, :] = drag_ref[...]


def pack(place, x, drag, members):
    rows, cols = drag.shape
    message = jax.ShapeDtypeStruct((3 * members + rows, cols), F32)
    return pl.pallas_call(
        functools.partial(pack_kernel, members, rows),
        out_shape=(message, message),
        in_specs=[SSPEC, VSPEC, VSPEC],
        out_specs=(VSPEC,) * 2,
        compiler_params=pltpu.CompilerParams(vmem_limit_bytes=VMEM_LIMIT),
        cost_estimate=pl.CostEstimate(flops=1_000_000, bytes_accessed=4_000_000, transcendentals=0),
    )(place, x, drag)


def corner_kernel(place_ref, drag_ref, even_ref, odd_ref, left_ref, right_ref, margin_ref, even_out, odd_out):
    count, cols = left_ref.shape
    rows = drag_ref.shape[0]
    half = cols // 2
    odd_y = place_ref[0] % place_ref[5] % 2 == 1
    odd_x = place_ref[0] // place_ref[5] % 2 == 1
    even, odd = even_ref[...], odd_ref[...]
    left, right = jnp.where(odd_x, even, odd), jnp.where(odd_x, odd, even)
    margin = jnp.where(lanes_of((rows, cols)) < half, right[count:], left[count:])
    margin_ref[...] = margin
    left, right = left[:count], right[:count]
    left_ref[...] = left
    right_ref[...] = right
    lane = lanes_of((count, cols))
    slot, column = lane % half // MARGIN, lane % MARGIN
    mine = column > jnp.where(lane < half, slot, MARGIN - 1 - slot)
    both = jnp.where(mine, left, roll_lanes(right, half))
    count = count // 2
    head, tail = both[:count], both[count:]
    first_half = lanes_of((count, cols)) < half
    lower = jnp.where(first_half, head, roll_lanes(tail, half))
    upper = jnp.where(first_half, roll_lanes(head, half), tail)
    even_out[:count, :] = jnp.where(odd_y, lower, upper)
    odd_out[:count, :] = jnp.where(odd_y, upper, lower)
    drag = drag_ref[...]
    for at, part in ((count, drag), (count + MARGIN, margin)):
        lower, upper = part[:MARGIN], part[rows - MARGIN :]
        even_out[at : at + MARGIN, :] = jnp.where(odd_y, lower, upper)
        odd_out[at : at + MARGIN, :] = jnp.where(odd_y, upper, lower)


def corner(place, drag, even, odd):
    rows, cols = drag.shape
    count = even.shape[0] - rows
    edge = jax.ShapeDtypeStruct((count, cols), F32)
    message = jax.ShapeDtypeStruct((count // 2 + 2 * MARGIN, cols), F32)
    return pl.pallas_call(
        corner_kernel,
        out_shape=(edge, edge, jax.ShapeDtypeStruct((rows, cols), F32), message, message),
        in_specs=[SSPEC] + [VSPEC] * 3,
        out_specs=(VSPEC,) * 5,
        compiler_params=pltpu.CompilerParams(vmem_limit_bytes=VMEM_LIMIT),
    )(place, drag, even, odd)


def grid_factor(place_ref, shape, rows, cols):
    row, col = sublanes_of(shape), lanes_of(shape)
    wide = 2 * cols
    low, high = jnp.where(place_ref[3] == 1, MARGIN, 0), jnp.where(place_ref[4] == 1, MARGIN + rows, rows + 2 * MARGIN)
    first, last = jnp.where(place_ref[1] == 1, wide, wide - MARGIN), jnp.where(place_ref[2] == 1, cols, cols + MARGIN)
    ok = (row >= low) & (row < high) & ((col < last) | (col >= first))
    return jnp.where(ok, 1.0, 0.0)


def wide_row(lane, main, left, left_at, right, right_at):
    cols = main.shape[1]
    halo = jnp.where(lane >= cols - MARGIN, roll_lanes(left, cols - MARGIN - left_at), 0.0)
    halo = jnp.where(lane < MARGIN, roll_lanes(right, -right_at), halo)
    return jnp.concatenate([main, halo], axis=1)


def shift_matrix(wide):
    source, target = sublanes_of((wide, wide)), lanes_of((wide, wide))
    after, before = source == (target + 1) % wide, target == (source + 1) % wide
    return jnp.where(after, 1.0, jnp.where(before, -1.0, 0.0)).astype(BF16)


def tall(x):
    return jnp.concatenate([x] * (GROUP // 8), axis=0)


def column_slope(x, shift):
    rows, group, wide = x.shape
    x = x.reshape(rows * group, wide)
    top = x.astype(BF16)
    rest = (x - top.astype(F32)).astype(BF16)
    slope = jnp.dot(top, shift, preferred_element_type=F32) + jnp.dot(rest, shift, preferred_element_type=F32)
    return slope.reshape(rows, group, wide)


def interior_kernel(members, rows, place_ref, x_ref, left_ref, right_ref, drag_ref, margin_ref, state, keep, slope):
    cols = x_ref.shape[1]
    wide = 2 * cols
    lane = lanes_of((8, cols))
    factor = -0.2 * grid_factor(place_ref, (rows + 2 * MARGIN, wide), rows, cols)
    shift = shift_matrix(wide)
    kept = 1.0 - jnp.concatenate([drag_ref[...], margin_ref[...]], axis=1)
    for r in range(rows):
        keep[r] = jnp.broadcast_to(kept[r : r + 1, :], (8, wide))
        slope[r] = jnp.broadcast_to(factor[MARGIN + r : MARGIN + r + 1, :], (8, wide))

    def first(g, carry):
        here = pl.ds(pl.multiple_of(g * 8, 8), 8)
        for f in range(3):
            at = pl.ds(pl.multiple_of(f * members + g * 8, 8), 8)
            left, right = left_ref[at, :], right_ref[at, :]
            for r in range(rows):
                main = x_ref[pl.ds((f * members + g * 8) * rows + r, 8, stride=rows), :]
                state[f, r, here, :] = wide_row(lane, main, left, MARGIN * r, right, MARGIN * (rows - 1 - r))
        return carry

    lax.fori_loop(0, members // 8, first, 0)

    groups = [pl.ds(m, GROUP) for m in range(0, members, GROUP)]
    for step in range(STEPS):
        low, high = 1 + 2 * step, rows - 1 - 2 * step
        if low >= high:
            break
        for here in groups:
            d = column_slope(state[1, low:high, here, :], shift)
            for r in range(low, high):
                div = d[r - low] + (state[2, r + 1, here, :] - state[2, r - 1, here, :])
                state[0, r, here, :] = state[0, r, here, :] + tall(slope[r]) * div
        low, high = low + 1, high - 1
        if low >= high:
            break
        for here in groups:
            d = column_slope(state[0, low:high, here, :], shift)
            for r in range(low, high):
                u, v = state[1, r, here, :], state[2, r, here, :]
                k, c = tall(keep[r]), tall(slope[r])
                state[1, r, here, :] = k * u + c * d[r - low] + 0.1 * v
                state[2, r, here, :] = k * v + c * (state[0, r + 1, here, :] - state[0, r - 1, here, :]) - 0.1 * u


def interior(place, x, left, right, drag, margin, members):
    rows, cols = drag.shape
    return pl.pallas_call(
        functools.partial(interior_kernel, members, rows),
        out_shape=jax.ShapeDtypeStruct((3, rows, members, 2 * cols), F32),
        in_specs=[SSPEC] + [VSPEC] * 5,
        out_specs=VSPEC,
        scratch_shapes=[pltpu.VMEM((rows, 8, 2 * cols), F32)] * 2,
        compiler_params=pltpu.CompilerParams(vmem_limit_bytes=VMEM_LIMIT),
        cost_estimate=pl.CostEstimate(flops=30_000_000, bytes_accessed=10_000_000, transcendentals=0),
    )(place, x, left, right, drag, margin)


def forecast_kernel(
    members, rows,
    place_ref, order_ref, owner_ref, cell_ref,
    inner_ref, above_ref, below_ref, ceven_ref, codd_ref, drag_ref, margin_ref,
    out_ref, prior_ref,
    state, keep, slope,
):
    cols = above_ref.shape[2]
    wide = 2 * cols
    total = rows + 2 * MARGIN
    half = cols // 2
    lane = lanes_of((GROUP, cols))
    factor = -0.2 * grid_factor(place_ref, (total, wide), rows, cols)
    odd_y = place_ref[0] % place_ref[5] % 2 == 1
    shift = shift_matrix(wide)
    count = 3 * members // 2
    parts = []
    for here, own in ((count, drag_ref), (count + MARGIN, margin_ref)):
        even, odd = ceven_ref[here : here + MARGIN, :], codd_ref[here : here + MARGIN, :]
        above, below = jnp.where(odd_y, even, odd), jnp.where(odd_y, odd, even)
        parts.append(jnp.concatenate([above, own[...], below], axis=0))
    kept = 1.0 - jnp.concatenate(parts, axis=1)
    for r in range(total):
        keep[r] = jnp.broadcast_to(kept[r : r + 1, :], (8, wide))
        slope[r] = jnp.broadcast_to(factor[r : r + 1, :], (8, wide))

    groups = range(members // GROUP)
    for g in groups:
        here = pl.ds(g * GROUP, GROUP)
        for f in range(3):
            at = f * members + g * GROUP
            base = half if at >= count else 0
            at = pl.ds(at % count, GROUP)
            ceven, codd = ceven_ref[at, :], codd_ref[at, :]
            cab, cbe = jnp.where(odd_y, ceven, codd), jnp.where(odd_y, codd, ceven)
            depth = MARGIN if f == 2 else MARGIN - 1
            for d in range(depth):
                r = MARGIN - depth + d
                main = above_ref[f * (MARGIN - 1) + d, here, :]
                state[g, f, r] = wide_row(lane, main, cab, base + MARGIN * r, cab, base + MARGIN * (MARGIN - 1 - r))
                main = below_ref[f * (MARGIN - 1) + d, here, :]
                state[g, f, MARGIN + rows + d] = wide_row(
                    lane, main, cbe, base + MARGIN * d, cbe, base + MARGIN * (MARGIN - 1 - d)
                )
            for r in range(rows):
                state[g, f, MARGIN + r] = inner_ref[f, r, here, :]

    def heights(g, spans):
        for low, high in spans:
            d = column_slope(state[g, 1, low:high], shift)
            for r in range(low, high):
                div = d[r - low] + (state[g, 2, r + 1] - state[g, 2, r - 1])
                state[g, 0, r] = state[g, 0, r] + tall(slope[r]) * div

    def flows(g, spans, final):
        here = pl.ds(g * GROUP, GROUP)
        for low, high in spans:
            d = column_slope(state[g, 0, low:high], shift)
            for r in range(low, high):
                u, v = state[g, 1, r], state[g, 2, r]
                k, c = tall(keep[r]), tall(slope[r])
                u, v = (
                    k * u + c * d[r - low] + 0.1 * v,
                    k * v + c * (state[g, 0, r + 1] - state[g, 0, r - 1]) - 0.1 * u,
                )
                if final:
                    for f, value in enumerate((state[g, 0, r], u, v)):
                        out_ref[f * rows + r - MARGIN, here, :] = value[:, 0:cols]
                else:
                    state[g, 1, r] = u
                    state[g, 2, r] = v

    for step in range(STEPS):
        first, last = MARGIN - MARGIN + 1 + 2 * step, MARGIN + rows + MARGIN - 1 - 2 * step
        done, still = MARGIN + 1 + 2 * step, MARGIN + rows - 1 - 2 * step
        for g in groups:
            heights(g, ((first, done), (still, last)))
        for g in groups:
            flows(g, ((first + 1, done + 1), (still - 1, last - 1)), step == STEPS - 1)
    prior_ref[...] = jnp.zeros_like(prior_ref)
    eight = lanes_of((8, cols))
    for i in range(order_ref.shape[0]):
        which = order_ref[i]

        @pl.when(owner_ref[which] == place_ref[0])
        def _():
            cell = cell_ref[which]
            one = jnp.where(eight == cell % cols, 1.0, 0.0)
            prior_ref[i : i + 1, 0:members] = lax.dot_general(
                one, out_ref[cell // cols], NT, precision=HIGHEST, preferred_element_type=F32
            )[0:1]


def forecast(place, order, owner, cell, inner, *arrays):
    _, rows, members, wide = inner.shape
    cols = wide // 2
    total = rows + 2 * MARGIN
    return pl.pallas_call(
        functools.partial(forecast_kernel, members, rows),
        out_shape=(
            jax.ShapeDtypeStruct((3 * rows, members, cols), F32),
            jax.ShapeDtypeStruct((order.shape[0], cols), F32),
        ),
        in_specs=[SSPEC] * 4 + [VSPEC] * (1 + len(arrays)),
        out_specs=(VSPEC, VSPEC),
        scratch_shapes=[pltpu.VMEM((members // GROUP, 3, total, GROUP, wide), F32)] + [pltpu.VMEM((total, 8, wide), F32)] * 2,
        compiler_params=pltpu.CompilerParams(vmem_limit_bytes=VMEM_LIMIT),
        cost_estimate=pl.CostEstimate(flops=60_000_000, bytes_accessed=30_000_000, transcendentals=0),
    )(place, order, owner, cell, inner, *arrays)


def localize(distance, reach, taper_ref):
    picked = jnp.zeros(distance.shape, F32)
    levels = taper_ref.shape[0]
    capped = jnp.minimum(distance, levels - 1)
    for d in range(levels):
        picked = jnp.where(capped == d, taper_ref[d], picked)
    return jnp.where(distance <= reach, picked, 0.0)


def assimilate_kernel(
    members, rows,
    place_ref, order_ref, owner_ref, reach_ref, value_ref, error_ref, taper_ref,
    prior_ref, forecast_ref,
    result_ref,
    out_ref, sems,
):
    n_obs = order_ref.shape[0]
    cols = prior_ref.shape[1]
    size_y = place_ref[5]
    lane1 = lanes_of((1, cols))
    lane = lanes_of((n_obs, cols))
    sub = sublanes_of((n_obs, cols))

    tile_row = jnp.zeros((1, cols), jnp.int32)
    tile_col = jnp.zeros((n_obs, cols), jnp.int32)
    reach_row = jnp.zeros((1, cols), jnp.int32)
    reach_col = jnp.zeros((n_obs, cols), jnp.int32)
    which = [order_ref[i] for i in range(n_obs)]
    for i, k in enumerate(which):
        tile_row = jnp.where(lane1 == i, owner_ref[k], tile_row)
        tile_col = jnp.where(sub == i, owner_ref[k], tile_col)
        reach_row = jnp.where(lane1 == i, reach_ref[k], reach_row)
        reach_col = jnp.where(sub == i, reach_ref[k], reach_col)
    rx, ry = tile_row // size_y, tile_row % size_y
    cx, cy = tile_col // size_y, tile_col % size_y
    distance = jnp.maximum(jnp.abs(cx - rx), jnp.abs(cy - ry))
    onto = localize(distance, reach_row, taper_ref)
    onto_t = localize(distance, reach_col, taper_ref)
    mine = place_ref[0]
    own = localize(
        jnp.maximum(jnp.abs(mine // size_y - rx), jnp.abs(mine % size_y - ry)), reach_row, taper_ref
    )

    priors = prior_ref[...]
    inside = lane < members
    mean_col = jnp.sum(jnp.where(inside, priors, 0.0), axis=1, keepdims=True) / members
    anomalies = jnp.where(inside, priors - mean_col, 0.0)
    padded = jnp.concatenate([anomalies, jnp.zeros((cols - n_obs, cols), F32)], axis=0)
    table = lax.dot_general(anomalies, padded, NT, precision=HIGHEST, preferred_element_type=F32)
    table = jnp.concatenate([table, jnp.transpose(padded)[:members]], axis=0)
    mean = jnp.zeros((1, cols), F32)
    for i in range(n_obs):
        mean = jnp.where(lane1 == i, mean_col[i : i + 1, :], mean)

    scales = jnp.zeros((1, cols), F32)
    increments = []
    power = jnp.broadcast_to(table[0:1, 0:1], (1, cols))
    for i, k in enumerate(which):
        error = error_ref[k]
        row = table[i : i + 1, :]
        column = jnp.broadcast_to(table[:, i : i + 1], table.shape)
        variance = power / (members - 1) + EPS
        root = lax.rsqrt(1.0 + variance * (1.0 / error))
        scaled = 1.0 / ((members - 1) * variance)
        shift = variance * (value_ref[k] - jnp.broadcast_to(mean[:, i : i + 1], row.shape)) * (root * root * (1.0 / error))
        shrink = root - 1.0
        weight = scaled * jnp.broadcast_to(own[:, i : i + 1], row.shape)
        alpha_row = onto_t[i : i + 1, :] * row * scaled
        later = lane1 > i
        h = jnp.where(later, shrink * alpha_row, 0.0)
        q = jnp.where(later, shrink * (row + h * power), 0.0)
        alpha = jnp.concatenate(
            [jnp.broadcast_to(onto[:, i : i + 1], onto.shape) * column[:n_obs] * scaled, column[n_obs:] * weight], axis=0
        )
        if i + 1 < n_obs:
            beside, ahead, reach_on = (
                jnp.broadcast_to(x[:, i + 1 : i + 2], row.shape)
                for x in (row, table[i + 1 : i + 2, :], onto_t[i : i + 1, :])
            )
            step = reach_on * beside * scaled
            power = ahead + beside * (shrink * step) + step * (shrink * (beside + shrink * step * power))
        table = table + column * h + alpha * q
        mean = mean + alpha_row * shift
        now = anomalies[i : i + 1, :]
        increments.append(shift + shrink * now)
        anomalies = anomalies + jnp.where(sub > i, shrink * alpha[:n_obs], 0.0) * now
        scales = jnp.where(lane1 == i, weight, scales)
    left = table[n_obs:, :] * scales
    right = jnp.where(inside, jnp.concatenate(increments, axis=0), 0.0)
    right = jnp.concatenate([right, jnp.zeros((cols - n_obs, cols), F32)], axis=0)
    change = jnp.dot(left, right, precision=HIGHEST, preferred_element_type=F32)
    change = jnp.concatenate([change, jnp.zeros((cols - members, cols), F32)], axis=0)
    change = jnp.transpose(change)[:members, :]
    high = change.astype(BF16).astype(F32)
    low = change - high
    zero = jnp.zeros((members, cols), F32)
    high = jnp.concatenate([high, zero], axis=1)
    low = jnp.concatenate([low, zero], axis=1)
    factor = (high + roll_lanes(high, members) + roll_lanes(low, 2 * members)).astype(BF16)

    block = 4
    for at in range(0, 3 * rows, block):
        x = jnp.concatenate([forecast_ref[at + b] for b in range(block)], axis=1)
        xh = x.astype(BF16)
        xl = (x - xh.astype(F32)).astype(BF16)
        stack = jnp.concatenate([xh, xl, xh, jnp.zeros((2 * cols - 3 * members, block * cols), BF16)], axis=0)
        y = x + jnp.dot(factor, stack, preferred_element_type=F32)
        for b in range(block):
            f, r = divmod(at + b, rows)
            out_ref[pl.ds(f * members * rows + r, members, stride=rows), :] = y[:, b * cols : (b + 1) * cols]
        if (at + block) % rows == 0:
            field = pl.ds(at // rows * members * rows, members * rows)
            pltpu.make_async_copy(out_ref.at[field], result_ref.at[field], sems.at[at // rows]).start()
    for f in range(3):
        field = pl.ds(f * members * rows, members * rows)
        pltpu.make_async_copy(out_ref.at[field], result_ref.at[field], sems.at[f]).wait()


def assimilate(place, order, owner, reach, value, error, taper, priors, states, members, rows):
    cols = priors.shape[1]
    return pl.pallas_call(
        functools.partial(assimilate_kernel, members, rows),
        out_shape=jax.ShapeDtypeStruct((3 * members * rows, cols), F32),
        in_specs=[SSPEC] * 7 + [VSPEC] * 2,
        out_specs=pl.BlockSpec(memory_space=pl.ANY),
        scratch_shapes=[pltpu.VMEM((3 * members * rows, cols), F32), pltpu.SemaphoreType.DMA((3,))],
        compiler_params=pltpu.CompilerParams(vmem_limit_bytes=VMEM_LIMIT),
    )(place, order, owner, reach, value, error, taper, priors, states)


def to_neighbours(axis, lower, upper):
    count = lax.axis_size(axis)
    forward = [(i, i + 1) for i in range(count - 1)]
    backward = [(target, source) for source, target in forward]
    return lax.ppermute(upper, axis, forward), lax.ppermute(lower, axis, backward)


def swap_pairs(x, axis, start):
    pairs = [(i, i + 1) for i in range(start, lax.axis_size(axis) - 1, 2)]
    return lax.ppermute(x, axis, pairs + [(b, a) for a, b in pairs])


def add_over(x, axes):
    for axis in axes:
        count = lax.axis_size(axis)
        if count & (count - 1):
            x = lax.psum(x, axis)
            continue
        span = 1
        while span < count:
            x = x + lax.ppermute(x, axis, [(i, i ^ span) for i in range(count)])
            span *= 2
    return x


def body(status, drag, value, error, taper, order, owner, cell, reach):
    members, rows, cols = status.shape[1:]
    ix, iy = lax.axis_index("gx"), lax.axis_index("gy")
    size_x, size_y = lax.axis_size("gx"), lax.axis_size("gy")
    place = jnp.stack(
        [
            ix * size_y + iy,
            (ix == 0).astype(jnp.int32),
            (ix == size_x - 1).astype(jnp.int32),
            (iy == 0).astype(jnp.int32),
            (iy == size_y - 1).astype(jnp.int32),
            jnp.int32(size_y),
        ]
    ).astype(jnp.int32)
    flat = status.reshape(3 * members * rows, cols)
    lower, upper = bands(flat, members, rows)
    above, below = to_neighbours("gy", lower, upper)
    even, odd = pack(place, flat, drag, members)
    even, odd = swap_pairs(even, "gx", 0), swap_pairs(odd, "gx", 1)
    left, right, margin, even, odd = corner(place, drag, even, odd)
    inner = interior(place, flat, left, right, drag, margin, members)
    even, odd, inner = lax.optimization_barrier((even, odd, inner))
    even, odd = swap_pairs(even, "gy", 0), swap_pairs(odd, "gy", 1)
    states, priors = forecast(place, order, owner, cell, inner, above, below, even, odd, drag, margin)
    priors = add_over(priors, ("gx", "gy"))
    result = assimilate(place, order, owner, reach, value, error, taper, priors, states, members, rows)
    return result.reshape(status.shape)


def solution(mesh):
    in_specs = (P(None, None, "gy", "gx"), P("gy", "gx"), P(), P(), P(), P(), P(), P(), P())
    out_specs = P(None, None, "gy", "gx")
    return jax.shard_map(body, mesh=mesh, in_specs=in_specs, out_specs=out_specs, check_vma=False)
```

```python
import functools

import jax
import jax.numpy as jnp
from jax import lax
from jax.experimental import pallas as pl
from jax.experimental.pallas import tpu as pltpu
from jax.sharding import PartitionSpec as P

STEPS = 4
MARGIN = 2 * STEPS
EPS = 1e-06
NT = (((1,), (1,)), ((), ()))
HIGHEST = lax.Precision.HIGHEST
F32 = jnp.float32
BF16 = jnp.bfloat16
VMEM_LIMIT = 24 * 1024 * 1024
GROUP = 40
AHEAD = 3

VSPEC = pl.BlockSpec(memory_space=pltpu.VMEM)
SSPEC = pl.BlockSpec(memory_space=pltpu.SMEM)


def lanes_of(shape):
    return lax.broadcasted_iota(jnp.int32, shape, len(shape) - 1)


def sublanes_of(shape):
    return lax.broadcasted_iota(jnp.int32, shape, len(shape) - 2)


def roll_lanes(x, shift):
    size = x.shape[-1]
    shift = shift % size
    return x if shift == 0 else pltpu.roll(x, shift, x.ndim - 1)


def band_kernel(members, rows, x_hbm, lower_hbm, upper_hbm, x_ref, lower_ref, upper_ref, sems):
    def arrive(f):
        field = pl.ds(f * members * rows, members * rows)
        return pltpu.make_async_copy(x_hbm.at[field], x_ref.at[field], sems.at[0, f])

    def leave(f, side):
        source, target = ((lower_ref, lower_hbm), (upper_ref, upper_hbm))[side]
        here = pl.ds(f * (MARGIN - 1), MARGIN if f == 2 else MARGIN - 1)
        return pltpu.make_async_copy(source.at[here], target.at[here], sems.at[1 + side, f])

    for f in range(3):
        arrive(f).start()
    for f in range(3):
        arrive(f).wait()
        depth = MARGIN if f == 2 else MARGIN - 1
        for d in range(depth):
            at = f * members * rows + d
            lower_ref[f * (MARGIN - 1) + d] = x_ref[pl.ds(at, members, stride=rows), :]
            upper_ref[f * (MARGIN - 1) + d] = x_ref[pl.ds(at + rows - depth, members, stride=rows), :]
        leave(f, 0).start()
        leave(f, 1).start()
    for f in range(3):
        leave(f, 0).wait()
        leave(f, 1).wait()


def bands(x, members, rows):
    cols = x.shape[1]
    shape = (3 * MARGIN - 2, members, cols)
    return pl.pallas_call(
        functools.partial(band_kernel, members, rows),
        out_shape=(jax.ShapeDtypeStruct(shape, F32),) * 2,
        in_specs=[pl.BlockSpec(memory_space=pltpu.HBM)],
        out_specs=(pl.BlockSpec(memory_space=pl.ANY),) * 2,
        scratch_shapes=[pltpu.VMEM(x.shape, F32)] + [pltpu.VMEM(shape, F32)] * 2 + [pltpu.SemaphoreType.DMA((3, 3))],
        compiler_params=pltpu.CompilerParams(vmem_limit_bytes=60 * 1024 * 1024),
        cost_estimate=pl.CostEstimate(flops=1_000_000, bytes_accessed=4_000_000, transcendentals=0),
    )(x)


def pack_kernel(members, rows, place_ref, x_ref, drag_ref, even_ref, odd_ref):
    cols = x_ref.shape[1]
    lane = lanes_of((8, cols))
    slot = lane // MARGIN
    odd_x = place_ref[0] // place_ref[5] % 2 == 1

    def group(g, carry):
        for f in range(3):
            row = [x_ref[pl.ds((f * members + g * 8) * rows + r, 8, stride=rows), :] for r in range(rows)]
            left, right = row[rows - 1], roll_lanes(row[rows - 1], MARGIN * rows)
            for r in range(rows - 1):
                both = roll_lanes(jnp.where(lane < cols // 2, row[rows - 2 - r], row[r]), MARGIN * (r + 1))
                left = jnp.where(slot == r + 1, both, left)
                right = jnp.where(slot == r, both, right)
            at = pl.ds(pl.multiple_of(f * members + g * 8, 8), 8)
            even_ref[at, :] = jnp.where(odd_x, left, right)
            odd_ref[at, :] = jnp.where(odd_x, right, left)
        return carry

    lax.fori_loop(0, members // 8, group, 0)
    even_ref[3 * members :, :] = drag_ref[...]
    odd_ref[3 * members :, :] = drag_ref[...]


def pack(place, x, drag, members):
    rows, cols = drag.shape
    message = jax.ShapeDtypeStruct((3 * members + rows, cols), F32)
    return pl.pallas_call(
        functools.partial(pack_kernel, members, rows),
        out_shape=(message, message),
        in_specs=[SSPEC, VSPEC, VSPEC],
        out_specs=(VSPEC,) * 2,
        compiler_params=pltpu.CompilerParams(vmem_limit_bytes=VMEM_LIMIT),
        cost_estimate=pl.CostEstimate(flops=1_000_000, bytes_accessed=4_000_000, transcendentals=0),
    )(place, x, drag)


def corner_kernel(place_ref, drag_ref, even_ref, odd_ref, left_ref, right_ref, margin_ref, even_out, odd_out):
    count, cols = left_ref.shape
    rows = drag_ref.shape[0]
    half = cols // 2
    odd_y = place_ref[0] % place_ref[5] % 2 == 1
    odd_x = place_ref[0] // place_ref[5] % 2 == 1
    even, odd = even_ref[...], odd_ref[...]
    left, right = jnp.where(odd_x, even, odd), jnp.where(odd_x, odd, even)
    margin = jnp.where(lanes_of((rows, cols)) < half, right[count:], left[count:])
    margin_ref[...] = margin
    left, right = left[:count], right[:count]
    left_ref[...] = left
    right_ref[...] = right
    lane = lanes_of((count, cols))
    slot, column = lane % half // MARGIN, lane % MARGIN
    mine = column > jnp.where(lane < half, slot, MARGIN - 1 - slot)
    both = jnp.where(mine, left, roll_lanes(right, half))
    count = count // 2
    head, tail = both[:count], both[count:]
    first_half = lanes_of((count, cols)) < half
    lower = jnp.where(first_half, head, roll_lanes(tail, half))
    upper = jnp.where(first_half, roll_lanes(head, half), tail)
    even_out[:count, :] = jnp.where(odd_y, lower, upper)
    odd_out[:count, :] = jnp.where(odd_y, upper, lower)
    drag = drag_ref[...]
    for at, part in ((count, drag), (count + MARGIN, margin)):
        lower, upper = part[:MARGIN], part[rows - MARGIN :]
        even_out[at : at + MARGIN, :] = jnp.where(odd_y, lower, upper)
        odd_out[at : at + MARGIN, :] = jnp.where(odd_y, upper, lower)


def corner(place, drag, even, odd):
    rows, cols = drag.shape
    count = even.shape[0] - rows
    edge = jax.ShapeDtypeStruct((count, cols), F32)
    message = jax.ShapeDtypeStruct((count // 2 + 2 * MARGIN, cols), F32)
    return pl.pallas_call(
        corner_kernel,
        out_shape=(edge, edge, jax.ShapeDtypeStruct((rows, cols), F32), message, message),
        in_specs=[SSPEC] + [VSPEC] * 3,
        out_specs=(VSPEC,) * 5,
        compiler_params=pltpu.CompilerParams(vmem_limit_bytes=VMEM_LIMIT),
    )(place, drag, even, odd)


def grid_factor(place_ref, shape, rows, cols):
    row, col = sublanes_of(shape), lanes_of(shape)
    wide = 2 * cols
    low, high = jnp.where(place_ref[3] == 1, MARGIN, 0), jnp.where(place_ref[4] == 1, MARGIN + rows, rows + 2 * MARGIN)
    first, last = jnp.where(place_ref[1] == 1, wide, wide - MARGIN), jnp.where(place_ref[2] == 1, cols, cols + MARGIN)
    ok = (row >= low) & (row < high) & ((col < last) | (col >= first))
    return jnp.where(ok, 1.0, 0.0)


def wide_row(lane, main, left, left_at, right, right_at):
    cols = main.shape[1]
    halo = jnp.where(lane >= cols - MARGIN, roll_lanes(left, cols - MARGIN - left_at), 0.0)
    halo = jnp.where(lane < MARGIN, roll_lanes(right, -right_at), halo)
    return jnp.concatenate([main, halo], axis=1)


def shift_matrix(wide):
    source, target = sublanes_of((wide, wide)), lanes_of((wide, wide))
    after, before = source == (target + 1) % wide, target == (source + 1) % wide
    return jnp.where(after, 1.0, jnp.where(before, -1.0, 0.0)).astype(BF16)


def tall(x):
    return jnp.concatenate([x] * (GROUP // 8), axis=0)


def column_slope(x, shift):
    rows, group, wide = x.shape
    x = x.reshape(rows * group, wide)
    top = x.astype(BF16)
    rest = (x - top.astype(F32)).astype(BF16)
    slope = jnp.dot(top, shift, preferred_element_type=F32) + jnp.dot(rest, shift, preferred_element_type=F32)
    return slope.reshape(rows, group, wide)


def interior_kernel(members, rows, place_ref, x_ref, left_ref, right_ref, drag_ref, margin_ref, state, keep, slope):
    cols = x_ref.shape[1]
    wide = 2 * cols
    lane = lanes_of((8, cols))
    factor = -0.2 * grid_factor(place_ref, (rows + 2 * MARGIN, wide), rows, cols)
    shift = shift_matrix(wide)
    kept = 1.0 - jnp.concatenate([drag_ref[...], margin_ref[...]], axis=1)
    for r in range(rows):
        keep[r] = jnp.broadcast_to(kept[r : r + 1, :], (8, wide))
        slope[r] = jnp.broadcast_to(factor[MARGIN + r : MARGIN + r + 1, :], (8, wide))

    def first(g, carry):
        here = pl.ds(pl.multiple_of(g * 8, 8), 8)
        for f in range(3):
            at = pl.ds(pl.multiple_of(f * members + g * 8, 8), 8)
            left, right = left_ref[at, :], right_ref[at, :]
            for r in range(rows):
                main = x_ref[pl.ds((f * members + g * 8) * rows + r, 8, stride=rows), :]
                state[f, r, here, :] = wide_row(lane, main, left, MARGIN * r, right, MARGIN * (rows - 1 - r))
        return carry

    lax.fori_loop(0, members // 8, first, 0)

    groups = [pl.ds(m, GROUP) for m in range(0, members, GROUP)]
    for step in range(AHEAD):
        low, high = 1 + 2 * step, rows - 1 - 2 * step
        if low >= high:
            break
        for here in groups:
            d = column_slope(state[1, low:high, here, :], shift)
            for r in range(low, high):
                div = d[r - low] + (state[2, r + 1, here, :] - state[2, r - 1, here, :])
                state[0, r, here, :] = state[0, r, here, :] + tall(slope[r]) * div
        low, high = low + 1, high - 1
        if low >= high:
            break
        for here in groups:
            d = column_slope(state[0, low:high, here, :], shift)
            for r in range(low, high):
                u, v = state[1, r, here, :], state[2, r, here, :]
                k, c = tall(keep[r]), tall(slope[r])
                state[1, r, here, :] = k * u + c * d[r - low] + 0.1 * v
                state[2, r, here, :] = k * v + c * (state[0, r + 1, here, :] - state[0, r - 1, here, :]) - 0.1 * u


def interior(place, x, left, right, drag, margin, members):
    rows, cols = drag.shape
    return pl.pallas_call(
        functools.partial(interior_kernel, members, rows),
        out_shape=jax.ShapeDtypeStruct((3, rows, members, 2 * cols), F32),
        in_specs=[SSPEC] + [VSPEC] * 5,
        out_specs=VSPEC,
        scratch_shapes=[pltpu.VMEM((rows, 8, 2 * cols), F32)] * 2,
        compiler_params=pltpu.CompilerParams(vmem_limit_bytes=VMEM_LIMIT),
        cost_estimate=pl.CostEstimate(flops=30_000_000, bytes_accessed=10_000_000, transcendentals=0),
    )(place, x, left, right, drag, margin)


def forecast_kernel(
    members, rows,
    place_ref, order_ref, owner_ref, cell_ref,
    inner_ref, above_ref, below_ref, ceven_ref, codd_ref, drag_ref, margin_ref,
    out_ref, prior_ref,
    state, keep, slope,
):
    cols = above_ref.shape[2]
    wide = 2 * cols
    total = rows + 2 * MARGIN
    half = cols // 2
    lane = lanes_of((GROUP, cols))
    factor = -0.2 * grid_factor(place_ref, (total, wide), rows, cols)
    odd_y = place_ref[0] % place_ref[5] % 2 == 1
    shift = shift_matrix(wide)
    count = 3 * members // 2
    parts = []
    for here, own in ((count, drag_ref), (count + MARGIN, margin_ref)):
        even, odd = ceven_ref[here : here + MARGIN, :], codd_ref[here : here + MARGIN, :]
        above, below = jnp.where(odd_y, even, odd), jnp.where(odd_y, odd, even)
        parts.append(jnp.concatenate([above, own[...], below], axis=0))
    kept = 1.0 - jnp.concatenate(parts, axis=1)
    for r in range(total):
        keep[r] = jnp.broadcast_to(kept[r : r + 1, :], (8, wide))
        slope[r] = jnp.broadcast_to(factor[r : r + 1, :], (8, wide))

    groups = range(members // GROUP)
    for g in groups:
        here = pl.ds(g * GROUP, GROUP)
        for f in range(3):
            at = f * members + g * GROUP
            base = half if at >= count else 0
            at = pl.ds(at % count, GROUP)
            ceven, codd = ceven_ref[at, :], codd_ref[at, :]
            cab, cbe = jnp.where(odd_y, ceven, codd), jnp.where(odd_y, codd, ceven)
            depth = MARGIN if f == 2 else MARGIN - 1
            for d in range(depth):
                r = MARGIN - depth + d
                main = above_ref[f * (MARGIN - 1) + d, here, :]
                state[g, f, r] = wide_row(lane, main, cab, base + MARGIN * r, cab, base + MARGIN * (MARGIN - 1 - r))
                main = below_ref[f * (MARGIN - 1) + d, here, :]
                state[g, f, MARGIN + rows + d] = wide_row(
                    lane, main, cbe, base + MARGIN * d, cbe, base + MARGIN * (MARGIN - 1 - d)
                )
            for r in range(rows):
                state[g, f, MARGIN + r] = inner_ref[f, r, here, :]

    def heights(g, spans):
        for low, high in spans:
            d = column_slope(state[g, 1, low:high], shift)
            for r in range(low, high):
                div = d[r - low] + (state[g, 2, r + 1] - state[g, 2, r - 1])
                state[g, 0, r] = state[g, 0, r] + tall(slope[r]) * div

    def flows(g, spans, final):
        here = pl.ds(g * GROUP, GROUP)
        for low, high in spans:
            d = column_slope(state[g, 0, low:high], shift)
            for r in range(low, high):
                u, v = state[g, 1, r], state[g, 2, r]
                k, c = tall(keep[r]), tall(slope[r])
                u, v = (
                    k * u + c * d[r - low] + 0.1 * v,
                    k * v + c * (state[g, 0, r + 1] - state[g, 0, r - 1]) - 0.1 * u,
                )
                if final:
                    for f, value in enumerate((state[g, 0, r], u, v)):
                        out_ref[f * rows + r - MARGIN, here, :] = value[:, 0:cols]
                else:
                    state[g, 1, r] = u
                    state[g, 2, r] = v

    for step in range(STEPS):
        first, last = MARGIN - MARGIN + 1 + 2 * step, MARGIN + rows + MARGIN - 1 - 2 * step
        done, still = MARGIN + 1 + 2 * step, MARGIN + rows - 1 - 2 * step
        if step >= AHEAD:
            done = still = MARGIN + rows // 2
        for g in groups:
            heights(g, ((first, done), (still, last)))
        for g in groups:
            flows(g, ((first + 1, done + (step < AHEAD)), (still - (step < AHEAD), last - 1)), step == STEPS - 1)
    prior_ref[...] = jnp.zeros_like(prior_ref)
    eight = lanes_of((8, cols))
    for i in range(order_ref.shape[0]):
        which = order_ref[i]

        @pl.when(owner_ref[which] == place_ref[0])
        def _():
            cell = cell_ref[which]
            one = jnp.where(eight == cell % cols, 1.0, 0.0)
            prior_ref[i : i + 1, 0:members] = lax.dot_general(
                one, out_ref[cell // cols], NT, precision=HIGHEST, preferred_element_type=F32
            )[0:1]


def forecast(place, order, owner, cell, inner, *arrays):
    _, rows, members, wide = inner.shape
    cols = wide // 2
    total = rows + 2 * MARGIN
    return pl.pallas_call(
        functools.partial(forecast_kernel, members, rows),
        out_shape=(
            jax.ShapeDtypeStruct((3 * rows, members, cols), F32),
            jax.ShapeDtypeStruct((order.shape[0], cols), F32),
        ),
        in_specs=[SSPEC] * 4 + [VSPEC] * (1 + len(arrays)),
        out_specs=(VSPEC, VSPEC),
        scratch_shapes=[pltpu.VMEM((members // GROUP, 3, total, GROUP, wide), F32)] + [pltpu.VMEM((total, 8, wide), F32)] * 2,
        compiler_params=pltpu.CompilerParams(vmem_limit_bytes=VMEM_LIMIT),
        cost_estimate=pl.CostEstimate(flops=60_000_000, bytes_accessed=30_000_000, transcendentals=0),
    )(place, order, owner, cell, inner, *arrays)


def localize(distance, reach, taper_ref):
    picked = jnp.zeros(distance.shape, F32)
    levels = taper_ref.shape[0]
    capped = jnp.minimum(distance, levels - 1)
    for d in range(levels):
        picked = jnp.where(capped == d, taper_ref[d], picked)
    return jnp.where(distance <= reach, picked, 0.0)


def assimilate_kernel(
    members, rows,
    place_ref, order_ref, owner_ref, reach_ref, value_ref, error_ref, taper_ref,
    prior_ref, forecast_ref,
    result_ref,
    out_ref, sems,
):
    n_obs = order_ref.shape[0]
    cols = prior_ref.shape[1]
    size_y = place_ref[5]
    lane1 = lanes_of((1, cols))
    lane = lanes_of((n_obs, cols))
    sub = sublanes_of((n_obs, cols))

    tile_row = jnp.zeros((1, cols), jnp.int32)
    tile_col = jnp.zeros((n_obs, cols), jnp.int32)
    reach_row = jnp.zeros((1, cols), jnp.int32)
    reach_col = jnp.zeros((n_obs, cols), jnp.int32)
    which = [order_ref[i] for i in range(n_obs)]
    for i, k in enumerate(which):
        tile_row = jnp.where(lane1 == i, owner_ref[k], tile_row)
        tile_col = jnp.where(sub == i, owner_ref[k], tile_col)
        reach_row = jnp.where(lane1 == i, reach_ref[k], reach_row)
        reach_col = jnp.where(sub == i, reach_ref[k], reach_col)
    rx, ry = tile_row // size_y, tile_row % size_y
    cx, cy = tile_col // size_y, tile_col % size_y
    distance = jnp.maximum(jnp.abs(cx - rx), jnp.abs(cy - ry))
    onto = localize(distance, reach_row, taper_ref)
    onto_t = localize(distance, reach_col, taper_ref)
    mine = place_ref[0]
    own = localize(
        jnp.maximum(jnp.abs(mine // size_y - rx), jnp.abs(mine % size_y - ry)), reach_row, taper_ref
    )

    priors = prior_ref[...]
    inside = lane < members
    mean_col = jnp.sum(jnp.where(inside, priors, 0.0), axis=1, keepdims=True) / members
    anomalies = jnp.where(inside, priors - mean_col, 0.0)
    padded = jnp.concatenate([anomalies, jnp.zeros((cols - n_obs, cols), F32)], axis=0)
    table = lax.dot_general(anomalies, padded, NT, precision=HIGHEST, preferred_element_type=F32)
    table = jnp.concatenate([table, jnp.transpose(padded)[:members]], axis=0)
    mean = jnp.zeros((1, cols), F32)
    for i in range(n_obs):
        mean = jnp.where(lane1 == i, mean_col[i : i + 1, :], mean)

    scales = jnp.zeros((1, cols), F32)
    increments = []
    power = jnp.broadcast_to(table[0:1, 0:1], (1, cols))
    for i, k in enumerate(which):
        error = error_ref[k]
        row = table[i : i + 1, :]
        column = jnp.broadcast_to(table[:, i : i + 1], table.shape)
        variance = power / (members - 1) + EPS
        root = lax.rsqrt(1.0 + variance * (1.0 / error))
        scaled = 1.0 / ((members - 1) * variance)
        shift = variance * (value_ref[k] - jnp.broadcast_to(mean[:, i : i + 1], row.shape)) * (root * root * (1.0 / error))
        shrink = root - 1.0
        weight = scaled * jnp.broadcast_to(own[:, i : i + 1], row.shape)
        alpha_row = onto_t[i : i + 1, :] * row * scaled
        later = lane1 > i
        h = jnp.where(later, shrink * alpha_row, 0.0)
        q = jnp.where(later, shrink * (row + h * power), 0.0)
        alpha = jnp.concatenate(
            [jnp.broadcast_to(onto[:, i : i + 1], onto.shape) * column[:n_obs] * scaled, column[n_obs:] * weight], axis=0
        )
        if i + 1 < n_obs:
            beside, ahead, reach_on = (
                jnp.broadcast_to(x[:, i + 1 : i + 2], row.shape)
                for x in (row, table[i + 1 : i + 2, :], onto_t[i : i + 1, :])
            )
            step = reach_on * beside * scaled
            power = ahead + beside * (shrink * step) + step * (shrink * (beside + shrink * step * power))
        table = table + column * h + alpha * q
        mean = mean + alpha_row * shift
        now = anomalies[i : i + 1, :]
        increments.append(shift + shrink * now)
        anomalies = anomalies + jnp.where(sub > i, shrink * alpha[:n_obs], 0.0) * now
        scales = jnp.where(lane1 == i, weight, scales)
    left = table[n_obs:, :] * scales
    right = jnp.where(inside, jnp.concatenate(increments, axis=0), 0.0)
    right = jnp.concatenate([right, jnp.zeros((cols - n_obs, cols), F32)], axis=0)
    change = jnp.dot(left, right, precision=HIGHEST, preferred_element_type=F32)
    change = jnp.concatenate([change, jnp.zeros((cols - members, cols), F32)], axis=0)
    change = jnp.transpose(change)[:members, :]
    high = change.astype(BF16).astype(F32)
    low = change - high
    zero = jnp.zeros((members, cols), F32)
    high = jnp.concatenate([high, zero], axis=1)
    low = jnp.concatenate([low, zero], axis=1)
    factor = (high + roll_lanes(high, members) + roll_lanes(low, 2 * members)).astype(BF16)

    block = 4
    for at in range(0, 3 * rows, block):
        x = jnp.concatenate([forecast_ref[at + b] for b in range(block)], axis=1)
        xh = x.astype(BF16)
        xl = (x - xh.astype(F32)).astype(BF16)
        stack = jnp.concatenate([xh, xl, xh, jnp.zeros((2 * cols - 3 * members, block * cols), BF16)], axis=0)
        y = x + jnp.dot(factor, stack, preferred_element_type=F32)
        for b in range(block):
            f, r = divmod(at + b, rows)
            out_ref[pl.ds(f * members * rows + r, members, stride=rows), :] = y[:, b * cols : (b + 1) * cols]
        if (at + block) % rows == 0:
            field = pl.ds(at // rows * members * rows, members * rows)
            pltpu.make_async_copy(out_ref.at[field], result_ref.at[field], sems.at[at // rows]).start()
    for f in range(3):
        field = pl.ds(f * members * rows, members * rows)
        pltpu.make_async_copy(out_ref.at[field], result_ref.at[field], sems.at[f]).wait()


def assimilate(place, order, owner, reach, value, error, taper, priors, states, members, rows):
    cols = priors.shape[1]
    return pl.pallas_call(
        functools.partial(assimilate_kernel, members, rows),
        out_shape=jax.ShapeDtypeStruct((3 * members * rows, cols), F32),
        in_specs=[SSPEC] * 7 + [VSPEC] * 2,
        out_specs=pl.BlockSpec(memory_space=pl.ANY),
        scratch_shapes=[pltpu.VMEM((3 * members * rows, cols), F32), pltpu.SemaphoreType.DMA((3,))],
        compiler_params=pltpu.CompilerParams(vmem_limit_bytes=VMEM_LIMIT),
    )(place, order, owner, reach, value, error, taper, priors, states)


def to_neighbours(axis, lower, upper):
    count = lax.axis_size(axis)
    forward = [(i, i + 1) for i in range(count - 1)]
    backward = [(target, source) for source, target in forward]
    return lax.ppermute(upper, axis, forward), lax.ppermute(lower, axis, backward)


def swap_pairs(x, axis, start):
    pairs = [(i, i + 1) for i in range(start, lax.axis_size(axis) - 1, 2)]
    return lax.ppermute(x, axis, pairs + [(b, a) for a, b in pairs])


def add_over(x, axes):
    for axis in axes:
        count = lax.axis_size(axis)
        if count & (count - 1):
            x = lax.psum(x, axis)
            continue
        span = 1
        while span < count:
            x = x + lax.ppermute(x, axis, [(i, i ^ span) for i in range(count)])
            span *= 2
    return x


def body(status, drag, value, error, taper, order, owner, cell, reach):
    members, rows, cols = status.shape[1:]
    ix, iy = lax.axis_index("gx"), lax.axis_index("gy")
    size_x, size_y = lax.axis_size("gx"), lax.axis_size("gy")
    place = jnp.stack(
        [
            ix * size_y + iy,
            (ix == 0).astype(jnp.int32),
            (ix == size_x - 1).astype(jnp.int32),
            (iy == 0).astype(jnp.int32),
            (iy == size_y - 1).astype(jnp.int32),
            jnp.int32(size_y),
        ]
    ).astype(jnp.int32)
    flat = status.reshape(3 * members * rows, cols)
    lower, upper = bands(flat, members, rows)
    above, below = to_neighbours("gy", lower, upper)
    even, odd = pack(place, flat, drag, members)
    even, odd = swap_pairs(even, "gx", 0), swap_pairs(odd, "gx", 1)
    left, right, margin, even, odd = corner(place, drag, even, odd)
    even, odd = swap_pairs(even, "gy", 0), swap_pairs(odd, "gy", 1)
    inner = interior(place, flat, left, right, drag, margin, members)
    states, priors = forecast(place, order, owner, cell, inner, above, below, even, odd, drag, margin)
    priors = add_over(priors, ("gx", "gy"))
    result = assimilate(place, order, owner, reach, value, error, taper, priors, states, members, rows)
    return result.reshape(status.shape)


def solution(mesh):
    in_specs = (P(None, None, "gy", "gx"), P("gy", "gx"), P(), P(), P(), P(), P(), P(), P())
    out_specs = P(None, None, "gy", "gx")
    return jax.shard_map(body, mesh=mesh, in_specs=in_specs, out_specs=out_specs, check_vma=False)
```

```python
import functools

import jax
import jax.numpy as jnp
from jax import lax
from jax.experimental import pallas as pl
from jax.experimental.pallas import tpu as pltpu
from jax.sharding import PartitionSpec as P

STEPS = 4
MARGIN = 2 * STEPS
EPS = 1e-06
NT = (((1,), (1,)), ((), ()))
HIGHEST = lax.Precision.HIGHEST
F32 = jnp.float32
BF16 = jnp.bfloat16
VMEM_LIMIT = 24 * 1024 * 1024
GROUP = 40

VSPEC = pl.BlockSpec(memory_space=pltpu.VMEM)
SSPEC = pl.BlockSpec(memory_space=pltpu.SMEM)


def lanes_of(shape):
    return lax.broadcasted_iota(jnp.int32, shape, len(shape) - 1)


def sublanes_of(shape):
    return lax.broadcasted_iota(jnp.int32, shape, len(shape) - 2)


def roll_lanes(x, shift):
    size = x.shape[-1]
    shift = shift % size
    return x if shift == 0 else pltpu.roll(x, shift, x.ndim - 1)


def band_kernel(members, rows, x_hbm, lower_hbm, upper_hbm, x_ref, lower_ref, upper_ref, sems):
    def arrive(f):
        field = pl.ds(f * members * rows, members * rows)
        return pltpu.make_async_copy(x_hbm.at[field], x_ref.at[field], sems.at[0, f])

    def leave(f, side):
        source, target = ((lower_ref, lower_hbm), (upper_ref, upper_hbm))[side]
        here = pl.ds(f * (MARGIN - 1), MARGIN if f == 2 else MARGIN - 1)
        return pltpu.make_async_copy(source.at[here], target.at[here], sems.at[1 + side, f])

    for f in range(3):
        arrive(f).start()
    for f in range(3):
        arrive(f).wait()
        depth = MARGIN if f == 2 else MARGIN - 1
        for d in range(depth):
            at = f * members * rows + d
            lower_ref[f * (MARGIN - 1) + d] = x_ref[pl.ds(at, members, stride=rows), :]
            upper_ref[f * (MARGIN - 1) + d] = x_ref[pl.ds(at + rows - depth, members, stride=rows), :]
        leave(f, 0).start()
        leave(f, 1).start()
    for f in range(3):
        leave(f, 0).wait()
        leave(f, 1).wait()


def bands(x, members, rows):
    cols = x.shape[1]
    shape = (3 * MARGIN - 2, members, cols)
    return pl.pallas_call(
        functools.partial(band_kernel, members, rows),
        out_shape=(jax.ShapeDtypeStruct(shape, F32),) * 2,
        in_specs=[pl.BlockSpec(memory_space=pltpu.HBM)],
        out_specs=(pl.BlockSpec(memory_space=pl.ANY),) * 2,
        scratch_shapes=[pltpu.VMEM(x.shape, F32)] + [pltpu.VMEM(shape, F32)] * 2 + [pltpu.SemaphoreType.DMA((3, 3))],
        compiler_params=pltpu.CompilerParams(vmem_limit_bytes=60 * 1024 * 1024),
        cost_estimate=pl.CostEstimate(flops=1_000_000, bytes_accessed=4_000_000, transcendentals=0),
    )(x)


def pack_kernel(members, rows, place_ref, x_ref, drag_ref, even_ref, odd_ref):
    cols = x_ref.shape[1]
    lane = lanes_of((8, cols))
    slot = lane // MARGIN
    odd_x = place_ref[0] // place_ref[5] % 2 == 1

    def group(g, carry):
        for f in range(3):
            row = [x_ref[pl.ds((f * members + g * 8) * rows + r, 8, stride=rows), :] for r in range(rows)]
            left, right = row[rows - 1], roll_lanes(row[rows - 1], MARGIN * rows)
            for r in range(rows - 1):
                both = roll_lanes(jnp.where(lane < cols // 2, row[rows - 2 - r], row[r]), MARGIN * (r + 1))
                left = jnp.where(slot == r + 1, both, left)
                right = jnp.where(slot == r, both, right)
            at = pl.ds(pl.multiple_of(f * members + g * 8, 8), 8)
            even_ref[at, :] = jnp.where(odd_x, left, right)
            odd_ref[at, :] = jnp.where(odd_x, right, left)
        return carry

    lax.fori_loop(0, members // 8, group, 0)
    even_ref[3 * members :, :] = drag_ref[...]
    odd_ref[3 * members :, :] = drag_ref[...]


def pack(place, x, drag, members):
    rows, cols = drag.shape
    message = jax.ShapeDtypeStruct((3 * members + rows, cols), F32)
    return pl.pallas_call(
        functools.partial(pack_kernel, members, rows),
        out_shape=(message, message),
        in_specs=[SSPEC, VSPEC, VSPEC],
        out_specs=(VSPEC,) * 2,
        compiler_params=pltpu.CompilerParams(vmem_limit_bytes=VMEM_LIMIT),
        cost_estimate=pl.CostEstimate(flops=1_000_000, bytes_accessed=4_000_000, transcendentals=0),
    )(place, x, drag)


def corner_kernel(place_ref, drag_ref, even_ref, odd_ref, left_ref, right_ref, margin_ref, even_out, odd_out):
    count, cols = left_ref.shape
    rows = drag_ref.shape[0]
    half = cols // 2
    odd_y = place_ref[0] % place_ref[5] % 2 == 1
    odd_x = place_ref[0] // place_ref[5] % 2 == 1
    even, odd = even_ref[...], odd_ref[...]
    left, right = jnp.where(odd_x, even, odd), jnp.where(odd_x, odd, even)
    margin = jnp.where(lanes_of((rows, cols)) < half, right[count:], left[count:])
    margin_ref[...] = margin
    left, right = left[:count], right[:count]
    left_ref[...] = left
    right_ref[...] = right
    lane = lanes_of((count, cols))
    slot, column = lane % half // MARGIN, lane % MARGIN
    mine = column > jnp.where(lane < half, slot, MARGIN - 1 - slot)
    both = jnp.where(mine, left, roll_lanes(right, half))
    count = count // 2
    head, tail = both[:count], both[count:]
    first_half = lanes_of((count, cols)) < half
    lower = jnp.where(first_half, head, roll_lanes(tail, half))
    upper = jnp.where(first_half, roll_lanes(head, half), tail)
    even_out[:count, :] = jnp.where(odd_y, lower, upper)
    odd_out[:count, :] = jnp.where(odd_y, upper, lower)
    drag = drag_ref[...]
    for at, part in ((count, drag), (count + MARGIN, margin)):
        lower, upper = part[:MARGIN], part[rows - MARGIN :]
        even_out[at : at + MARGIN, :] = jnp.where(odd_y, lower, upper)
        odd_out[at : at + MARGIN, :] = jnp.where(odd_y, upper, lower)


def corner(place, drag, even, odd):
    rows, cols = drag.shape
    count = even.shape[0] - rows
    edge = jax.ShapeDtypeStruct((count, cols), F32)
    message = jax.ShapeDtypeStruct((count // 2 + 2 * MARGIN, cols), F32)
    return pl.pallas_call(
        corner_kernel,
        out_shape=(edge, edge, jax.ShapeDtypeStruct((rows, cols), F32), message, message),
        in_specs=[SSPEC] + [VSPEC] * 3,
        out_specs=(VSPEC,) * 5,
        compiler_params=pltpu.CompilerParams(vmem_limit_bytes=VMEM_LIMIT),
    )(place, drag, even, odd)


def grid_factor(place_ref, shape, rows, cols):
    row, col = sublanes_of(shape), lanes_of(shape)
    wide = 2 * cols
    low, high = jnp.where(place_ref[3] == 1, MARGIN, 0), jnp.where(place_ref[4] == 1, MARGIN + rows, rows + 2 * MARGIN)
    first, last = jnp.where(place_ref[1] == 1, wide, wide - MARGIN), jnp.where(place_ref[2] == 1, cols, cols + MARGIN)
    ok = (row >= low) & (row < high) & ((col < last) | (col >= first))
    return jnp.where(ok, 1.0, 0.0)


def wide_row(lane, main, left, left_at, right, right_at):
    cols = main.shape[1]
    halo = jnp.where(lane >= cols - MARGIN, roll_lanes(left, cols - MARGIN - left_at), 0.0)
    halo = jnp.where(lane < MARGIN, roll_lanes(right, -right_at), halo)
    return jnp.concatenate([main, halo], axis=1)


def shift_matrix(wide):
    source, target = sublanes_of((wide, wide)), lanes_of((wide, wide))
    after, before = source == (target + 1) % wide, target == (source + 1) % wide
    return jnp.where(after, 1.0, jnp.where(before, -1.0, 0.0)).astype(BF16)


def tall(x):
    return jnp.concatenate([x] * (GROUP // 8), axis=0)


def column_slope(x, shift):
    rows, group, wide = x.shape
    x = x.reshape(rows * group, wide)
    top = x.astype(BF16)
    rest = (x - top.astype(F32)).astype(BF16)
    slope = jnp.dot(top, shift, preferred_element_type=F32) + jnp.dot(rest, shift, preferred_element_type=F32)
    return slope.reshape(rows, group, wide)


def interior_kernel(members, rows, place_ref, x_ref, left_ref, right_ref, drag_ref, margin_ref, state, keep, slope):
    cols = x_ref.shape[1]
    wide = 2 * cols
    lane = lanes_of((8, cols))
    factor = -0.2 * grid_factor(place_ref, (rows + 2 * MARGIN, wide), rows, cols)
    shift = shift_matrix(wide)
    kept = 1.0 - jnp.concatenate([drag_ref[...], margin_ref[...]], axis=1)
    for r in range(rows):
        keep[r] = jnp.broadcast_to(kept[r : r + 1, :], (8, wide))
        slope[r] = jnp.broadcast_to(factor[MARGIN + r : MARGIN + r + 1, :], (8, wide))

    def first(g, carry):
        here = pl.ds(pl.multiple_of(g * 8, 8), 8)
        for f in range(3):
            at = pl.ds(pl.multiple_of(f * members + g * 8, 8), 8)
            left, right = left_ref[at, :], right_ref[at, :]
            for r in range(rows):
                main = x_ref[pl.ds((f * members + g * 8) * rows + r, 8, stride=rows), :]
                state[f, r, here, :] = wide_row(lane, main, left, MARGIN * r, right, MARGIN * (rows - 1 - r))
        return carry

    lax.fori_loop(0, members // 8, first, 0)

    groups = [pl.ds(m, GROUP) for m in range(0, members, GROUP)]
    for step in range(STEPS):
        low, high = 1 + 2 * step, rows - 1 - 2 * step
        if low >= high:
            break
        for here in groups:
            d = column_slope(state[1, low:high, here, :], shift)
            for r in range(low, high):
                div = d[r - low] + (state[2, r + 1, here, :] - state[2, r - 1, here, :])
                state[0, r, here, :] = state[0, r, here, :] + tall(slope[r]) * div
        low, high = low + 1, high - 1
        if low >= high:
            break
        for here in groups:
            d = column_slope(state[0, low:high, here, :], shift)
            for r in range(low, high):
                u, v = state[1, r, here, :], state[2, r, here, :]
                k, c = tall(keep[r]), tall(slope[r])
                state[1, r, here, :] = k * u + c * d[r - low] + 0.1 * v
                state[2, r, here, :] = k * v + c * (state[0, r + 1, here, :] - state[0, r - 1, here, :]) - 0.1 * u


def interior(place, x, left, right, drag, margin, members):
    rows, cols = drag.shape
    return pl.pallas_call(
        functools.partial(interior_kernel, members, rows),
        out_shape=jax.ShapeDtypeStruct((3, rows, members, 2 * cols), F32),
        in_specs=[SSPEC] + [VSPEC] * 5,
        out_specs=VSPEC,
        scratch_shapes=[pltpu.VMEM((rows, 8, 2 * cols), F32)] * 2,
        compiler_params=pltpu.CompilerParams(vmem_limit_bytes=VMEM_LIMIT),
        cost_estimate=pl.CostEstimate(flops=30_000_000, bytes_accessed=10_000_000, transcendentals=0),
    )(place, x, left, right, drag, margin)


def forecast_kernel(
    members, rows,
    place_ref, order_ref, owner_ref, cell_ref,
    inner_ref, above_ref, below_ref, ceven_ref, codd_ref, drag_ref, margin_ref,
    out_ref, prior_ref,
    state, keep, slope,
):
    cols = above_ref.shape[2]
    wide = 2 * cols
    total = rows + 2 * MARGIN
    half = cols // 2
    lane = lanes_of((GROUP, cols))
    factor = -0.2 * grid_factor(place_ref, (total, wide), rows, cols)
    odd_y = place_ref[0] % place_ref[5] % 2 == 1
    shift = shift_matrix(wide)
    count = 3 * members // 2
    parts = []
    for here, own in ((count, drag_ref), (count + MARGIN, margin_ref)):
        even, odd = ceven_ref[here : here + MARGIN, :], codd_ref[here : here + MARGIN, :]
        above, below = jnp.where(odd_y, even, odd), jnp.where(odd_y, odd, even)
        parts.append(jnp.concatenate([above, own[...], below], axis=0))
    kept = 1.0 - jnp.concatenate(parts, axis=1)
    for r in range(total):
        keep[r] = jnp.broadcast_to(kept[r : r + 1, :], (8, wide))
        slope[r] = jnp.broadcast_to(factor[r : r + 1, :], (8, wide))

    groups = range(members // GROUP)
    for g in groups:
        here = pl.ds(g * GROUP, GROUP)
        for f in range(3):
            at = f * members + g * GROUP
            base = half if at >= count else 0
            at = pl.ds(at % count, GROUP)
            ceven, codd = ceven_ref[at, :], codd_ref[at, :]
            cab, cbe = jnp.where(odd_y, ceven, codd), jnp.where(odd_y, codd, ceven)
            depth = MARGIN if f == 2 else MARGIN - 1
            for d in range(depth):
                r = MARGIN - depth + d
                main = above_ref[f * (MARGIN - 1) + d, here, :]
                state[g, f, r] = wide_row(lane, main, cab, base + MARGIN * r, cab, base + MARGIN * (MARGIN - 1 - r))
                main = below_ref[f * (MARGIN - 1) + d, here, :]
                state[g, f, MARGIN + rows + d] = wide_row(
                    lane, main, cbe, base + MARGIN * d, cbe, base + MARGIN * (MARGIN - 1 - d)
                )
            for r in range(rows):
                state[g, f, MARGIN + r] = inner_ref[f, r, here, :]

    def heights(g, spans):
        for low, high in spans:
            d = column_slope(state[g, 1, low:high], shift)
            for r in range(low, high):
                div = d[r - low] + (state[g, 2, r + 1] - state[g, 2, r - 1])
                state[g, 0, r] = state[g, 0, r] + tall(slope[r]) * div

    def flows(g, spans, final):
        here = pl.ds(g * GROUP, GROUP)
        for low, high in spans:
            d = column_slope(state[g, 0, low:high], shift)
            for r in range(low, high):
                u, v = state[g, 1, r], state[g, 2, r]
                k, c = tall(keep[r]), tall(slope[r])
                u, v = (
                    k * u + c * d[r - low] + 0.1 * v,
                    k * v + c * (state[g, 0, r + 1] - state[g, 0, r - 1]) - 0.1 * u,
                )
                if final:
                    for f, value in enumerate((state[g, 0, r], u, v)):
                        out_ref[f * rows + r - MARGIN, here, :] = value[:, 0:cols]
                else:
                    state[g, 1, r] = u
                    state[g, 2, r] = v

    for step in range(STEPS):
        first, last = MARGIN - MARGIN + 1 + 2 * step, MARGIN + rows + MARGIN - 1 - 2 * step
        done, still = MARGIN + 1 + 2 * step, MARGIN + rows - 1 - 2 * step
        for g in groups:
            heights(g, ((first, done), (still, last)))
        for g in groups:
            flows(g, ((first + 1, done + 1), (still - 1, last - 1)), step == STEPS - 1)
    prior_ref[...] = jnp.zeros_like(prior_ref)
    eight = lanes_of((8, cols))
    for i in range(order_ref.shape[0]):
        which = order_ref[i]

        @pl.when(owner_ref[which] == place_ref[0])
        def _():
            cell = cell_ref[which]
            one = jnp.where(eight == cell % cols, 1.0, 0.0)
            prior_ref[i : i + 1, 0:members] = lax.dot_general(
                one, out_ref[cell // cols], NT, precision=HIGHEST, preferred_element_type=F32
            )[0:1]


def forecast(place, order, owner, cell, inner, *arrays):
    _, rows, members, wide = inner.shape
    cols = wide // 2
    total = rows + 2 * MARGIN
    return pl.pallas_call(
        functools.partial(forecast_kernel, members, rows),
        out_shape=(
            jax.ShapeDtypeStruct((3 * rows, members, cols), F32),
            jax.ShapeDtypeStruct((order.shape[0], cols), F32),
        ),
        in_specs=[SSPEC] * 4 + [VSPEC] * (1 + len(arrays)),
        out_specs=(VSPEC, VSPEC),
        scratch_shapes=[pltpu.VMEM((members // GROUP, 3, total, GROUP, wide), F32)] + [pltpu.VMEM((total, 8, wide), F32)] * 2,
        compiler_params=pltpu.CompilerParams(vmem_limit_bytes=VMEM_LIMIT),
        cost_estimate=pl.CostEstimate(flops=60_000_000, bytes_accessed=30_000_000, transcendentals=0),
    )(place, order, owner, cell, inner, *arrays)


def localize(distance, reach, taper_ref):
    picked = jnp.zeros(distance.shape, F32)
    levels = taper_ref.shape[0]
    capped = jnp.minimum(distance, levels - 1)
    for d in range(levels):
        picked = jnp.where(capped == d, taper_ref[d], picked)
    return jnp.where(distance <= reach, picked, 0.0)


def assimilate_kernel(
    members, rows,
    place_ref, order_ref, owner_ref, reach_ref, value_ref, error_ref, taper_ref,
    prior_ref, forecast_ref,
    result_ref,
    out_ref, sems,
):
    n_obs = order_ref.shape[0]
    cols = prior_ref.shape[1]
    size_y = place_ref[5]
    lane1 = lanes_of((1, cols))
    lane = lanes_of((n_obs, cols))
    sub = sublanes_of((n_obs, cols))

    tile_row = jnp.zeros((1, cols), jnp.int32)
    tile_col = jnp.zeros((n_obs, cols), jnp.int32)
    reach_row = jnp.zeros((1, cols), jnp.int32)
    reach_col = jnp.zeros((n_obs, cols), jnp.int32)
    which = [order_ref[i] for i in range(n_obs)]
    for i, k in enumerate(which):
        tile_row = jnp.where(lane1 == i, owner_ref[k], tile_row)
        tile_col = jnp.where(sub == i, owner_ref[k], tile_col)
        reach_row = jnp.where(lane1 == i, reach_ref[k], reach_row)
        reach_col = jnp.where(sub == i, reach_ref[k], reach_col)
    rx, ry = tile_row // size_y, tile_row % size_y
    cx, cy = tile_col // size_y, tile_col % size_y
    distance = jnp.maximum(jnp.abs(cx - rx), jnp.abs(cy - ry))
    onto = localize(distance, reach_row, taper_ref)
    onto_t = localize(distance, reach_col, taper_ref)
    mine = place_ref[0]
    own = localize(
        jnp.maximum(jnp.abs(mine // size_y - rx), jnp.abs(mine % size_y - ry)), reach_row, taper_ref
    )

    priors = prior_ref[...]
    inside = lane < members
    mean_col = jnp.sum(jnp.where(inside, priors, 0.0), axis=1, keepdims=True) / members
    anomalies = jnp.where(inside, priors - mean_col, 0.0)
    padded = jnp.concatenate([anomalies, jnp.zeros((cols - n_obs, cols), F32)], axis=0)
    table = lax.dot_general(anomalies, padded, NT, precision=HIGHEST, preferred_element_type=F32)
    table = jnp.concatenate([table, jnp.transpose(padded)[:members]], axis=0)
    mean = jnp.zeros((1, cols), F32)
    for i in range(n_obs):
        mean = jnp.where(lane1 == i, mean_col[i : i + 1, :], mean)

    scales = jnp.zeros((1, cols), F32)
    increments = []
    power = jnp.broadcast_to(table[0:1, 0:1], (1, cols))
    for i, k in enumerate(which):
        error = error_ref[k]
        row = table[i : i + 1, :]
        column = jnp.broadcast_to(table[:, i : i + 1], table.shape)
        variance = power / (members - 1) + EPS
        root = lax.rsqrt(1.0 + variance * (1.0 / error))
        scaled = 1.0 / ((members - 1) * variance)
        shift = variance * (value_ref[k] - jnp.broadcast_to(mean[:, i : i + 1], row.shape)) * (root * root * (1.0 / error))
        shrink = root - 1.0
        weight = scaled * jnp.broadcast_to(own[:, i : i + 1], row.shape)
        alpha_row = onto_t[i : i + 1, :] * row * scaled
        later = lane1 > i
        h = jnp.where(later, shrink * alpha_row, 0.0)
        q = jnp.where(later, shrink * (row + h * power), 0.0)
        alpha = jnp.concatenate(
            [jnp.broadcast_to(onto[:, i : i + 1], onto.shape) * column[:n_obs] * scaled, column[n_obs:] * weight], axis=0
        )
        if i + 1 < n_obs:
            beside, ahead, reach_on = (
                jnp.broadcast_to(x[:, i + 1 : i + 2], row.shape)
                for x in (row, table[i + 1 : i + 2, :], onto_t[i : i + 1, :])
            )
            step = reach_on * beside * scaled
            power = ahead + beside * (shrink * step) + step * (shrink * (beside + shrink * step * power))
        table = table + column * h + alpha * q
        mean = mean + alpha_row * shift
        now = anomalies[i : i + 1, :]
        increments.append(shift + shrink * now)
        anomalies = anomalies + jnp.where(sub > i, shrink * alpha[:n_obs], 0.0) * now
        scales = jnp.where(lane1 == i, weight, scales)
    left = table[n_obs:, :] * scales
    right = jnp.where(inside, jnp.concatenate(increments, axis=0), 0.0)
    right = jnp.concatenate([right, jnp.zeros((cols - n_obs, cols), F32)], axis=0)
    change = jnp.dot(left, right, precision=HIGHEST, preferred_element_type=F32)
    change = jnp.concatenate([change, jnp.zeros((cols - members, cols), F32)], axis=0)
    change = jnp.transpose(change)[:members, :]
    high = change.astype(BF16).astype(F32)
    low = change - high
    zero = jnp.zeros((members, cols), F32)
    high = jnp.concatenate([high, zero], axis=1)
    low = jnp.concatenate([low, zero], axis=1)
    factor = (high + roll_lanes(high, members) + roll_lanes(low, 2 * members)).astype(BF16)

    block = 4
    for at in range(0, 3 * rows, block):
        x = jnp.concatenate([forecast_ref[at + b] for b in range(block)], axis=1)
        xh = x.astype(BF16)
        xl = (x - xh.astype(F32)).astype(BF16)
        stack = jnp.concatenate([xh, xl, xh, jnp.zeros((2 * cols - 3 * members, block * cols), BF16)], axis=0)
        y = x + jnp.dot(factor, stack, preferred_element_type=F32)
        for b in range(block):
            f, r = divmod(at + b, rows)
            out_ref[pl.ds(f * members * rows + r, members, stride=rows), :] = y[:, b * cols : (b + 1) * cols]
        if (at + block) % rows == 0:
            field = pl.ds(at // rows * members * rows, members * rows)
            pltpu.make_async_copy(out_ref.at[field], result_ref.at[field], sems.at[at // rows]).start()
    for f in range(3):
        field = pl.ds(f * members * rows, members * rows)
        pltpu.make_async_copy(out_ref.at[field], result_ref.at[field], sems.at[f]).wait()


def assimilate(place, order, owner, reach, value, error, taper, priors, states, members, rows):
    cols = priors.shape[1]
    return pl.pallas_call(
        functools.partial(assimilate_kernel, members, rows),
        out_shape=jax.ShapeDtypeStruct((3 * members * rows, cols), F32),
        in_specs=[SSPEC] * 7 + [VSPEC] * 2,
        out_specs=pl.BlockSpec(memory_space=pl.ANY),
        scratch_shapes=[pltpu.VMEM((3 * members * rows, cols), F32), pltpu.SemaphoreType.DMA((3,))],
        compiler_params=pltpu.CompilerParams(vmem_limit_bytes=VMEM_LIMIT),
    )(place, order, owner, reach, value, error, taper, priors, states)


def to_neighbours(axis, lower, upper):
    count = lax.axis_size(axis)
    forward = [(i, i + 1) for i in range(count - 1)]
    backward = [(target, source) for source, target in forward]
    return lax.ppermute(upper, axis, forward), lax.ppermute(lower, axis, backward)


def swap_pairs(x, axis, start):
    pairs = [(i, i + 1) for i in range(start, lax.axis_size(axis) - 1, 2)]
    return lax.ppermute(x, axis, pairs + [(b, a) for a, b in pairs])


def add_over(x, axes):
    for axis in axes:
        count = lax.axis_size(axis)
        if count & (count - 1):
            x = lax.psum(x, axis)
            continue
        span = count // 2
        while span:
            x = x + lax.ppermute(x, axis, [(i, i ^ span) for i in range(count)])
            span //= 2
    return x


def body(status, drag, value, error, taper, order, owner, cell, reach):
    members, rows, cols = status.shape[1:]
    ix, iy = lax.axis_index("gx"), lax.axis_index("gy")
    size_x, size_y = lax.axis_size("gx"), lax.axis_size("gy")
    place = jnp.stack(
        [
            ix * size_y + iy,
            (ix == 0).astype(jnp.int32),
            (ix == size_x - 1).astype(jnp.int32),
            (iy == 0).astype(jnp.int32),
            (iy == size_y - 1).astype(jnp.int32),
            jnp.int32(size_y),
        ]
    ).astype(jnp.int32)
    flat = status.reshape(3 * members * rows, cols)
    lower, upper = bands(flat, members, rows)
    above, below = to_neighbours("gy", lower, upper)
    even, odd = pack(place, flat, drag, members)
    even, odd = swap_pairs(even, "gx", 0), swap_pairs(odd, "gx", 1)
    left, right, margin, even, odd = corner(place, drag, even, odd)
    even, odd = swap_pairs(even, "gy", 0), swap_pairs(odd, "gy", 1)
    inner = interior(place, flat, left, right, drag, margin, members)
    states, priors = forecast(place, order, owner, cell, inner, above, below, even, odd, drag, margin)
    priors = add_over(priors, ("gx", "gy"))
    result = assimilate(place, order, owner, reach, value, error, taper, priors, states, members, rows)
    return result.reshape(status.shape)


def solution(mesh):
    in_specs = (P(None, None, "gy", "gx"), P("gy", "gx"), P(), P(), P(), P(), P(), P(), P())
    out_specs = P(None, None, "gy", "gx")
    return jax.shard_map(body, mesh=mesh, in_specs=in_specs, out_specs=out_specs, check_vma=False)
```

```python
import functools

import jax
import jax.numpy as jnp
from jax import lax
from jax.experimental import pallas as pl
from jax.experimental.pallas import tpu as pltpu
from jax.sharding import PartitionSpec as P

STEPS = 4
MARGIN = 2 * STEPS
EPS = 1e-06
NT = (((1,), (1,)), ((), ()))
HIGHEST = lax.Precision.HIGHEST
F32 = jnp.float32
BF16 = jnp.bfloat16
VMEM_LIMIT = 24 * 1024 * 1024
GROUP = 40

VSPEC = pl.BlockSpec(memory_space=pltpu.VMEM)
SSPEC = pl.BlockSpec(memory_space=pltpu.SMEM)


def lanes_of(shape):
    return lax.broadcasted_iota(jnp.int32, shape, len(shape) - 1)


def sublanes_of(shape):
    return lax.broadcasted_iota(jnp.int32, shape, len(shape) - 2)


def roll_lanes(x, shift):
    size = x.shape[-1]
    shift = shift % size
    return x if shift == 0 else pltpu.roll(x, shift, x.ndim - 1)


def band_kernel(members, rows, x_hbm, lower_hbm, upper_hbm, x_ref, lower_ref, upper_ref, sems):
    def arrive(f):
        field = pl.ds(f * members * rows, members * rows)
        return pltpu.make_async_copy(x_hbm.at[field], x_ref.at[field], sems.at[0, f])

    def leave(f, side):
        source, target = ((lower_ref, lower_hbm), (upper_ref, upper_hbm))[side]
        here = pl.ds(f * (MARGIN - 1), MARGIN if f == 2 else MARGIN - 1)
        return pltpu.make_async_copy(source.at[here], target.at[here], sems.at[1 + side, f])

    for f in range(3):
        arrive(f).start()
    for f in range(3):
        arrive(f).wait()
        depth = MARGIN if f == 2 else MARGIN - 1
        for d in range(depth):
            at = f * members * rows + d
            lower_ref[f * (MARGIN - 1) + d] = x_ref[pl.ds(at, members, stride=rows), :]
            upper_ref[f * (MARGIN - 1) + d] = x_ref[pl.ds(at + rows - depth, members, stride=rows), :]
        leave(f, 0).start()
        leave(f, 1).start()
    for f in range(3):
        leave(f, 0).wait()
        leave(f, 1).wait()


def bands(x, members, rows):
    cols = x.shape[1]
    shape = (3 * MARGIN - 2, members, cols)
    return pl.pallas_call(
        functools.partial(band_kernel, members, rows),
        out_shape=(jax.ShapeDtypeStruct(shape, F32),) * 2,
        in_specs=[pl.BlockSpec(memory_space=pltpu.HBM)],
        out_specs=(pl.BlockSpec(memory_space=pl.ANY),) * 2,
        scratch_shapes=[pltpu.VMEM(x.shape, F32)] + [pltpu.VMEM(shape, F32)] * 2 + [pltpu.SemaphoreType.DMA((3, 3))],
        compiler_params=pltpu.CompilerParams(vmem_limit_bytes=60 * 1024 * 1024),
        cost_estimate=pl.CostEstimate(flops=1_000_000, bytes_accessed=4_000_000, transcendentals=0),
    )(x)


def pack_kernel(members, rows, place_ref, x_ref, drag_ref, even_ref, odd_ref):
    cols = x_ref.shape[1]
    lane = lanes_of((8, cols))
    slot = lane // MARGIN
    odd_x = place_ref[0] // place_ref[5] % 2 == 1

    def group(g, carry):
        for f in range(3):
            row = [x_ref[pl.ds((f * members + g * 8) * rows + r, 8, stride=rows), :] for r in range(rows)]
            left, right = row[rows - 1], roll_lanes(row[rows - 1], MARGIN * rows)
            for r in range(rows - 1):
                both = roll_lanes(jnp.where(lane < cols // 2, row[rows - 2 - r], row[r]), MARGIN * (r + 1))
                left = jnp.where(slot == r + 1, both, left)
                right = jnp.where(slot == r, both, right)
            at = pl.ds(pl.multiple_of(f * members + g * 8, 8), 8)
            even_ref[at, :] = jnp.where(odd_x, left, right)
            odd_ref[at, :] = jnp.where(odd_x, right, left)
        return carry

    lax.fori_loop(0, members // 8, group, 0)
    even_ref[3 * members :, :] = drag_ref[...]
    odd_ref[3 * members :, :] = drag_ref[...]


def pack(place, x, drag, members):
    rows, cols = drag.shape
    message = jax.ShapeDtypeStruct((3 * members + rows, cols), F32)
    return pl.pallas_call(
        functools.partial(pack_kernel, members, rows),
        out_shape=(message, message),
        in_specs=[SSPEC, VSPEC, VSPEC],
        out_specs=(VSPEC,) * 2,
        compiler_params=pltpu.CompilerParams(vmem_limit_bytes=VMEM_LIMIT),
        cost_estimate=pl.CostEstimate(flops=1_000_000, bytes_accessed=4_000_000, transcendentals=0),
    )(place, x, drag)


def corner_kernel(place_ref, drag_ref, even_ref, odd_ref, left_ref, right_ref, margin_ref, even_out, odd_out):
    count, cols = left_ref.shape
    rows = drag_ref.shape[0]
    half = cols // 2
    odd_y = place_ref[0] % place_ref[5] % 2 == 1
    odd_x = place_ref[0] // place_ref[5] % 2 == 1
    even, odd = even_ref[...], odd_ref[...]
    left, right = jnp.where(odd_x, even, odd), jnp.where(odd_x, odd, even)
    margin = jnp.where(lanes_of((rows, cols)) < half, right[count:], left[count:])
    margin_ref[...] = margin
    left, right = left[:count], right[:count]
    left_ref[...] = left
    right_ref[...] = right
    lane = lanes_of((count, cols))
    slot, column = lane % half // MARGIN, lane % MARGIN
    mine = column > jnp.where(lane < half, slot, MARGIN - 1 - slot)
    both = jnp.where(mine, left, roll_lanes(right, half))
    count = count // 2
    head, tail = both[:count], both[count:]
    first_half = lanes_of((count, cols)) < half
    lower = jnp.where(first_half, head, roll_lanes(tail, half))
    upper = jnp.where(first_half, roll_lanes(head, half), tail)
    even_out[:count, :] = jnp.where(odd_y, lower, upper)
    odd_out[:count, :] = jnp.where(odd_y, upper, lower)
    drag = drag_ref[...]
    for at, part in ((count, drag), (count + MARGIN, margin)):
        lower, upper = part[:MARGIN], part[rows - MARGIN :]
        even_out[at : at + MARGIN, :] = jnp.where(odd_y, lower, upper)
        odd_out[at : at + MARGIN, :] = jnp.where(odd_y, upper, lower)


def corner(place, drag, even, odd):
    rows, cols = drag.shape
    count = even.shape[0] - rows
    edge = jax.ShapeDtypeStruct((count, cols), F32)
    message = jax.ShapeDtypeStruct((count // 2 + 2 * MARGIN, cols), F32)
    return pl.pallas_call(
        corner_kernel,
        out_shape=(edge, edge, jax.ShapeDtypeStruct((rows, cols), F32), message, message),
        in_specs=[SSPEC] + [VSPEC] * 3,
        out_specs=(VSPEC,) * 5,
        compiler_params=pltpu.CompilerParams(vmem_limit_bytes=VMEM_LIMIT),
    )(place, drag, even, odd)


def grid_factor(place_ref, shape, rows, cols):
    row, col = sublanes_of(shape), lanes_of(shape)
    wide = 2 * cols
    low, high = jnp.where(place_ref[3] == 1, MARGIN, 0), jnp.where(place_ref[4] == 1, MARGIN + rows, rows + 2 * MARGIN)
    first, last = jnp.where(place_ref[1] == 1, wide, wide - MARGIN), jnp.where(place_ref[2] == 1, cols, cols + MARGIN)
    ok = (row >= low) & (row < high) & ((col < last) | (col >= first))
    return jnp.where(ok, 1.0, 0.0)


def wide_row(lane, main, left, left_at, right, right_at):
    cols = main.shape[1]
    halo = jnp.where(lane >= cols - MARGIN, roll_lanes(left, cols - MARGIN - left_at), 0.0)
    halo = jnp.where(lane < MARGIN, roll_lanes(right, -right_at), halo)
    return jnp.concatenate([main, halo], axis=1)


def shift_matrix(wide):
    source, target = sublanes_of((wide, wide)), lanes_of((wide, wide))
    after, before = source == (target + 1) % wide, target == (source + 1) % wide
    return jnp.where(after, 1.0, jnp.where(before, -1.0, 0.0)).astype(BF16)


def tall(x):
    return jnp.concatenate([x] * (GROUP // 8), axis=0)


def column_slope(x, shift):
    rows, group, wide = x.shape
    x = x.reshape(rows * group, wide)
    top = x.astype(BF16)
    rest = (x - top.astype(F32)).astype(BF16)
    slope = jnp.dot(top, shift, preferred_element_type=F32) + jnp.dot(rest, shift, preferred_element_type=F32)
    return slope.reshape(rows, group, wide)


def interior_kernel(members, rows, place_ref, x_ref, left_ref, right_ref, drag_ref, margin_ref, state, keep, slope):
    cols = x_ref.shape[1]
    wide = 2 * cols
    lane = lanes_of((8, cols))
    factor = -0.2 * grid_factor(place_ref, (rows + 2 * MARGIN, wide), rows, cols)
    shift = shift_matrix(wide)
    kept = 1.0 - jnp.concatenate([drag_ref[...], margin_ref[...]], axis=1)
    for r in range(rows):
        keep[r] = jnp.broadcast_to(kept[r : r + 1, :], (8, wide))
        slope[r] = jnp.broadcast_to(factor[MARGIN + r : MARGIN + r + 1, :], (8, wide))

    def first(g, carry):
        here = pl.ds(pl.multiple_of(g * 8, 8), 8)
        for f in range(3):
            at = pl.ds(pl.multiple_of(f * members + g * 8, 8), 8)
            left, right = left_ref[at, :], right_ref[at, :]
            for r in range(rows):
                main = x_ref[pl.ds((f * members + g * 8) * rows + r, 8, stride=rows), :]
                state[f, r, here, :] = wide_row(lane, main, left, MARGIN * r, right, MARGIN * (rows - 1 - r))
        return carry

    lax.fori_loop(0, members // 8, first, 0)

    groups = [pl.ds(m, GROUP) for m in range(0, members, GROUP)]
    for step in range(STEPS):
        low, high = 1 + 2 * step, rows - 1 - 2 * step
        if low >= high:
            break
        for here in groups:
            d = column_slope(state[1, low:high, here, :], shift)
            for r in range(low, high):
                div = d[r - low] + (state[2, r + 1, here, :] - state[2, r - 1, here, :])
                state[0, r, here, :] = state[0, r, here, :] + tall(slope[r]) * div
        low, high = low + 1, high - 1
        if low >= high:
            break
        for here in groups:
            d = column_slope(state[0, low:high, here, :], shift)
            for r in range(low, high):
                u, v = state[1, r, here, :], state[2, r, here, :]
                k, c = tall(keep[r]), tall(slope[r])
                state[1, r, here, :] = k * u + c * d[r - low] + 0.1 * v
                state[2, r, here, :] = k * v + c * (state[0, r + 1, here, :] - state[0, r - 1, here, :]) - 0.1 * u


def interior(place, x, left, right, drag, margin, members):
    rows, cols = drag.shape
    return pl.pallas_call(
        functools.partial(interior_kernel, members, rows),
        out_shape=jax.ShapeDtypeStruct((3, rows, members, 2 * cols), F32),
        in_specs=[SSPEC] + [VSPEC] * 5,
        out_specs=VSPEC,
        scratch_shapes=[pltpu.VMEM((rows, 8, 2 * cols), F32)] * 2,
        compiler_params=pltpu.CompilerParams(vmem_limit_bytes=VMEM_LIMIT),
        cost_estimate=pl.CostEstimate(flops=30_000_000, bytes_accessed=10_000_000, transcendentals=0),
    )(place, x, left, right, drag, margin)


def forecast_kernel(
    members, rows,
    place_ref, order_ref, owner_ref, cell_ref,
    inner_ref, above_ref, below_ref, ceven_ref, codd_ref, drag_ref, margin_ref,
    out_ref, prior_ref,
    state, keep, slope,
):
    cols = above_ref.shape[2]
    wide = 2 * cols
    total = rows + 2 * MARGIN
    half = cols // 2
    lane = lanes_of((GROUP, cols))
    factor = -0.2 * grid_factor(place_ref, (total, wide), rows, cols)
    odd_y = place_ref[0] % place_ref[5] % 2 == 1
    shift = shift_matrix(wide)
    count = 3 * members // 2
    parts = []
    for here, own in ((count, drag_ref), (count + MARGIN, margin_ref)):
        even, odd = ceven_ref[here : here + MARGIN, :], codd_ref[here : here + MARGIN, :]
        above, below = jnp.where(odd_y, even, odd), jnp.where(odd_y, odd, even)
        parts.append(jnp.concatenate([above, own[...], below], axis=0))
    kept = 1.0 - jnp.concatenate(parts, axis=1)
    for r in range(total):
        keep[r] = jnp.broadcast_to(kept[r : r + 1, :], (8, wide))
        slope[r] = jnp.broadcast_to(factor[r : r + 1, :], (8, wide))

    groups = range(members // GROUP)
    for g in groups:
        here = pl.ds(g * GROUP, GROUP)
        for f in range(3):
            at = f * members + g * GROUP
            base = half if at >= count else 0
            at = pl.ds(at % count, GROUP)
            ceven, codd = ceven_ref[at, :], codd_ref[at, :]
            cab, cbe = jnp.where(odd_y, ceven, codd), jnp.where(odd_y, codd, ceven)
            depth = MARGIN if f == 2 else MARGIN - 1
            for d in range(depth):
                r = MARGIN - depth + d
                main = above_ref[f * (MARGIN - 1) + d, here, :]
                state[g, f, r] = wide_row(lane, main, cab, base + MARGIN * r, cab, base + MARGIN * (MARGIN - 1 - r))
                main = below_ref[f * (MARGIN - 1) + d, here, :]
                state[g, f, MARGIN + rows + d] = wide_row(
                    lane, main, cbe, base + MARGIN * d, cbe, base + MARGIN * (MARGIN - 1 - d)
                )
            for r in range(rows):
                state[g, f, MARGIN + r] = inner_ref[f, r, here, :]

    def heights(g, spans):
        for low, high in spans:
            d = column_slope(state[g, 1, low:high], shift)
            for r in range(low, high):
                div = d[r - low] + (state[g, 2, r + 1] - state[g, 2, r - 1])
                state[g, 0, r] = state[g, 0, r] + tall(slope[r]) * div

    def flows(g, spans, final):
        here = pl.ds(g * GROUP, GROUP)
        for low, high in spans:
            d = column_slope(state[g, 0, low:high], shift)
            for r in range(low, high):
                u, v = state[g, 1, r], state[g, 2, r]
                k, c = tall(keep[r]), tall(slope[r])
                u, v = (
                    k * u + c * d[r - low] + 0.1 * v,
                    k * v + c * (state[g, 0, r + 1] - state[g, 0, r - 1]) - 0.1 * u,
                )
                if final:
                    for f, value in enumerate((state[g, 0, r], u, v)):
                        out_ref[f * rows + r - MARGIN, here, :] = value[:, 0:cols]
                else:
                    state[g, 1, r] = u
                    state[g, 2, r] = v

    for step in range(STEPS):
        first, last = MARGIN - MARGIN + 1 + 2 * step, MARGIN + rows + MARGIN - 1 - 2 * step
        done, still = MARGIN + 1 + 2 * step, MARGIN + rows - 1 - 2 * step
        for g in groups:
            heights(g, ((first, done), (still, last)))
        for g in groups:
            flows(g, ((first + 1, done + 1), (still - 1, last - 1)), step == STEPS - 1)
    prior_ref[...] = jnp.zeros_like(prior_ref)
    eight = lanes_of((8, cols))
    for i in range(order_ref.shape[0]):
        which = order_ref[i]

        @pl.when(owner_ref[which] == place_ref[0])
        def _():
            cell = cell_ref[which]
            one = jnp.where(eight == cell % cols, 1.0, 0.0)
            prior_ref[i : i + 1, 0:members] = lax.dot_general(
                one, out_ref[cell // cols], NT, precision=HIGHEST, preferred_element_type=F32
            )[0:1]


def forecast(place, order, owner, cell, inner, *arrays):
    _, rows, members, wide = inner.shape
    cols = wide // 2
    total = rows + 2 * MARGIN
    return pl.pallas_call(
        functools.partial(forecast_kernel, members, rows),
        out_shape=(
            jax.ShapeDtypeStruct((3 * rows, members, cols), F32),
            jax.ShapeDtypeStruct((order.shape[0], cols), F32),
        ),
        in_specs=[SSPEC] * 4 + [VSPEC] * (1 + len(arrays)),
        out_specs=(VSPEC, VSPEC),
        scratch_shapes=[pltpu.VMEM((members // GROUP, 3, total, GROUP, wide), F32)] + [pltpu.VMEM((total, 8, wide), F32)] * 2,
        compiler_params=pltpu.CompilerParams(vmem_limit_bytes=VMEM_LIMIT),
        cost_estimate=pl.CostEstimate(flops=60_000_000, bytes_accessed=30_000_000, transcendentals=0),
    )(place, order, owner, cell, inner, *arrays)


def localize(distance, reach, taper_ref):
    picked = jnp.zeros(distance.shape, F32)
    levels = taper_ref.shape[0]
    capped = jnp.minimum(distance, levels - 1)
    for d in range(levels):
        picked = jnp.where(capped == d, taper_ref[d], picked)
    return jnp.where(distance <= reach, picked, 0.0)


def assimilate_kernel(
    members, rows,
    place_ref, order_ref, owner_ref, reach_ref, value_ref, error_ref, taper_ref,
    prior_ref, forecast_ref,
    result_ref,
    out_ref, sems,
):
    n_obs = order_ref.shape[0]
    cols = prior_ref.shape[1]
    size_y = place_ref[5]
    lane1 = lanes_of((1, cols))
    lane = lanes_of((n_obs, cols))
    sub = sublanes_of((n_obs, cols))

    tile_row = jnp.zeros((1, cols), jnp.int32)
    tile_col = jnp.zeros((n_obs, cols), jnp.int32)
    reach_row = jnp.zeros((1, cols), jnp.int32)
    reach_col = jnp.zeros((n_obs, cols), jnp.int32)
    which = [order_ref[i] for i in range(n_obs)]
    for i, k in enumerate(which):
        tile_row = jnp.where(lane1 == i, owner_ref[k], tile_row)
        tile_col = jnp.where(sub == i, owner_ref[k], tile_col)
        reach_row = jnp.where(lane1 == i, reach_ref[k], reach_row)
        reach_col = jnp.where(sub == i, reach_ref[k], reach_col)
    rx, ry = tile_row // size_y, tile_row % size_y
    cx, cy = tile_col // size_y, tile_col % size_y
    distance = jnp.maximum(jnp.abs(cx - rx), jnp.abs(cy - ry))
    onto = localize(distance, reach_row, taper_ref)
    onto_t = localize(distance, reach_col, taper_ref)
    mine = place_ref[0]
    own = localize(
        jnp.maximum(jnp.abs(mine // size_y - rx), jnp.abs(mine % size_y - ry)), reach_row, taper_ref
    )

    priors = prior_ref[...]
    inside = lane < members
    mean_col = jnp.sum(jnp.where(inside, priors, 0.0), axis=1, keepdims=True) / members
    anomalies = jnp.where(inside, priors - mean_col, 0.0)
    padded = jnp.concatenate([anomalies, jnp.zeros((cols - n_obs, cols), F32)], axis=0)
    table = lax.dot_general(anomalies, padded, NT, precision=HIGHEST, preferred_element_type=F32)
    table = jnp.concatenate([table, jnp.transpose(padded)[:members]], axis=0)
    mean = jnp.zeros((1, cols), F32)
    for i in range(n_obs):
        mean = jnp.where(lane1 == i, mean_col[i : i + 1, :], mean)

    scales = jnp.zeros((1, cols), F32)
    increments = []
    power = jnp.broadcast_to(table[0:1, 0:1], (1, cols))
    for i, k in enumerate(which):
        error = error_ref[k]
        row = table[i : i + 1, :]
        column = jnp.broadcast_to(table[:, i : i + 1], table.shape)
        variance = power / (members - 1) + EPS
        root = lax.rsqrt(1.0 + variance * (1.0 / error))
        scaled = 1.0 / ((members - 1) * variance)
        shift = variance * (value_ref[k] - jnp.broadcast_to(mean[:, i : i + 1], row.shape)) * (root * root * (1.0 / error))
        shrink = root - 1.0
        weight = scaled * jnp.broadcast_to(own[:, i : i + 1], row.shape)
        alpha_row = onto_t[i : i + 1, :] * row * scaled
        later = lane1 > i
        h = jnp.where(later, shrink * alpha_row, 0.0)
        q = jnp.where(later, shrink * (row + h * power), 0.0)
        alpha = jnp.concatenate(
            [jnp.broadcast_to(onto[:, i : i + 1], onto.shape) * column[:n_obs] * scaled, column[n_obs:] * weight], axis=0
        )
        if i + 1 < n_obs:
            beside, ahead, reach_on = (
                jnp.broadcast_to(x[:, i + 1 : i + 2], row.shape)
                for x in (row, table[i + 1 : i + 2, :], onto_t[i : i + 1, :])
            )
            step = reach_on * beside * scaled
            power = ahead + beside * (shrink * step) + step * (shrink * (beside + shrink * step * power))
        table = table + column * h + alpha * q
        mean = mean + alpha_row * shift
        now = anomalies[i : i + 1, :]
        increments.append(shift + shrink * now)
        anomalies = anomalies + jnp.where(sub > i, shrink * alpha[:n_obs], 0.0) * now
        scales = jnp.where(lane1 == i, weight, scales)
    left = table[n_obs:, :] * scales
    right = jnp.where(inside, jnp.concatenate(increments, axis=0), 0.0)
    right = jnp.concatenate([right, jnp.zeros((cols - n_obs, cols), F32)], axis=0)
    change = jnp.dot(left, right, precision=HIGHEST, preferred_element_type=F32)
    change = jnp.concatenate([change, jnp.zeros((cols - members, cols), F32)], axis=0)
    change = jnp.transpose(change)[:members, :]
    high = change.astype(BF16).astype(F32)
    low = change - high
    zero = jnp.zeros((members, cols), F32)
    high = jnp.concatenate([high, zero], axis=1)
    low = jnp.concatenate([low, zero], axis=1)
    factor = (high + roll_lanes(high, members) + roll_lanes(low, 2 * members)).astype(BF16)

    block = 8
    for at in range(0, 3 * rows, block):
        x = jnp.concatenate([forecast_ref[at + b] for b in range(block)], axis=1)
        xh = x.astype(BF16)
        xl = (x - xh.astype(F32)).astype(BF16)
        stack = jnp.concatenate([xh, xl, xh, jnp.zeros((2 * cols - 3 * members, block * cols), BF16)], axis=0)
        y = x + jnp.dot(factor, stack, preferred_element_type=F32)
        for b in range(block):
            f, r = divmod(at + b, rows)
            out_ref[pl.ds(f * members * rows + r, members, stride=rows), :] = y[:, b * cols : (b + 1) * cols]
        if (at + block) % rows == 0:
            field = pl.ds(at // rows * members * rows, members * rows)
            pltpu.make_async_copy(out_ref.at[field], result_ref.at[field], sems.at[at // rows]).start()
    for f in range(3):
        field = pl.ds(f * members * rows, members * rows)
        pltpu.make_async_copy(out_ref.at[field], result_ref.at[field], sems.at[f]).wait()


def assimilate(place, order, owner, reach, value, error, taper, priors, states, members, rows):
    cols = priors.shape[1]
    return pl.pallas_call(
        functools.partial(assimilate_kernel, members, rows),
        out_shape=jax.ShapeDtypeStruct((3 * members * rows, cols), F32),
        in_specs=[SSPEC] * 7 + [VSPEC] * 2,
        out_specs=pl.BlockSpec(memory_space=pl.ANY),
        scratch_shapes=[pltpu.VMEM((3 * members * rows, cols), F32), pltpu.SemaphoreType.DMA((3,))],
        compiler_params=pltpu.CompilerParams(vmem_limit_bytes=VMEM_LIMIT),
    )(place, order, owner, reach, value, error, taper, priors, states)


def to_neighbours(axis, lower, upper):
    count = lax.axis_size(axis)
    forward = [(i, i + 1) for i in range(count - 1)]
    backward = [(target, source) for source, target in forward]
    return lax.ppermute(upper, axis, forward), lax.ppermute(lower, axis, backward)


def swap_pairs(x, axis, start):
    pairs = [(i, i + 1) for i in range(start, lax.axis_size(axis) - 1, 2)]
    return lax.ppermute(x, axis, pairs + [(b, a) for a, b in pairs])


def add_over(x, axes):
    for axis in axes:
        count = lax.axis_size(axis)
        if count & (count - 1):
            x = lax.psum(x, axis)
            continue
        span = 1
        while span < count:
            x = x + lax.ppermute(x, axis, [(i, i ^ span) for i in range(count)])
            span *= 2
    return x


def body(status, drag, value, error, taper, order, owner, cell, reach):
    members, rows, cols = status.shape[1:]
    ix, iy = lax.axis_index("gx"), lax.axis_index("gy")
    size_x, size_y = lax.axis_size("gx"), lax.axis_size("gy")
    place = jnp.stack(
        [
            ix * size_y + iy,
            (ix == 0).astype(jnp.int32),
            (ix == size_x - 1).astype(jnp.int32),
            (iy == 0).astype(jnp.int32),
            (iy == size_y - 1).astype(jnp.int32),
            jnp.int32(size_y),
        ]
    ).astype(jnp.int32)
    flat = status.reshape(3 * members * rows, cols)
    lower, upper = bands(flat, members, rows)
    above, below = to_neighbours("gy", lower, upper)
    even, odd = pack(place, flat, drag, members)
    even, odd = swap_pairs(even, "gx", 0), swap_pairs(odd, "gx", 1)
    left, right, margin, even, odd = corner(place, drag, even, odd)
    even, odd = swap_pairs(even, "gy", 0), swap_pairs(odd, "gy", 1)
    inner = interior(place, flat, left, right, drag, margin, members)
    states, priors = forecast(place, order, owner, cell, inner, above, below, even, odd, drag, margin)
    priors = add_over(priors, ("gx", "gy"))
    result = assimilate(place, order, owner, reach, value, error, taper, priors, states, members, rows)
    return result.reshape(status.shape)


def solution(mesh):
    in_specs = (P(None, None, "gy", "gx"), P("gy", "gx"), P(), P(), P(), P(), P(), P(), P())
    out_specs = P(None, None, "gy", "gx")
    return jax.shard_map(body, mesh=mesh, in_specs=in_specs, out_specs=out_specs, check_vma=False)
```
